32 devices in a mesh: rep: 4 (over y, core), shard: 8 (over z, x).
Axes of the slice: x: 2, y: 2, z: 4, core: 2. Of those that a mesh axis runs over, the one named last changes fastest.
Arguments:
- tokens: bfloat16 [16384, 1024], P(('rep', 'shard')), may hold values from -6 to 6
- state_in: bfloat16 [16, 512, 1024], P('rep', 'shard'), may hold values from -6 to 6
- gain_tok: bfloat16 [1024], P('shard'), may hold values from 0.5 to 1.5
- gain_state: bfloat16 [1024], P('shard'), may hold values from 0.5 to 1.5
- gain_mlp: bfloat16 [1024], P('shard'), may hold values from 0.5 to 1.5
- w_tok: bfloat16 [1024, 3072], P('shard'), may hold values from -0.1875 to 0.1875
- w_state: bfloat16 [1024, 3072], P('shard'), may hold values from -0.1875 to 0.1875
- w_out: bfloat16 [1024, 1024], P('shard'), may hold values from -3.5 to 3.5
- w_update: bfloat16 [1024, 1024], P('shard'), may hold values from -3.5 to 3.5
- gate_bias: bfloat16 [1024], P('shard'), may hold values from -3 to 3
- rel_bias: bfloat16 [8, 32], P('shard'), may hold values from -4 to 4
- w_up: bfloat16 [4096, 1024], P('shard'), may hold values from -0.1875 to 0.1875
- w_down: bfloat16 [4096, 1024], P('shard'), may hold values from -0.09375 to 0.09375
- d_out: bfloat16 [16384, 1024], P(('rep', 'shard')), may hold values from -6 to 6
- d_state_next: bfloat16 [16, 512, 1024], P('rep', 'shard'), may hold values from -6 to 6
Outputs:
- output: bfloat16 [16384, 1024], P(('rep', 'shard'))
- state_next: float32 [16, 512, 1024], P('rep', 'shard')
- grad_tokens: float32 [16384, 1024], P(('rep', 'shard'))
- grad_state_in: float32 [16, 512, 1024], P('rep', 'shard')
- grad_gain_tok: float32 [1024], P('shard')
- grad_gain_state: float32 [1024], P('shard')
- grad_gain_mlp: float32 [1024], P('shard')
- grad_w_tok: float32 [1024, 3072], P('shard')
- grad_w_state: float32 [1024, 3072], P('shard')
- grad_w_out: float32 [1024, 1024], P('shard')
- grad_w_update: float32 [1024, 1024], P('shard')
- grad_gate_bias: float32 [1024], P('shard')
- grad_rel_bias: float32 [8, 32], P('shard')
- grad_w_up: float32 [4096, 1024], P('shard')
- grad_w_down: float32 [4096, 1024], P('shard')
The draws below stay inside these ranges and needn't reach their ends.
All inputs are finite; a program needn't handle non-finite values.
Results may differ from the reference program's by a relative error of at most 0.017.
Values may be sent and summed in bfloat16 or wider, within the bound.
No kernel may reach another device: no remote copies, remote signals or barrier semaphores. Data moves between devices by JAX's collectives and lax.ppermute only.
A program may use at most 320 MiB of HBM per device.

```python
import math
from functools import partial
import jax
import jax.numpy as jnp
import numpy as np
from jax import lax

D = 1024
H = 8
FF = 4096
BLK = 512
M = 512
NB = 32
REACH = 128
NBLK = 2
SEQS = 16
TOKENS = 16384


def shard_levels(stream_key, extent, cuts, low, high):
    gain = 1.0
    for axis_at, parts in cuts:
        draws = jax.random.uniform(jax.random.fold_in(jax.random.fold_in(stream_key, 6), axis_at), (parts,), jnp.float32, low / len(cuts), high / len(cuts))
        gain = gain * jnp.repeat(jnp.exp(draws), extent[axis_at] // parts).reshape((-1,) + (1,) * (len(extent) - 1 - axis_at))
    return gain


def scatter_about(stream_key, shape, deviation, bound, cuts=(), held_as=jnp.bfloat16):
    drawn = jax.random.normal(stream_key, shape, jnp.float32) * deviation
    if len(cuts) > 0:
        drawn = shard_levels(stream_key, shape, cuts, -0.22, 0.18) * drawn
    return jnp.clip(drawn, min=-bound, max=bound).astype(held_as)


def setup_inputs(seed: int = 0) -> dict:
    keys = jax.random.split(jax.random.key(seed), 16)
    return {
        "tokens": scatter_about(keys[0], (TOKENS, D), 1.0, 6.0, ((0, 32),)),
        "state_in": scatter_about(keys[1], (SEQS, M, D), 1.0, 6.0, ((0, 4), (1, 8))),
        "gain_tok": jnp.clip(1.0 + 0.1 * jax.random.normal(keys[2], (D,), jnp.float32), 0.5, 1.5).astype(jnp.bfloat16),
        "gain_state": jnp.clip(1.0 + 0.1 * jax.random.normal(keys[3], (D,), jnp.float32), 0.5, 1.5).astype(jnp.bfloat16),
        "gain_mlp": jnp.clip(1.0 + 0.1 * jax.random.normal(keys[4], (D,), jnp.float32), 0.5, 1.5).astype(jnp.bfloat16),
        "w_tok": scatter_about(keys[5], (D, 3 * D), D ** -0.5, 0.1875, ((0, 8),)),
        "w_state": scatter_about(keys[6], (D, 3 * D), D ** -0.5, 0.1875, ((0, 8),)),
        "w_out": scatter_about(keys[7], (D, D), (max(3 * D // (M + BLK), 1)) ** -0.5, 3.5, ((0, 8),)),
        "w_update": scatter_about(keys[8], (D, D), (max(3 * D // (M + BLK), 1)) ** -0.5, 3.5, ((0, 8),)),
        "gate_bias": jnp.clip(jax.random.uniform(keys[9], (D,), jnp.float32, -3.0, 3.0) * shard_levels(keys[9], (D,), ((0, 8),), -0.4, 0.0), -3.0, 3.0).astype(jnp.bfloat16),
        "rel_bias": scatter_about(keys[10], (H, NB), 1.0, 4.0, ((0, 8),)),
        "w_up": scatter_about(keys[11], (FF, D), D ** -0.5, 0.1875, ((0, 8),)),
        "w_down": scatter_about(keys[12], (FF, D), FF ** -0.5, 0.09375, ((0, 8),)),
        "d_out": scatter_about(keys[13], (TOKENS, D), 1.0, 6.0, ((0, 32),)),
        "d_state_next": scatter_about(keys[14], (SEQS, M, D), 1.0, 6.0, ((0, 4), (1, 8))),
    }


@jax.custom_vjp
def low(v):
    return lax.optimization_barrier(v.astype(jnp.bfloat16)).astype(jnp.float32)

@jax.custom_vjp
def low_back(v):
    return v

def low_keep(v):
    return (low(v), None)

def low_pass(kept, grad):
    return (grad,)

def back_keep(v):
    return (v, None)

def back_low(kept, grad):
    return (low(grad),)
low.defvjp(low_keep, low_pass)
low_back.defvjp(back_keep, back_low)
eps = 1e-06
top_precision = lax.Precision.HIGHEST

def bucket_table(block_len, bucket_count, reach_len):
    distance = np.arange(2 * block_len + 1)
    exact_count = bucket_count // 2
    log_ratio = np.log(np.maximum(distance, 1) / exact_count) / np.log(reach_len / exact_count)
    far_bucket = np.minimum(exact_count + np.floor(log_ratio * (bucket_count - exact_count)).astype(np.int64), bucket_count - 1)
    return np.where(distance < exact_count, distance, far_bucket).astype(np.int32)

def position_tables():
    row_index = np.arange(BLK)[:, None]
    col_index = np.arange(2 * BLK)[None, :]
    distance = row_index + BLK - col_index
    allowed_pos = (distance >= 0) & (distance <= BLK)
    bucket_ids = bucket_table(BLK, NB, REACH)[np.clip(distance, 0, 2 * BLK)]
    return (allowed_pos, bucket_ids)

def layer_norm(values, gain_vec):
    centered = values - lax.optimization_barrier(jnp.mean(values, axis=-1, keepdims=True))
    variance = lax.optimization_barrier(jnp.mean(centered * centered, axis=-1, keepdims=True))
    return centered * lax.rsqrt(variance + eps) * gain_vec

def round_both(values):
    return low(low_back(values))

def product(first_op, second_op):
    return jnp.dot(first_op, second_op, precision=top_precision)

def split_heads(values):
    return values.reshape(values.shape[0], H, D // H)

def attention(queries, key_rows, values, pos_bias, allowed):
    score_scale = 1.0 / math.sqrt(D // H)
    scores = jnp.einsum('qhd,khd->hqk', split_heads(queries), split_heads(key_rows), precision=top_precision) * score_scale + pos_bias
    scores = low_back(scores)
    scores = jnp.where(allowed, scores, -1e+30)
    weights = low(jax.nn.softmax(scores, axis=-1))
    mixture = jnp.einsum('hqk,khd->qhd', weights, split_heads(values), precision=top_precision)
    return round_both(mixture.reshape(queries.shape[0], D))

def block_step(params, carried, inputs):
    gain_tok, gain_state, gain_mlp, w_tok, w_state, w_out, w_update, gate_bias, rel_bias, w_up, w_down = params
    memory, prev_keys, prev_values = carried
    block_rows, has_prev = inputs
    allowed_pos, bucket_ids = position_tables()
    normed = low(layer_norm(block_rows, gain_tok))
    projected = round_both(product(normed, w_tok))
    queries, key_rows, values = jnp.split(projected, 3, axis=1)
    mem_normed = low(layer_norm(memory, gain_state))
    mem_proj = round_both(product(mem_normed, w_state))
    mem_queries, mem_keys, mem_values = jnp.split(mem_proj, 3, axis=1)
    col_later = np.arange(2 * BLK)[None, :] >= BLK
    window = jnp.logical_and(allowed_pos, jnp.logical_or(col_later, has_prev))
    allowed = jnp.concatenate([jnp.ones((BLK, M), jnp.bool_), window], axis=1)
    pos_bias = jnp.concatenate([jnp.zeros((H, BLK, M), jnp.float32), rel_bias[:, bucket_ids]], axis=2)
    mixture = attention(queries, jnp.concatenate([mem_keys, prev_keys, key_rows]), jnp.concatenate([mem_values, prev_values, values]), pos_bias, allowed)
    attn_out = low_back(product(mixture, w_out))
    middle = block_rows + attn_out
    hidden_in = low(layer_norm(middle, gain_mlp))
    up_proj = low_back(product(hidden_in, w_up.T))
    active = low(jax.nn.gelu(up_proj, approximate=False))
    output = middle + low_back(product(active, w_down))
    mem_mixture = attention(mem_queries, jnp.concatenate([mem_keys, key_rows]), jnp.concatenate([mem_values, values]), 0.0, True)
    update = low_back(product(mem_mixture, w_update))
    gate_value = jax.nn.sigmoid(gate_bias)
    new_memory = gate_value * memory + (1.0 - gate_value) * update
    return ((new_memory, key_rows, values), output)

def forward(params, tokens, starts):
    blocks = tokens.reshape(SEQS, NBLK, BLK, D)
    has_prev = jnp.arange(NBLK) > 0
    step_fn = jax.checkpoint(partial(block_step, params))

    def one_sequence(counter, seq_items):
        seq_blocks, start_memory = seq_items
        zero_rows = jnp.zeros((BLK, D), jnp.float32)
        final_carry, outputs = lax.scan(step_fn, (start_memory, zero_rows, zero_rows), (seq_blocks, has_prev))
        return (counter, (outputs, final_carry[0]))
    counter, (outputs, finals) = lax.scan(one_sequence, jnp.zeros((), jnp.float32), (blocks, starts))
    return (outputs.reshape(TOKENS, D), finals)

def reference(tokens, state_in, gain_tok, gain_state, gain_mlp, w_tok, w_state, w_out, w_update, gate_bias, rel_bias, w_up, w_down, d_out, d_state_next):
    params = tuple((weight_arg.astype(jnp.float32) for weight_arg in (gain_tok, gain_state, gain_mlp, w_tok, w_state, w_out, w_update, gate_bias, rel_bias, w_up, w_down)))
    results, pull_back = jax.vjp(forward, params, tokens.astype(jnp.float32), state_in.astype(jnp.float32))
    grad_params, grad_tokens, grad_states = pull_back((d_out.astype(jnp.float32), d_state_next.astype(jnp.float32)))
    return (results[0].astype(jnp.bfloat16), results[1], grad_tokens, grad_states, grad_params[0], grad_params[1], grad_params[2], grad_params[3], grad_params[4], grad_params[5], grad_params[6], grad_params[7], grad_params[8], grad_params[9], grad_params[10])
```

```python
import functools
import math

import jax
import jax.numpy as jnp
import numpy as np
from jax import lax
from jax.experimental import pallas as pl
from jax.experimental.pallas import tpu as pltpu
from jax.sharding import Mesh
from jax.sharding import PartitionSpec as P


D = 1024
H = 8
HL = 4
DH = D // H
BLK = 512
M = 512
NB = 32
REACH = 128
HALF = 256
KEEP = HL * DH
NEG = -1e30
eps = 1e-06
SCALE = 1.0 / math.sqrt(DH)
BF = jnp.bfloat16
F32 = jnp.float32

AXIS_BITS = {"c": ("c", 1), "x": ("x", 1), "y": ("g", 1), "z1": ("s", 1), "z2": ("s", 2)}
VMEM_CAP = 56 * 1024 * 1024


def xch(value, bit):
    axis, mask = AXIS_BITS[bit]
    count = lax.axis_size(axis)
    return lax.ppermute(value, axis, [(i, i ^ mask) for i in range(count)])


def diag_send(value):
    return lax.ppermute(value, ("c", "x"), [(1, 2), (2, 1)])


def gather_bits(piece, order):
    held = piece
    for bit in order[:-1]:
        held = jnp.stack([held, xch(held, bit)])
    return held, xch(held, order[-1])


def reduce_bits(parts, order):
    for bit in order:
        got = xch(parts[1], bit)
        parts = (parts[0].astype(F32) + got.astype(F32)).astype(BF)
    return over_groups(parts)


def over_groups(part):
    groups = lax.axis_size("g")
    step = 2
    while step < groups:
        got = lax.ppermute(part, "g", [(i, i ^ step) for i in range(groups)])
        part = (part.astype(F32) + got.astype(F32)).astype(part.dtype)
        step *= 2
    return part


def untwist(value, bits):
    for axis, bit in enumerate(bits):
        value = jnp.where(bit == 1, jnp.flip(value, axis), value)
    return value


def mm(a, b):
    return jnp.dot(a, b, preferred_element_type=F32)


def mm_nt(a, b):
    return lax.dot_general(a, b, (((1,), (1,)), ((), ())), preferred_element_type=F32)


def mm_tn(a, b):
    return lax.dot_general(a, b, (((0,), (0,)), ((), ())), preferred_element_type=F32)


def norm_parts(values):
    centered = values - jnp.mean(values, axis=-1, keepdims=True)
    variance = jnp.mean(centered * centered, axis=-1, keepdims=True)
    rstd = lax.rsqrt(variance + eps)
    return centered * rstd, rstd


def norm_back(values, gain, grad):
    hat, rstd = norm_parts(values)
    g = grad * gain
    inner = g - jnp.mean(g, axis=-1, keepdims=True)
    inner = inner - hat * jnp.mean(g * hat, axis=-1, keepdims=True)
    return inner * rstd, grad * hat


def bucket_table(block_len, bucket_count, reach_len):
    distance = np.arange(2 * block_len + 1)
    exact = bucket_count // 2
    ratio = np.log(np.maximum(distance, 1) / exact) / np.log(reach_len / exact)
    far = np.minimum(
        exact + np.floor(ratio * (bucket_count - exact)).astype(np.int64), bucket_count - 1
    )
    return np.where(distance < exact, distance, far).astype(np.int32)


def slab_buckets():
    s = np.arange(8)[:, None]
    col = np.arange(BLK)[None, :]
    return bucket_table(BLK, NB, REACH)[(s - col) % BLK].reshape(-1)


def params(flops=0, moved=0, trans=0, grid=1):
    return dict(
        compiler_params=pltpu.CompilerParams(
            vmem_limit_bytes=VMEM_CAP, dimension_semantics=("arbitrary",) * grid
        ),
        cost_estimate=pl.CostEstimate(flops=flops, bytes_accessed=moved, transcendentals=trans),
    )


def full(shape, memory_space=None):
    return pl.BlockSpec(shape, lambda *_: (0,) * len(shape))


def pick_kernel(me, tok, st, *outs):
    c, y = me[0], me[3]
    for sub in range(3):
        for i in range(2):
            j = 6 * y + 2 * sub + i
            col = (j // HL) * D + (2 * (j % HL) + c) * DH
            src = pl.ds(pl.multiple_of(col, DH), DH)
            dst = slice(i * DH, (i + 1) * DH)
            outs[sub][0:DH, dst] = tok[:, src]
            outs[sub][DH : 2 * DH, dst] = st[:, src]


def pick_columns(me, w_tok, w_state):
    one = jax.ShapeDtypeStruct((2 * DH, 2 * DH), BF)
    return pl.pallas_call(
        pick_kernel,
        grid_spec=pltpu.PrefetchScalarGridSpec(
            num_scalar_prefetch=1,
            grid=(1,),
            in_specs=[full(w_tok.shape), full(w_state.shape)],
            out_specs=[full((2 * DH, 2 * DH))] * 3,
        ),
        out_shape=[one] * 3,
        name="pick",
        **params(moved=3 * 2**20),
    )(me, w_tok, w_state)


def lay_kernel(me, a0, a1, b0, b1, c0, c1, tok, st, small):
    q = pl.program_id(0)
    x0, y0 = me[1], me[3]
    low = lax.rem(q, 2) == 0
    c_val = jnp.where(low, c0[...], c1[...])
    for xr in range(2):
        for yr in range(2):
            va = (a0, a1)[xr][yr, 0, 0]
            vb = (b0, b1)[yr][0, xr, 0]
            vc = c_val[xr, yr, 0]
            rows = pl.ds(pl.multiple_of((x0 ^ xr) * DH, DH), DH)
            for sub, v in enumerate((va, vb, vc)):
                cols = pl.ds(pl.multiple_of((y0 ^ yr) * 768 + sub * 256, 256), 256)
                tok[rows, cols] = v[0:DH]
                st[rows, cols] = v[DH : 2 * DH]
        small[x0 ^ xr] = (a0, a1)[xr][0, 0, 0, 2 * DH : 2 * DH + 16]


def lay_tables(me, a, b, c):
    ra = a[0].shape[-2]
    a_spec = pl.BlockSpec((2, 1, 1, ra, 256), lambda q, me: (0, q % 2, q // 2, 0, 0))
    b_spec = pl.BlockSpec((1, 2, 1, 256, 256), lambda q, me: (q % 2, 0, q // 2, 0, 0))
    c_spec = pl.BlockSpec((2, 2, 1, 256, 256), lambda q, me: (0, 0, q // 2, 0, 0))
    w_spec = pl.BlockSpec((2 * DH, 3 * KEEP), lambda q, me: (q ^ me[2], 0))
    return pl.pallas_call(
        lay_kernel,
        grid_spec=pltpu.PrefetchScalarGridSpec(
            num_scalar_prefetch=1,
            grid=(4,),
            in_specs=[a_spec, a_spec, b_spec, b_spec, c_spec, c_spec],
            out_specs=[
                w_spec,
                w_spec,
                pl.BlockSpec((2, 16, 256), lambda q, me: (q ^ me[2], 0, 0)),
            ],
        ),
        out_shape=[
            jax.ShapeDtypeStruct((D, 3 * KEEP), BF),
            jax.ShapeDtypeStruct((D, 3 * KEEP), BF),
            jax.ShapeDtypeStruct((8, 16, 256), BF),
        ],
        name="lay",
        **params(moved=14 * 2**20),
    )(me, *a, *b, *c)


def lay_out_kernel(me, low, high, wo, wu):
    x0, z0, y0 = me[1], me[2], me[3]
    q = low.shape[3] // 2
    for xr in range(2):
        src = (low, high)[xr]
        for yr in range(2):
            for zr in range(4):
                v = src[yr, zr % 2, zr // 2]
                row = (z0 ^ zr) * DH + ((x0 ^ xr) * 2 + (y0 ^ yr)) * q
                rows = pl.ds(pl.multiple_of(row, q), q)
                wo[rows, :] = v[0:q]
                wu[rows, :] = v[q : 2 * q]


def lay_out_tables(me, low, high):
    one = jax.ShapeDtypeStruct((KEEP, D), BF)
    return pl.pallas_call(
        lay_out_kernel,
        grid_spec=pltpu.PrefetchScalarGridSpec(
            num_scalar_prefetch=1,
            grid=(1,),
            in_specs=[full(low.shape), full(high.shape)],
            out_specs=[full((KEEP, D))] * 2,
        ),
        out_shape=[one, one],
        name="lay_out",
        **params(moved=4 * 2**20),
    )(me, low, high)


def bias_kernel(base, out):
    slab = base[0]
    for a in range(0, 64, 2):
        two = jnp.concatenate(
            [pltpu.roll(slab, 8 * a, 1), pltpu.roll(slab, 8 * a + 8, 1)], axis=0
        )
        out[0, 8 * a : 8 * a + 16, :] = two.astype(BF)


def bias_tables(base):
    return pl.pallas_call(
        bias_kernel,
        grid=(HL,),
        in_specs=[pl.BlockSpec((1, 8, BLK), lambda h: (h, 0, 0))],
        out_specs=pl.BlockSpec((1, BLK, BLK), lambda h: (h, 0, 0)),
        out_shape=jax.ShapeDtypeStruct((HL, BLK, BLK), BF),
        name="bias",
        **params(moved=2 * 2**20),
    )(base)


def lower_mask():
    rows = lax.broadcasted_iota(jnp.int32, (HALF, HALF), 0)
    cols = lax.broadcasted_iota(jnp.int32, (HALF, HALF), 1)
    return rows >= cols


def head_lane(h):
    return lax.broadcasted_iota(jnp.int32, (HALF, DH), 1) == h


def window_scores(t, has_prev, qt, ko, kp, bias, rows, lower):
    near = bias[0, rows, rows].astype(F32)
    near_own = mm_nt(qt, ko[rows, :]) * SCALE
    if has_prev:
        near_prev = mm_nt(qt, kp[rows, :]) * SCALE
        s_near = jnp.where(lower, near_own, near_prev) + near
    else:
        s_near = jnp.where(lower, near_own + near, NEG)
    s_far = None
    if t == 1:
        s_far = mm_nt(qt, ko[0:HALF, :]) * SCALE + bias[0, rows, 0:HALF].astype(F32)
    elif has_prev:
        s_far = mm_nt(qt, kp[HALF:BLK, :]) * SCALE + bias[0, rows, HALF:BLK].astype(F32)
    s_edge = None
    if has_prev:
        pair = qt.astype(F32) * kp[rows, :].astype(F32)
        s_edge = jnp.sum(pair, axis=1, keepdims=True) * SCALE + bias[0, 0:1, 1:2].astype(F32)
    return s_near, s_far, s_edge


def tok_fwd_kernel(has_prev, *refs):
    if has_prev:
        q, km, vm, ko, vo, bias, kp, vp, out, logs = refs
    else:
        q, km, vm, ko, vo, bias, out, logs = refs
        kp = vp = None
    h = pl.program_id(0)
    lower = lower_mask()
    for t in range(2):
        rows = slice(t * HALF, (t + 1) * HALF)
        qt = q[rows, :]
        s_mem = mm_nt(qt, km[...]) * SCALE
        s_near, s_far, s_edge = window_scores(t, has_prev, qt, ko, kp, bias, rows, lower)
        top = jnp.maximum(
            jnp.max(s_mem, axis=1, keepdims=True), jnp.max(s_near, axis=1, keepdims=True)
        )
        if s_far is not None:
            top = jnp.maximum(top, jnp.max(s_far, axis=1, keepdims=True))
        if has_prev:
            top = jnp.maximum(top, s_edge)
        e_mem = jnp.exp(s_mem - top)
        e_near = jnp.exp(s_near - top)
        total = jnp.sum(e_mem, axis=1, keepdims=True) + jnp.sum(e_near, axis=1, keepdims=True)
        acc = mm(e_mem.astype(BF), vm[...])
        if has_prev:
            acc += mm(jnp.where(lower, e_near, 0.0).astype(BF), vo[rows, :])
            acc += mm(jnp.where(lower, 0.0, e_near).astype(BF), vp[rows, :])
            e_edge = jnp.exp(s_edge - top)
            total += e_edge
            acc += e_edge * vp[rows, :].astype(F32)
        else:
            acc += mm(e_near.astype(BF), vo[rows, :])
        if s_far is not None:
            e_far = jnp.exp(s_far - top)
            total += jnp.sum(e_far, axis=1, keepdims=True)
            v_far = vo[0:HALF, :] if t == 1 else vp[HALF:BLK, :]
            acc += mm(e_far.astype(BF), v_far)
        out[rows, :] = (acc / total).astype(BF)
        keep = jnp.where(h == 0, 0.0, logs[rows, :])
        logs[rows, :] = jnp.where(head_lane(h), top + jnp.log(total), keep)


def col(block, at):
    return pl.BlockSpec((BLK, DH), lambda h: (block, at * HL + h))


def tok_forward(block, proj, mem_proj, bias):
    has_prev = block > 0
    specs = [col(block, 0), col(0, 1), col(0, 2), col(block, 1), col(block, 2)]
    specs += [pl.BlockSpec((1, BLK, BLK), lambda h: (h, 0, 0))]
    ops = [proj, mem_proj, mem_proj, proj, proj, bias]
    if has_prev:
        specs += [col(block - 1, 1), col(block - 1, 2)]
        ops += [proj, proj]
    return pl.pallas_call(
        functools.partial(tok_fwd_kernel, has_prev),
        grid=(HL,),
        in_specs=specs,
        out_specs=[col(0, 0), full((BLK, DH))],
        out_shape=[
            jax.ShapeDtypeStruct((BLK, KEEP), BF),
            jax.ShapeDtypeStruct((BLK, DH), F32),
        ],
        name="tok_fwd",
        **params(flops=4 * BLK * 1280 * KEEP, moved=8 * 2**20, trans=HL * BLK * 1024),
    )(*ops)


def mem_fwd_kernel(q, ks, vs, ko, vo, out, logs):
    h = pl.program_id(0)
    for t in range(2):
        rows = slice(t * HALF, (t + 1) * HALF)
        qt = q[rows, :]
        s1 = mm_nt(qt, ks[...]) * SCALE
        s2 = mm_nt(qt, ko[...]) * SCALE
        top = jnp.maximum(jnp.max(s1, axis=1, keepdims=True), jnp.max(s2, axis=1, keepdims=True))
        e1 = jnp.exp(s1 - top)
        e2 = jnp.exp(s2 - top)
        total = jnp.sum(e1, axis=1, keepdims=True) + jnp.sum(e2, axis=1, keepdims=True)
        acc = mm(e1.astype(BF), vs[...]) + mm(e2.astype(BF), vo[...])
        out[rows, :] = (acc / total).astype(BF)
        keep = jnp.where(h == 0, 0.0, logs[rows, :])
        logs[rows, :] = jnp.where(head_lane(h), top + jnp.log(total), keep)


def mem_forward(block, proj, mem_proj):
    return pl.pallas_call(
        mem_fwd_kernel,
        grid=(HL,),
        in_specs=[col(0, 0), col(0, 1), col(0, 2), col(block, 1), col(block, 2)],
        out_specs=[col(0, 0), full((BLK, DH))],
        out_shape=[
            jax.ShapeDtypeStruct((BLK, KEEP), BF),
            jax.ShapeDtypeStruct((BLK, DH), F32),
        ],
        name="mem_fwd",
        **params(flops=4 * BLK * 1024 * KEEP, moved=4 * 2**20, trans=HL * BLK * 1024),
    )(mem_proj, mem_proj, mem_proj, proj, proj)


def head_cols(at, h):
    return pl.ds(pl.multiple_of((at * HL + h) * DH, DH), DH)


def mem_bwd_kernel(final, *refs):
    if final:
        q, ks, vs, ko, vo, do, logs, aks, avs, aq, ak, av, d_mem, d_tok, dks, dvs, dko, dvo = refs
    else:
        q, ks, vs, ko, vo, do, logs, d_mem, d_tok, dks, dvs, dko, dvo = refs
    h = pl.program_id(0)
    kind = BF if final else F32
    for t in range(2):
        rows = slice(t * HALF, (t + 1) * HALF)
        qt = q[rows, :]
        dt = do[rows, :]
        log_t = jnp.sum(jnp.where(head_lane(h), logs[rows, :], 0.0), axis=1, keepdims=True)
        p1 = jnp.exp(mm_nt(qt, ks[...]) * SCALE - log_t)
        p2 = jnp.exp(mm_nt(qt, ko[...]) * SCALE - log_t)
        w1 = mm_nt(dt, vs[...])
        w2 = mm_nt(dt, vo[...])
        inner = jnp.sum(p1 * w1, axis=1, keepdims=True) + jnp.sum(p2 * w2, axis=1, keepdims=True)
        g1 = (p1 * (w1 - inner)).astype(BF)
        g2 = (p2 * (w2 - inner)).astype(BF)
        dq = (mm(g1, ks[...]) + mm(g2, ko[...])) * SCALE
        d_mem[rows, head_cols(0, h)] = dq.astype(kind)
        terms = (
            (dks, mm_tn(g1, qt) * SCALE),
            (dko, mm_tn(g2, qt) * SCALE),
            (dvs, mm_tn(p1.astype(BF), dt)),
            (dvo, mm_tn(p2.astype(BF), dt)),
        )
        for ref, term in terms:
            if t == 0:
                ref[...] = term
            else:
                ref[...] += term
    if final:
        d_mem[:, head_cols(1, h)] = (dks[...] + aks[...]).astype(BF)
        d_mem[:, head_cols(2, h)] = (dvs[...] + avs[...]).astype(BF)
        d_tok[:, head_cols(0, h)] = aq[...].astype(BF)
        d_tok[:, head_cols(1, h)] = (dko[...] + ak[...]).astype(BF)
        d_tok[:, head_cols(2, h)] = (dvo[...] + av[...]).astype(BF)
    else:
        d_mem[:, head_cols(1, h)] = dks[...]
        d_mem[:, head_cols(2, h)] = dvs[...]
        d_tok[:, head_cols(0, h)] = dko[...]
        d_tok[:, head_cols(1, h)] = dvo[...]


def mem_backward(block, proj, mem_proj, grad_mix, logs, add_mem=None, add_tok=None):
    final = add_mem is not None
    specs = [col(0, 0), col(0, 1), col(0, 2), col(block, 1), col(block, 2), col(0, 0)]
    specs += [full((BLK, DH))]
    ops = [mem_proj, mem_proj, mem_proj, proj, proj, grad_mix, logs]
    if final:
        specs += [col(0, 0), col(0, 1), col(0, 0), col(0, 1), col(0, 2)]
        ops += [add_mem, add_mem, add_tok, add_tok, add_tok]
    kind = BF if final else F32
    wide = 3 * KEEP if final else 2 * KEEP
    return pl.pallas_call(
        functools.partial(mem_bwd_kernel, final),
        grid=(HL,),
        in_specs=specs,
        out_specs=[full((BLK, 3 * KEEP)), full((BLK, wide))],
        out_shape=[
            jax.ShapeDtypeStruct((BLK, 3 * KEEP), kind),
            jax.ShapeDtypeStruct((BLK, wide), kind),
        ],
        scratch_shapes=[pltpu.VMEM((BLK, DH), F32)] * 4,
        name="mem_bwd",
        **params(flops=10 * BLK * 1024 * KEEP, moved=9 * 2**20, trans=HL * BLK * 1024),
    )(*ops)


def tok_bwd_kernel(has_prev, *refs):
    if has_prev:
        q, km, vm, ko, vo, bias, do, logs, kp, vp, sq, sk, sv, ak, av = refs[:15]
        d_mem, d_tok, d_prev, rel, dkm, dvm, dko, dvo, dkp, dvp = refs[15:]
    else:
        q, km, vm, ko, vo, bias, do, logs, ak, av = refs[:10]
        d_mem, d_tok, rel, dkm, dvm, dko, dvo = refs[10:]
        kp = vp = None
    h = pl.program_id(0)
    lower = lower_mask()
    slab = jnp.zeros((8, BLK), F32)
    dko[...] = jnp.zeros_like(dko)
    dvo[...] = jnp.zeros_like(dvo)
    if has_prev:
        dkp[...] = jnp.zeros_like(dkp)
        dvp[...] = jnp.zeros_like(dvp)
    for t in range(2):
        rows = slice(t * HALF, (t + 1) * HALF)
        qt = q[rows, :]
        dt = do[rows, :]
        log_t = jnp.sum(jnp.where(head_lane(h), logs[rows, :], 0.0), axis=1, keepdims=True)
        p_mem = jnp.exp(mm_nt(qt, km[...]) * SCALE - log_t)
        s_near, s_far, s_edge = window_scores(t, has_prev, qt, ko, kp, bias, rows, lower)
        p_near = jnp.exp(s_near - log_t)
        w_mem = mm_nt(dt, vm[...])
        w_near = mm_nt(dt, vo[rows, :])
        inner = jnp.sum(p_mem * w_mem, axis=1, keepdims=True)
        if has_prev:
            w_near = jnp.where(lower, w_near, mm_nt(dt, vp[rows, :]))
            p_edge = jnp.exp(s_edge - log_t)
            v_edge = vp[rows, :].astype(F32)
            k_edge = kp[rows, :].astype(F32)
            w_edge = jnp.sum(dt.astype(F32) * v_edge, axis=1, keepdims=True)
            inner += p_edge * w_edge
        inner += jnp.sum(p_near * w_near, axis=1, keepdims=True)
        if s_far is not None:
            far = slice(0, HALF) if t == 1 else slice(HALF, BLK)
            k_far, v_far = (ko, vo) if t == 1 else (kp, vp)
            p_far = jnp.exp(s_far - log_t)
            w_far = mm_nt(dt, v_far[far, :])
            inner += jnp.sum(p_far * w_far, axis=1, keepdims=True)
        g_mem = (p_mem * (w_mem - inner)).astype(BF)
        g_near32 = p_near * (w_near - inner)
        g_near = g_near32.astype(BF)
        dq = mm(g_mem, km[...])
        zero = jnp.zeros((), BF)
        if has_prev:
            g_own = jnp.where(lower, g_near32, 0.0).astype(BF)
            g_prev = jnp.where(lower, 0.0, g_near32).astype(BF)
            p_own = jnp.where(lower, p_near, 0.0).astype(BF)
            p_prev = jnp.where(lower, 0.0, p_near).astype(BF)
            g_edge = (p_edge * (w_edge - inner)).astype(BF).astype(F32)
            p_edge16 = p_edge.astype(BF).astype(F32)
            dq += mm(g_prev, kp[rows, :]) + g_edge * k_edge
            dkp[rows, :] += mm_tn(g_prev, qt) + g_edge * qt.astype(F32)
            dvp[rows, :] += mm_tn(p_prev, dt) + p_edge16 * dt.astype(F32)
        else:
            g_own = g_near
            p_own = p_near.astype(BF)
        dq += mm(g_own, ko[rows, :])
        dko[rows, :] += mm_tn(g_own, qt)
        dvo[rows, :] += mm_tn(p_own, dt)
        g_far32 = jnp.zeros((HALF, HALF), F32)
        if s_far is not None:
            g_far = (p_far * (w_far - inner)).astype(BF)
            g_far32 = g_far.astype(F32)
            dq += mm(g_far, k_far[far, :])
            dk_far, dv_far = (dko, dvo) if t == 1 else (dkp, dvp)
            dk_far[far, :] += mm_tn(g_far, qt)
            dv_far[far, :] += mm_tn(p_far.astype(BF), dt)
        d_tok[rows, head_cols(0, h)] = (dq * SCALE).astype(d_tok.dtype)
        g_round = g_near.astype(F32)
        wide = [g_round, g_far32] if t == 0 else [g_far32, g_round]
        wide = jnp.concatenate(wide, axis=1)
        for a in range(HALF // 8):
            shift = (BLK - 8 * a - t * HALF) % BLK
            part = wide[8 * a : 8 * a + 8, :]
            slab = slab + (pltpu.roll(part, shift, 1) if shift else part)
        if has_prev:
            at = lax.broadcasted_iota(jnp.int32, (8, BLK), 0) * BLK
            at = at + lax.broadcasted_iota(jnp.int32, (8, BLK), 1)
            edge_sum = jnp.sum(g_edge, axis=0, keepdims=True)
            slab = slab + jnp.where(at == 1, edge_sum, 0.0)
        add_k = mm_tn(g_mem, qt)
        add_v = mm_tn(p_mem.astype(BF), dt)
        if t == 0:
            dkm[...] = add_k
            dvm[...] = add_v
        else:
            dkm[...] += add_k
            dvm[...] += add_v
    rel[0] = slab
    k_tok = dko[...] * SCALE + ak[...]
    v_tok = dvo[...] + av[...]
    d_tok[:, head_cols(1, h)] = k_tok.astype(d_tok.dtype)
    d_tok[:, head_cols(2, h)] = v_tok.astype(d_tok.dtype)
    if has_prev:
        d_mem[:, head_cols(0, h)] = sq[...].astype(BF)
        d_mem[:, head_cols(1, h)] = (dkm[...] * SCALE + sk[...]).astype(BF)
        d_mem[:, head_cols(2, h)] = (dvm[...] + sv[...]).astype(BF)
        d_prev[:, head_cols(0, h)] = dkp[...] * SCALE
        d_prev[:, head_cols(1, h)] = dvp[...]
    else:
        d_mem[:, head_cols(0, h)] = dkm[...] * SCALE
        d_mem[:, head_cols(1, h)] = dvm[...]


def tok_backward(block, proj, mem_proj, bias, grad_mix, logs, add_tok, add_mem=None):
    has_prev = block > 0
    specs = [col(block, 0), col(0, 1), col(0, 2), col(block, 1), col(block, 2)]
    specs += [pl.BlockSpec((1, BLK, BLK), lambda h: (h, 0, 0)), col(block, 0), full((BLK, DH))]
    ops = [proj, mem_proj, mem_proj, proj, proj, bias, grad_mix, logs]
    scratch = 4
    if has_prev:
        specs += [col(block - 1, 1), col(block - 1, 2), col(0, 0), col(0, 1), col(0, 2)]
        ops += [proj, proj, add_mem, add_mem, add_mem]
        scratch = 6
    specs += [col(0, 0), col(0, 1)]
    ops += [add_tok, add_tok]
    kind = BF if has_prev else F32
    rel_spec = pl.BlockSpec((1, 8, BLK), lambda h: (h, 0, 0))
    rel_shape = jax.ShapeDtypeStruct((HL, 8, BLK), F32)
    wide = 3 * KEEP if has_prev else 2 * KEEP
    out_specs = [full((BLK, wide)), full((BLK, 3 * KEEP))]
    out_shape = [
        jax.ShapeDtypeStruct((BLK, wide), kind),
        jax.ShapeDtypeStruct((BLK, 3 * KEEP), kind),
    ]
    if has_prev:
        out_specs.append(full((BLK, 2 * KEEP)))
        out_shape.append(jax.ShapeDtypeStruct((BLK, 2 * KEEP), F32))
    return pl.pallas_call(
        functools.partial(tok_bwd_kernel, has_prev),
        grid=(HL,),
        in_specs=specs,
        out_specs=out_specs + [rel_spec],
        out_shape=out_shape + [rel_shape],
        scratch_shapes=[pltpu.VMEM((BLK, DH), F32)] * scratch,
        name="tok_bwd",
        **params(flops=10 * BLK * 1280 * KEEP, moved=12 * 2**20, trans=HL * BLK * 1024),
    )(*ops)


def normal_parts(u):
    bell = jnp.exp(-0.5 * (u * u))
    t = 1.0 / (1.0 + (0.3275911 * math.sqrt(0.5)) * jnp.abs(u))
    poly = 1.061405429 * t - 1.453152027
    poly = poly * t + 1.421413741
    poly = poly * t - 0.284496736
    poly = poly * t + 0.254829592
    tail = (0.5 * poly) * (t * bell)
    return jnp.where(u >= 0, 1.0 - tail, tail), bell * (1.0 / math.sqrt(2.0 * math.pi))


def mlp_kernel(
    h0, h1, d0, d1, ua, ub, da, db, gu, gd, o0, o1, e0, e1, acc_o0, acc_o1, acc_e0, acc_e1
):
    t = pl.program_id(0)
    wu = jnp.where(t < 4, ua[...], ub[...])
    wd = jnp.where(lax.rem(t, 2) == 0, da[...], db[...])
    for r in range(2):
        h = (h0, h1)[r]
        d = (d0, d1)[r]
        acc_o = (acc_o0, acc_o1)[r]
        acc_e = (acc_e0, acc_e1)[r]
        u = mm_nt(h[...], wu)
        dg = mm_nt(d[...], wd)
        phi, pdf = normal_parts(u)
        g = (u * phi).astype(BF)
        du = (dg * (phi + u * pdf)).astype(BF)
        if r == 0:
            g_first, du_first = g, du
        o_term = mm(g, wd)
        e_term = mm(du, wu)

        @pl.when(t == 0)
        def _():
            acc_o[...] = o_term
            acc_e[...] = e_term

        @pl.when(t > 0)
        def _():
            acc_o[...] += o_term
            acc_e[...] += e_term

    gd[...] = (mm_tn(g_first, d0[...]) + mm_tn(g, d1[...])).astype(BF)
    gu[...] = (mm_tn(du_first, h0[...]) + mm_tn(du, h1[...])).astype(BF)

    @pl.when(t == 7)
    def _():
        o0[...] = acc_o0[...]
        o1[...] = acc_o1[...].astype(BF)
        e0[...] = acc_e0[...]
        e1[...] = acc_e1[...].astype(BF)


def mlp(h0, h1, d0, d1, ua, ub, da, db):
    act = full((BLK, D))
    tile = functools.partial(pl.BlockSpec, (HALF, D))
    return pl.pallas_call(
        mlp_kernel,
        grid=(8,),
        in_specs=[act] * 4
        + [
            tile(lambda t: (jnp.minimum(t, 3), 0)),
            tile(lambda t: (jnp.maximum(t - 4, 0), 0)),
            tile(lambda t: (t // 2, 0)),
            tile(lambda t: (t // 2, 0)),
        ],
        out_specs=[
            tile(lambda t: (((t // 2) % 2) * 4 + (t // 4) * 2 + t % 2, 0)),
            tile(lambda t: ((t // 4) * 4 + (t % 2) * 2 + (t // 2) % 2, 0)),
            act,
            act,
            act,
            act,
        ],
        out_shape=[
            jax.ShapeDtypeStruct((8 * HALF, D), BF),
            jax.ShapeDtypeStruct((8 * HALF, D), BF),
            jax.ShapeDtypeStruct((BLK, D), F32),
            jax.ShapeDtypeStruct((BLK, D), BF),
            jax.ShapeDtypeStruct((BLK, D), F32),
            jax.ShapeDtypeStruct((BLK, D), BF),
        ],
        scratch_shapes=[pltpu.VMEM((BLK, D), F32)] * 4,
        name="mlp",
        **params(flops=12 * D * D * 2 * D, moved=26 * 2**20, trans=4 * 2**20),
    )(h0, h1, d0, d1, ua, ub, da, db)


def proj_grad_kernel(me, xa, xb, sa, sb, pa, pb, ra, rb, out_a, out_b, out_c, tok, st):
    x0, y0 = me[1], me[3]
    tok[...] = mm_tn(xa[...], pa[...]) + mm_tn(xb[...], pb[...])
    st[...] = mm_tn(sa[...], ra[...]) + mm_tn(sb[...], rb[...])
    for xr in range(2):
        rows = pl.ds(pl.multiple_of((x0 ^ xr) * DH, DH), DH)
        for yr in range(2):
            dests = (out_a.at[xr, yr, 0, 0], out_b.at[yr, 0, xr, 0], out_c.at[0, xr, yr, 0])
            for sub, ref in enumerate(dests):
                cols = pl.ds(pl.multiple_of((y0 ^ yr) * 768 + sub * 256, 256), 256)
                ref[0:DH, :] = tok[rows, cols].astype(BF)
                ref[DH : 2 * DH, :] = st[rows, cols].astype(BF)


def proj_grads(me, xn, sn0, sn1, dp0, dp1, dr0, dr1):
    lhs = pl.BlockSpec((BLK, 2 * DH), lambda q, me: (0, q ^ me[2]))
    lhs1 = pl.BlockSpec((BLK, 2 * DH), lambda q, me: (1, q ^ me[2]))
    rhs = full((BLK, 3 * KEEP))
    shape = jax.ShapeDtypeStruct((2, 2, 2, 2, 2 * DH, 2 * DH), BF)
    tail = (2 * DH, 2 * DH)
    return pl.pallas_call(
        proj_grad_kernel,
        grid_spec=pltpu.PrefetchScalarGridSpec(
            num_scalar_prefetch=1,
            grid=(4,),
            in_specs=[lhs, lhs1, lhs, lhs, rhs, rhs, rhs, rhs],
            out_specs=[
                pl.BlockSpec((2, 2, 1, 1) + tail, lambda q, me: (0, 0, q % 2, q // 2, 0, 0)),
                pl.BlockSpec((2, 1, 2, 1) + tail, lambda q, me: (0, q % 2, 0, q // 2, 0, 0)),
                pl.BlockSpec((1, 2, 2, 1) + tail, lambda q, me: (q % 2, 0, 0, q // 2, 0, 0)),
            ],
            scratch_shapes=[pltpu.VMEM((2 * DH, 3 * KEEP), F32)] * 2,
        ),
        out_shape=[shape] * 3,
        name="proj_grad",
        **params(flops=4 * D * D * 3 * KEEP, moved=16 * 2**20),
    )(me, xn, xn, sn0, sn1, dp0, dp1, dr0, dr1)


def place_proj_kernel(me, p00, p01, p10, p11, tok, st):
    c0, y0 = me[0], me[3]
    for cr in range(2):
        for yr in range(2):
            src = ((p00, p01), (p10, p11))[cr][yr]
            for sub in range(3):
                for i in range(2):
                    j = 6 * (y0 ^ yr) + 2 * sub + i
                    at = (j // HL) * D + (2 * (j % HL) + (c0 ^ cr)) * DH
                    dst = pl.ds(pl.multiple_of(at, DH), DH)
                    cols = slice(i * DH, (i + 1) * DH)
                    tok[:, dst] = src[sub, 0:DH, cols].astype(F32)
                    st[:, dst] = src[sub, DH : 2 * DH, cols].astype(F32)


def place_proj(me, p00, p01, p10, p11):
    one = jax.ShapeDtypeStruct((DH, 3 * D), F32)
    return pl.pallas_call(
        place_proj_kernel,
        grid_spec=pltpu.PrefetchScalarGridSpec(
            num_scalar_prefetch=1,
            grid=(1,),
            in_specs=[full(p00.shape)] * 4,
            out_specs=[full((DH, 3 * D))] * 2,
        ),
        out_shape=[one, one],
        name="place_proj",
        **params(moved=5 * 2**20),
    )(me, p00, p01, p10, p11)


def place_mlp_kernel(me, p00, p01, p10, p11, up, down):
    c0, y0 = me[0], me[3]
    n = p00.shape[1]
    for cr in range(2):
        for yr in range(2):
            src = ((p00, p01), (p10, p11))[cr][yr]
            rows = pl.ds(pl.multiple_of(((c0 ^ cr) * 2 + (y0 ^ yr)) * n, n), n)
            up[rows, :] = src[0].astype(F32)
            down[rows, :] = src[1].astype(F32)


def place_mlp(me, p00, p01, p10, p11):
    one = jax.ShapeDtypeStruct((4 * p00.shape[1], D), F32)
    return pl.pallas_call(
        place_mlp_kernel,
        grid_spec=pltpu.PrefetchScalarGridSpec(
            num_scalar_prefetch=1,
            grid=(1,),
            in_specs=[full(p00.shape)] * 4,
            out_specs=[full(one.shape)] * 2,
        ),
        out_shape=[one, one],
        name="place_mlp",
        **params(moved=6 * 2**20),
    )(me, p00, p01, p10, p11)


def body(
    tokens,
    state_in,
    gain_tok,
    gain_state,
    gain_mlp,
    w_tok,
    w_state,
    w_out,
    w_update,
    gate_bias,
    rel_bias,
    w_up,
    w_down,
    d_out,
    d_state_next,
):
    c = lax.axis_index("c")
    x = lax.axis_index("x")
    z = lax.axis_index("s")
    y = lax.axis_index("g") % 2
    z1, z2 = z % 2, z // 2
    me = jnp.stack([c, x, z, y]).astype(jnp.int32)
    on_diag = c == x
    slots = state_in.shape[0]
    srows = state_in.shape[1]

    def cross(value):
        return jnp.where(on_diag, value, diag_send(value))

    def by_block(own, other):
        return jnp.where(c == 0, jnp.concatenate([own, other]), jnp.concatenate([other, own]))

    def my_half(rows):
        return lax.dynamic_slice_in_dim(rows, c * HALF, HALF, 0)

    def other_half(rows):
        return lax.dynamic_slice_in_dim(rows, (1 - c) * HALF, HALF, 0)

    def slot_rows(value):
        held = cross(value)
        parts = [lax.dynamic_index_in_dim(held, z, 0, keepdims=False)]
        for k in range(1, slots):
            send = lax.dynamic_index_in_dim(held, z ^ k, 0, keepdims=False)
            parts.append(lax.ppermute(send, "s", [(i, i ^ k) for i in range(slots)]))
        half = jnp.concatenate(parts)
        return by_block(half, xch(half, "c"))

    def owner_rows(half):
        parts = half.reshape(slots, srows, D)
        got = [parts[0]]
        for k in range(1, slots):
            got.append(lax.ppermute(parts[k], "s", [(i, i ^ k) for i in range(slots)]))
        stacked = jnp.stack(got).reshape(2, 2, srows, D)
        stacked = untwist(stacked, (z2, z1)).reshape(slots, srows, D)
        return cross(stacked).astype(F32)

    subs = pick_columns(me, w_tok, w_state)
    small = jnp.stack([gain_tok, gain_state, gain_mlp, gate_bias])
    small = jnp.concatenate([small, jnp.pad(rel_bias, ((0, 0), (0, DH - NB)))])
    small = jnp.pad(small, ((0, 11), (0, DH)))
    x_own = cross(tokens)
    x_oth = xch(x_own, "c")
    tab_a = gather_bits(jnp.concatenate([subs[0], small]), ("z2", "z1", "y", "x"))
    tab_b = gather_bits(subs[1], ("z2", "x", "z1", "y"))
    tab_c = gather_bits(subs[2], ("z2", "y", "x", "z1"))
    state0 = slot_rows(state_in).astype(F32)
    w_tok_l, w_state_l, small_all = lay_tables(me, tab_a, tab_b, tab_c)

    quarter = DH // 4
    at = (c * 2 + y) * quarter
    out_piece = cross(
        jnp.concatenate(
            [
                lax.dynamic_slice_in_dim(w_out, at, quarter, 0),
                lax.dynamic_slice_in_dim(w_update, at, quarter, 0),
            ]
        )
    )
    out_low, out_high = gather_bits(out_piece, ("z2", "z1", "y", "x"))
    wo, wu = lay_out_tables(me, out_low, out_high)
    hid = w_up.shape[0] // 4
    hid_at = (c * 2 + y) * hid
    up_a, up_b = gather_bits(
        lax.dynamic_slice_in_dim(w_up, hid_at, hid, 0), ("z2", "z1", "x", "y")
    )
    down_a, down_b = gather_bits(
        lax.dynamic_slice_in_dim(w_down, hid_at, hid, 0), ("z2", "x", "y", "z1")
    )
    d_own = cross(d_out)
    d_oth = xch(d_own, "c")
    ds2 = slot_rows(d_state_next).astype(F32)

    vectors = small_all[:, :4, :DH].transpose(1, 0, 2).reshape(4, D).astype(F32)
    g_tok, g_state, g_mlp = vectors[0], vectors[1], vectors[2]
    gate = jax.nn.sigmoid(vectors[3])
    rel_rows = small_all[:, 4, :NB].reshape(HL, 2, NB)
    rel_mine = lax.dynamic_index_in_dim(rel_rows, c, 1, keepdims=False)
    hot = jnp.asarray(slab_buckets())[None, :] == jnp.arange(NB, dtype=jnp.int32)[:, None]
    base = mm(rel_mine, hot.astype(BF)).reshape(HL, 8, BLK)
    bias = bias_tables(base)

    rows = by_block(x_own, x_oth).astype(F32)
    xn = (norm_parts(rows)[0] * g_tok).astype(BF)
    proj = mm(xn, w_tok_l).astype(BF)

    sn0 = (norm_parts(state0)[0] * g_state).astype(BF)
    r0 = mm(sn0, w_state_l).astype(BF)
    os0, log_s0 = mem_forward(0, proj, r0)
    zp0 = mm(os0, wu)
    zz0 = zp0 + xch(zp0.astype(BF), "c").astype(F32)
    state1 = gate * state0 + (1.0 - gate) * zz0
    sn1 = (norm_parts(state1)[0] * g_state).astype(BF)
    r1 = mm(sn1, w_state_l).astype(BF)

    ot0, log_t0 = tok_forward(0, proj, r0, bias)
    ot1, log_t1 = tok_forward(1, proj, r1, bias)
    part0, part1 = mm(ot0, wo), mm(ot1, wo)
    part_own = jnp.where(c == 0, part0, part1)
    part_oth = jnp.where(c == 0, part1, part0).astype(BF)
    mid = x_own.astype(F32) + part_own + xch(part_oth, "c").astype(F32)
    h_own = (norm_parts(mid)[0] * g_mlp).astype(BF)
    h_oth = xch(h_own, "c")

    os1, log_s1 = mem_forward(1, proj, r1)
    zp1 = mm(os1, wu)
    zz1 = my_half(zp1) + xch(other_half(zp1).astype(BF), "c").astype(F32)
    state1_half = my_half(state1)
    state2_half = gate * state1_half + (1.0 - gate) * zz1
    state_next = owner_rows(state2_half.astype(BF))

    dz1 = ((1.0 - gate) * ds2).astype(BF)
    dos1 = mm_nt(dz1, wu).astype(BF)
    dm1, dt1 = mem_backward(1, proj, r1, dos1, log_s1)

    gu, gd, o_own, o_oth, e_own, e_oth = mlp(
        h_own,
        h_oth,
        d_own,
        d_oth,
        up_a.reshape(-1, D),
        up_b.reshape(-1, D),
        down_a.reshape(-1, D),
        down_b.reshape(-1, D),
    )
    output = mid + o_own + xch(o_oth, "c").astype(F32)
    output = cross(output.astype(BF))
    gu = gu.reshape(2, 2, 2, 2, hid, D)
    gd = gd.reshape(2, 2, 2, 2, hid, D)
    gu = reduce_bits(gu, ("x", "y", "z1", "z2"))
    gd = reduce_bits(gd, ("y", "z1", "x", "z2"))

    dh = e_own + xch(e_oth, "c").astype(F32)
    back, gain_rows = norm_back(mid, g_mlp, dh)
    grad_g_mlp = jnp.sum(gain_rows, axis=0)
    dmid = d_own.astype(F32) + back
    da_own = dmid.astype(BF)
    da = by_block(da_own, xch(da_own, "c"))
    dot_all = mm_nt(da, wo).astype(BF)
    grad_wo = mm_tn(ot0, da[:BLK]) + mm_tn(ot1, da[BLK:])

    dr1, dp1, dprev, rel1 = tok_backward(1, proj, r1, bias, dot_all, log_t1, dt1, dm1)
    dsn1p = mm_nt(dr1, w_state_l)
    dsn1 = dsn1p + xch(dsn1p.astype(BF), "c").astype(F32)
    back1, gain1 = norm_back(state1, g_state, dsn1)
    ds1 = gate * ds2 + back1
    dz0 = ((1.0 - gate) * ds1).astype(BF)
    dos0 = mm_nt(dz0, wu).astype(BF)
    dm0, dt0, rel0 = tok_backward(0, proj, r0, bias, dot_all, log_t0, dprev)
    dr0, dp0 = mem_backward(0, proj, r0, dos0, log_s0, dm0, dt0)

    subs = proj_grads(me, xn, sn0, sn1, dp0, dp1, dr0, dr1)
    ga = reduce_bits(subs[0], ("x", "y", "z1", "z2"))
    gb = reduce_bits(subs[1], ("y", "z1", "x", "z2"))
    gc = reduce_bits(subs[2], ("z1", "x", "y", "z2"))
    grad_wu = mm_tn(os0, dz0) + mm_tn(os1, dz1)

    dsn0p = mm_nt(dr0, w_state_l)
    dsn0 = my_half(dsn0p) + xch(other_half(dsn0p).astype(BF), "c").astype(F32)
    back0, gain0 = norm_back(my_half(state0), g_state, dsn0)
    grad_state = owner_rows((gate * my_half(ds1) + back0).astype(BF))
    grad_g_state = jnp.sum(my_half(gain1) + gain0, axis=0)
    gate_rows = my_half(ds2) * (state1_half - zz1) + my_half(ds1) * my_half(state0 - zz0)
    grad_gate = jnp.sum(gate_rows, axis=0) * gate * (1.0 - gate)

    dxn0, dxn1 = mm_nt(dp0, w_tok_l), mm_nt(dp1, w_tok_l)
    dxn_own = jnp.where(c == 0, dxn0, dxn1)
    dxn_oth = jnp.where(c == 0, dxn1, dxn0).astype(BF)
    dxn = dxn_own + xch(dxn_oth, "c").astype(F32)
    back_x, gain_x = norm_back(x_own.astype(F32), g_tok, dxn)
    grad_g_tok = jnp.sum(gain_x, axis=0)
    grad_tokens = cross((dmid + back_x).astype(BF)).astype(F32)

    rel_sum = (rel0 + rel1).reshape(HL, 8 * BLK)
    grad_rel = lax.dot_general(
        rel_sum,
        hot.astype(F32),
        (((1,), (1,)), ((), ())),
        precision=lax.Precision.HIGHEST,
        preferred_element_type=F32,
    )
    both = jnp.stack([grad_rel, jnp.zeros_like(grad_rel)], axis=1)
    both = jnp.where(c == 0, both, jnp.flip(both, 1)).reshape(1, H * NB)
    vec = jnp.stack([grad_g_tok, grad_g_state, grad_g_mlp, grad_gate])
    vec = jnp.concatenate([vec, jnp.pad(both, ((0, 3), (0, D - H * NB)))])
    for bit in ("c", "x", "y", "z1", "z2"):
        vec = vec + xch(vec, bit)
    vec = over_groups(vec)
    spot = z * 2 + x
    own = lax.dynamic_slice_in_dim(vec[:4], spot * DH, DH, 1)
    rel_own = lax.dynamic_slice_in_dim(vec[4:5], spot * NB, NB, 1)

    outs = jnp.stack([grad_wo, grad_wu]).astype(BF).reshape(2, 2, 2, 2, 2, quarter, D)
    spots = {"z2": z2, "z1": z1, "x": x, "y": y}
    names = ["z2", "z1", "x", "y"]
    for bit in ("z1", "y", "x", "z2"):
        axis = names.index(bit) + 1
        names.remove(bit)
        keep = lax.dynamic_index_in_dim(outs, spots[bit], axis, keepdims=False)
        send = lax.dynamic_index_in_dim(outs, 1 - spots[bit], axis, keepdims=False)
        outs = (keep.astype(F32) + xch(send, bit).astype(F32)).astype(BF)
    outs = over_groups(outs)
    outs = jnp.stack([outs, xch(outs, "y")])
    outs = jnp.stack([outs, xch(outs, "x")])
    outs = untwist(outs, (x, y)).transpose(2, 0, 1, 3, 4).reshape(2, DH, D)
    outs = jnp.where(on_diag, outs, xch(outs, "c")).astype(F32)

    def spread(part):
        other = xch(part, "y")
        return part, other, xch(part, "c"), xch(other, "c")

    grad_up, grad_down = place_mlp(me, *spread(jnp.stack([gu, gd])))
    grad_tok_w, grad_state_w = place_proj(me, *spread(jnp.stack([ga, gb, gc])))

    return (
        output,
        state_next,
        grad_tokens,
        grad_state,
        own[0],
        own[1],
        own[2],
        grad_tok_w,
        grad_state_w,
        outs[0],
        outs[1],
        own[3],
        rel_own,
        grad_up,
        grad_down,
    )


def solution(mesh):
    reps, shards = mesh.devices.shape
    grid = Mesh(mesh.devices.reshape(reps // 2, 2, shards // 2, 2), ("g", "c", "s", "x"))
    rep, shard = ("g", "c"), ("s", "x")
    every = rep + shard
    by_token = P(every, None)
    by_state = P(rep, shard, None)
    line = P(shard)
    table = P(shard, None)
    params_spec = (line, line, line, table, table, table, table, line, table, table, table)
    return jax.shard_map(
        body,
        mesh=grid,
        in_specs=(by_token, by_state) + params_spec + (by_token, by_state),
        out_specs=(by_token, by_state, by_token, by_state) + params_spec,
        check_vma=False,
    )
```

```python
import functools
import math

import jax
import jax.numpy as jnp
import numpy as np
from jax import lax
from jax.experimental import pallas as pl
from jax.experimental.pallas import tpu as pltpu
from jax.sharding import Mesh
from jax.sharding import PartitionSpec as P


D = 1024
H = 8
HL = 4
DH = D // H
BLK = 512
M = 512
NB = 32
REACH = 128
HALF = 256
KEEP = HL * DH
NEG = -1e30
eps = 1e-06
SCALE = 1.0 / math.sqrt(DH)
BF = jnp.bfloat16
F32 = jnp.float32

AXIS_BITS = {"c": ("c", 1), "x": ("x", 1), "y": ("y", 1), "z1": ("s", 1), "z2": ("s", 2)}
VMEM_MLP = 44
VMEM_GRADS = 56
VMEM_MOST = 18
COST_CUT = 10


def xch(value, bit):
    axis, mask = AXIS_BITS[bit]
    count = lax.axis_size(axis)
    return lax.ppermute(value, axis, [(i, i ^ mask) for i in range(count)])


def diag_send(value):
    return lax.ppermute(value, ("c", "x"), [(1, 2), (2, 1)])


def over_groups(part):
    groups = lax.axis_size("h")
    step = 1
    while step < groups:
        got = lax.ppermute(part, "h", [(i, i ^ step) for i in range(groups)])
        part = (part.astype(F32) + got.astype(F32)).astype(part.dtype)
        step *= 2
    return part


def fence(values, done):
    leaves, tree = jax.tree.flatten(values)
    tied = lax.optimization_barrier(tuple(leaves) + tuple(jax.tree.leaves(done)))
    return jax.tree.unflatten(tree, tied[: len(leaves)])


def untwist(value, bits):
    for axis, bit in enumerate(bits):
        value = jnp.where(bit == 1, jnp.flip(value, axis), value)
    return value


def mm(a, b):
    return jnp.dot(a, b, preferred_element_type=F32)


def mm_nt(a, b):
    return lax.dot_general(a, b, (((1,), (1,)), ((), ())), preferred_element_type=F32)


def mm_tn(a, b):
    return lax.dot_general(a, b, (((0,), (0,)), ((), ())), preferred_element_type=F32)


def norm_parts(values):
    centered = values - jnp.mean(values, axis=-1, keepdims=True)
    variance = jnp.mean(centered * centered, axis=-1, keepdims=True)
    rstd = lax.rsqrt(variance + eps)
    return centered * rstd, rstd


def norm_back(values, gain, grad):
    hat, rstd = norm_parts(values)
    g = grad * gain
    inner = g - jnp.mean(g, axis=-1, keepdims=True)
    inner = inner - hat * jnp.mean(g * hat, axis=-1, keepdims=True)
    return inner * rstd, grad * hat


def bucket_table(block_len, bucket_count, reach_len):
    distance = np.arange(2 * block_len + 1)
    exact = bucket_count // 2
    ratio = np.log(np.maximum(distance, 1) / exact) / np.log(reach_len / exact)
    far = np.minimum(
        exact + np.floor(ratio * (bucket_count - exact)).astype(np.int64), bucket_count - 1
    )
    return np.where(distance < exact, distance, far).astype(np.int32)


def slab_buckets():
    s = np.arange(8)[:, None]
    col = np.arange(BLK)[None, :]
    return bucket_table(BLK, NB, REACH)[(s - col) % BLK].reshape(-1)


def params(flops=0, moved=0, trans=0, grid=1, vmem=VMEM_MOST):
    return dict(
        compiler_params=pltpu.CompilerParams(
            vmem_limit_bytes=vmem * 2**20, dimension_semantics=("arbitrary",) * grid
        ),
        cost_estimate=pl.CostEstimate(
            flops=flops // COST_CUT, bytes_accessed=moved // COST_CUT, transcendentals=0
        ),
    )


def full(shape, memory_space=None):
    return pl.BlockSpec(
        shape, lambda *_: (0,) * len(shape), pipeline_mode=pl.Buffered(buffer_count=1)
    )


def pick_kernel(me, tok, st, *outs):
    c, y = me[0], me[3]
    for sub in range(3):
        for i in range(2):
            j = 6 * y + 2 * sub + i
            col = (j // HL) * D + (2 * (j % HL) + c) * DH
            src = pl.ds(pl.multiple_of(col, DH), DH)
            dst = slice(i * DH, (i + 1) * DH)
            outs[sub][0:DH, dst] = tok[:, src]
            outs[sub][DH : 2 * DH, dst] = st[:, src]


def pick_columns(me, w_tok, w_state):
    one = jax.ShapeDtypeStruct((2 * DH, 2 * DH), BF)
    return pl.pallas_call(
        pick_kernel,
        grid_spec=pltpu.PrefetchScalarGridSpec(
            num_scalar_prefetch=1,
            grid=(1,),
            in_specs=[full(w_tok.shape), full(w_state.shape)],
            out_specs=[full((2 * DH, 2 * DH))] * 3,
        ),
        out_shape=[one] * 3,
        name="pick",
        **params(moved=3 * 2**20),
    )(me, w_tok, w_state)


def lay_kernel(me, a0, a1, b0, b1, c0, c1, tok, st, small):
    q = pl.program_id(0)
    x0, y0 = me[1], me[3]
    low = lax.rem(q, 2) == 0
    c_val = jnp.where(low, c0[...], c1[...])
    for xr in range(2):
        for yr in range(2):
            va = (a0, a1)[xr][yr, 0, 0]
            vb = (b0, b1)[yr][0, xr, 0]
            vc = c_val[xr, yr, 0]
            rows = pl.ds(pl.multiple_of((x0 ^ xr) * DH, DH), DH)
            for sub, v in enumerate((va, vb, vc)):
                cols = pl.ds(pl.multiple_of((y0 ^ yr) * 768 + sub * 256, 256), 256)
                tok[rows, cols] = v[0:DH]
                st[rows, cols] = v[DH : 2 * DH]
        small[x0 ^ xr] = (a0, a1)[xr][0, 0, 0, 2 * DH : 2 * DH + 16]


def lay_tables(me, a, b, c):
    ra = a[0].shape[-2]
    a_spec = pl.BlockSpec((2, 1, 1, ra, 256), lambda q, me: (0, q % 2, q // 2, 0, 0))
    b_spec = pl.BlockSpec((1, 2, 1, 256, 256), lambda q, me: (q % 2, 0, q // 2, 0, 0))
    c_spec = pl.BlockSpec((2, 2, 1, 256, 256), lambda q, me: (0, 0, q // 2, 0, 0))
    w_spec = pl.BlockSpec((2 * DH, 3 * KEEP), lambda q, me: (q ^ me[2], 0))
    return pl.pallas_call(
        lay_kernel,
        grid_spec=pltpu.PrefetchScalarGridSpec(
            num_scalar_prefetch=1,
            grid=(4,),
            in_specs=[a_spec, a_spec, b_spec, b_spec, c_spec, c_spec],
            out_specs=[
                w_spec,
                w_spec,
                pl.BlockSpec((2, 16, 256), lambda q, me: (q ^ me[2], 0, 0)),
            ],
        ),
        out_shape=[
            jax.ShapeDtypeStruct((D, 3 * KEEP), BF),
            jax.ShapeDtypeStruct((D, 3 * KEEP), BF),
            jax.ShapeDtypeStruct((8, 16, 256), BF),
        ],
        name="lay",
        **params(moved=14 * 2**20),
    )(me, *a, *b, *c)


def lay_out_kernel(me, low, high, wo, wu):
    x0, z0, y0 = me[1], me[2], me[3]
    q = low.shape[3] // 2
    for yr in range(2):
        src = (low, high)[yr]
        for xr in range(2):
            for zr in range(4):
                v = src[xr, zr % 2, zr // 2]
                row = (z0 ^ zr) * DH + ((x0 ^ xr) * 2 + (y0 ^ yr)) * q
                rows = pl.ds(pl.multiple_of(row, q), q)
                wo[rows, :] = v[0:q]
                wu[rows, :] = v[q : 2 * q]


def lay_out_tables(me, low, high):
    one = jax.ShapeDtypeStruct((KEEP, D), BF)
    return pl.pallas_call(
        lay_out_kernel,
        grid_spec=pltpu.PrefetchScalarGridSpec(
            num_scalar_prefetch=1,
            grid=(1,),
            in_specs=[full(low.shape), full(high.shape)],
            out_specs=[full((KEEP, D))] * 2,
        ),
        out_shape=[one, one],
        name="lay_out",
        **params(moved=4 * 2**20),
    )(me, low, high)


def bias_kernel(base, out):
    slab = base[0]
    for a in range(0, 64, 2):
        two = jnp.concatenate(
            [pltpu.roll(slab, 8 * a, 1), pltpu.roll(slab, 8 * a + 8, 1)], axis=0
        )
        out[0, 8 * a : 8 * a + 16, :] = two.astype(BF)


def bias_tables(base):
    return pl.pallas_call(
        bias_kernel,
        grid=(HL,),
        in_specs=[pl.BlockSpec((1, 8, BLK), lambda h: (h, 0, 0))],
        out_specs=pl.BlockSpec((1, BLK, BLK), lambda h: (h, 0, 0)),
        out_shape=jax.ShapeDtypeStruct((HL, BLK, BLK), BF),
        name="bias",
        **params(moved=2 * 2**20),
    )(base)


def lower_mask():
    rows = lax.broadcasted_iota(jnp.int32, (HALF, HALF), 0)
    cols = lax.broadcasted_iota(jnp.int32, (HALF, HALF), 1)
    return rows >= cols


def head_lane(h):
    return lax.broadcasted_iota(jnp.int32, (HALF, DH), 1) == h


def window_scores(t, has_prev, qt, ko, kp, bias, rows, lower):
    near = bias[0, rows, rows].astype(F32)
    near_own = mm_nt(qt, ko[rows, :]) * SCALE
    if has_prev:
        near_prev = mm_nt(qt, kp[rows, :]) * SCALE
        s_near = jnp.where(lower, near_own, near_prev) + near
    else:
        s_near = jnp.where(lower, near_own + near, NEG)
    s_far = None
    if t == 1:
        s_far = mm_nt(qt, ko[0:HALF, :]) * SCALE + bias[0, rows, 0:HALF].astype(F32)
    elif has_prev:
        s_far = mm_nt(qt, kp[HALF:BLK, :]) * SCALE + bias[0, rows, HALF:BLK].astype(F32)
    s_edge = None
    if has_prev:
        pair = qt.astype(F32) * kp[rows, :].astype(F32)
        s_edge = jnp.sum(pair, axis=1, keepdims=True) * SCALE + bias[0, 0:1, 1:2].astype(F32)
    return s_near, s_far, s_edge


def tok_fwd_kernel(has_prev, *refs):
    if has_prev:
        q, km, vm, ko, vo, bias, kp, vp, out, logs = refs
    else:
        q, km, vm, ko, vo, bias, out, logs = refs
        kp = vp = None
    h = pl.program_id(0)
    lower = lower_mask()
    for t in range(2):
        rows = slice(t * HALF, (t + 1) * HALF)
        qt = q[rows, :]
        s_mem = mm_nt(qt, km[...]) * SCALE
        s_near, s_far, s_edge = window_scores(t, has_prev, qt, ko, kp, bias, rows, lower)
        top = jnp.maximum(
            jnp.max(s_mem, axis=1, keepdims=True), jnp.max(s_near, axis=1, keepdims=True)
        )
        if s_far is not None:
            top = jnp.maximum(top, jnp.max(s_far, axis=1, keepdims=True))
        if has_prev:
            top = jnp.maximum(top, s_edge)
        e_mem = jnp.exp(s_mem - top)
        e_near = jnp.exp(s_near - top)
        total = jnp.sum(e_mem, axis=1, keepdims=True) + jnp.sum(e_near, axis=1, keepdims=True)
        acc = mm(e_mem.astype(BF), vm[...])
        if has_prev:
            acc += mm(jnp.where(lower, e_near, 0.0).astype(BF), vo[rows, :])
            acc += mm(jnp.where(lower, 0.0, e_near).astype(BF), vp[rows, :])
            e_edge = jnp.exp(s_edge - top)
            total += e_edge
            acc += e_edge * vp[rows, :].astype(F32)
        else:
            acc += mm(e_near.astype(BF), vo[rows, :])
        if s_far is not None:
            e_far = jnp.exp(s_far - top)
            total += jnp.sum(e_far, axis=1, keepdims=True)
            v_far = vo[0:HALF, :] if t == 1 else vp[HALF:BLK, :]
            acc += mm(e_far.astype(BF), v_far)
        out[rows, :] = (acc / total).astype(BF)
        keep = jnp.where(h == 0, 0.0, logs[rows, :])
        logs[rows, :] = jnp.where(head_lane(h), top + jnp.log(total), keep)


def col(block, at):
    return pl.BlockSpec((BLK, DH), lambda h: (block, at * HL + h))


def tok_forward(block, proj, mem_proj, bias):
    has_prev = block > 0
    specs = [col(block, 0), col(0, 1), col(0, 2), col(block, 1), col(block, 2)]
    specs += [pl.BlockSpec((1, BLK, BLK), lambda h: (h, 0, 0))]
    ops = [proj, mem_proj, mem_proj, proj, proj, bias]
    if has_prev:
        specs += [col(block - 1, 1), col(block - 1, 2)]
        ops += [proj, proj]
    return pl.pallas_call(
        functools.partial(tok_fwd_kernel, has_prev),
        grid=(HL,),
        in_specs=specs,
        out_specs=[col(0, 0), full((BLK, DH))],
        out_shape=[
            jax.ShapeDtypeStruct((BLK, KEEP), BF),
            jax.ShapeDtypeStruct((BLK, DH), F32),
        ],
        name="tok_fwd",
        **params(flops=4 * BLK * 1280 * KEEP, moved=8 * 2**20, trans=HL * BLK * 1024),
    )(*ops)


def mem_fwd_kernel(q, ks, vs, ko, vo, out, logs):
    h = pl.program_id(0)
    for t in range(2):
        rows = slice(t * HALF, (t + 1) * HALF)
        qt = q[rows, :]
        s1 = mm_nt(qt, ks[...]) * SCALE
        s2 = mm_nt(qt, ko[...]) * SCALE
        top = jnp.maximum(jnp.max(s1, axis=1, keepdims=True), jnp.max(s2, axis=1, keepdims=True))
        e1 = jnp.exp(s1 - top)
        e2 = jnp.exp(s2 - top)
        total = jnp.sum(e1, axis=1, keepdims=True) + jnp.sum(e2, axis=1, keepdims=True)
        acc = mm(e1.astype(BF), vs[...]) + mm(e2.astype(BF), vo[...])
        out[rows, :] = (acc / total).astype(BF)
        keep = jnp.where(h == 0, 0.0, logs[rows, :])
        logs[rows, :] = jnp.where(head_lane(h), top + jnp.log(total), keep)


def mem_forward(block, proj, mem_proj):
    return pl.pallas_call(
        mem_fwd_kernel,
        grid=(HL,),
        in_specs=[col(0, 0), col(0, 1), col(0, 2), col(block, 1), col(block, 2)],
        out_specs=[col(0, 0), full((BLK, DH))],
        out_shape=[
            jax.ShapeDtypeStruct((BLK, KEEP), BF),
            jax.ShapeDtypeStruct((BLK, DH), F32),
        ],
        name="mem_fwd",
        **params(flops=4 * BLK * 1024 * KEEP, moved=4 * 2**20, trans=HL * BLK * 1024),
    )(mem_proj, mem_proj, mem_proj, proj, proj)


def head_cols(at, h):
    return pl.ds(pl.multiple_of((at * HL + h) * DH, DH), DH)


def mem_bwd_kernel(final, *refs):
    if final:
        q, ks, vs, ko, vo, do, logs, aks, avs, aq, ak, av, d_mem, d_tok, dks, dvs, dko, dvo = refs
    else:
        q, ks, vs, ko, vo, do, logs, d_mem, d_tok, dks, dvs, dko, dvo = refs
    h = pl.program_id(0)
    kind = BF if final else F32
    for t in range(2):
        rows = slice(t * HALF, (t + 1) * HALF)
        qt = q[rows, :]
        dt = do[rows, :]
        log_t = jnp.sum(jnp.where(head_lane(h), logs[rows, :], 0.0), axis=1, keepdims=True)
        p1 = jnp.exp(mm_nt(qt, ks[...]) * SCALE - log_t)
        p2 = jnp.exp(mm_nt(qt, ko[...]) * SCALE - log_t)
        w1 = mm_nt(dt, vs[...])
        w2 = mm_nt(dt, vo[...])
        inner = jnp.sum(p1 * w1, axis=1, keepdims=True) + jnp.sum(p2 * w2, axis=1, keepdims=True)
        g1 = (p1 * (w1 - inner)).astype(BF)
        g2 = (p2 * (w2 - inner)).astype(BF)
        dq = (mm(g1, ks[...]) + mm(g2, ko[...])) * SCALE
        d_mem[rows, head_cols(0, h)] = dq.astype(kind)
        terms = (
            (dks, mm_tn(g1, qt) * SCALE),
            (dko, mm_tn(g2, qt) * SCALE),
            (dvs, mm_tn(p1.astype(BF), dt)),
            (dvo, mm_tn(p2.astype(BF), dt)),
        )
        for ref, term in terms:
            if t == 0:
                ref[...] = term
            else:
                ref[...] += term
    if final:
        d_mem[:, head_cols(1, h)] = (dks[...] + aks[...]).astype(BF)
        d_mem[:, head_cols(2, h)] = (dvs[...] + avs[...]).astype(BF)
        d_tok[:, head_cols(0, h)] = aq[...].astype(BF)
        d_tok[:, head_cols(1, h)] = (dko[...] + ak[...]).astype(BF)
        d_tok[:, head_cols(2, h)] = (dvo[...] + av[...]).astype(BF)
    else:
        d_mem[:, head_cols(1, h)] = dks[...]
        d_mem[:, head_cols(2, h)] = dvs[...]
        d_tok[:, head_cols(0, h)] = dko[...]
        d_tok[:, head_cols(1, h)] = dvo[...]


def mem_backward(block, proj, mem_proj, grad_mix, logs, add_mem=None, add_tok=None):
    final = add_mem is not None
    specs = [col(0, 0), col(0, 1), col(0, 2), col(block, 1), col(block, 2), col(0, 0)]
    specs += [full((BLK, DH))]
    ops = [mem_proj, mem_proj, mem_proj, proj, proj, grad_mix, logs]
    if final:
        specs += [col(0, 0), col(0, 1), col(0, 0), col(0, 1), col(0, 2)]
        ops += [add_mem, add_mem, add_tok, add_tok, add_tok]
    kind = BF if final else F32
    wide = 3 * KEEP if final else 2 * KEEP
    return pl.pallas_call(
        functools.partial(mem_bwd_kernel, final),
        grid=(HL,),
        in_specs=specs,
        out_specs=[full((BLK, 3 * KEEP)), full((BLK, wide))],
        out_shape=[
            jax.ShapeDtypeStruct((BLK, 3 * KEEP), kind),
            jax.ShapeDtypeStruct((BLK, wide), kind),
        ],
        scratch_shapes=[pltpu.VMEM((BLK, DH), F32)] * 4,
        name="mem_bwd",
        **params(flops=10 * BLK * 1024 * KEEP, moved=9 * 2**20, trans=HL * BLK * 1024),
    )(*ops)


def tok_bwd_kernel(has_prev, *refs):
    if has_prev:
        q, km, vm, ko, vo, bias, do, logs, kp, vp, sq, sk, sv, ak, av = refs[:15]
        d_mem, d_tok, d_prev, rel, dkm, dvm, dko, dvo, dkp, dvp = refs[15:]
    else:
        q, km, vm, ko, vo, bias, do, logs, ak, av = refs[:10]
        d_mem, d_tok, rel, dkm, dvm, dko, dvo = refs[10:]
        kp = vp = None
    h = pl.program_id(0)
    lower = lower_mask()
    slab = jnp.zeros((8, BLK), F32)
    dko[...] = jnp.zeros_like(dko)
    dvo[...] = jnp.zeros_like(dvo)
    if has_prev:
        dkp[...] = jnp.zeros_like(dkp)
        dvp[...] = jnp.zeros_like(dvp)
    for t in range(2):
        rows = slice(t * HALF, (t + 1) * HALF)
        qt = q[rows, :]
        dt = do[rows, :]
        log_t = jnp.sum(jnp.where(head_lane(h), logs[rows, :], 0.0), axis=1, keepdims=True)
        p_mem = jnp.exp(mm_nt(qt, km[...]) * SCALE - log_t)
        s_near, s_far, s_edge = window_scores(t, has_prev, qt, ko, kp, bias, rows, lower)
        p_near = jnp.exp(s_near - log_t)
        w_mem = mm_nt(dt, vm[...])
        w_near = mm_nt(dt, vo[rows, :])
        inner = jnp.sum(p_mem * w_mem, axis=1, keepdims=True)
        if has_prev:
            w_near = jnp.where(lower, w_near, mm_nt(dt, vp[rows, :]))
            p_edge = jnp.exp(s_edge - log_t)
            v_edge = vp[rows, :].astype(F32)
            k_edge = kp[rows, :].astype(F32)
            w_edge = jnp.sum(dt.astype(F32) * v_edge, axis=1, keepdims=True)
            inner += p_edge * w_edge
        inner += jnp.sum(p_near * w_near, axis=1, keepdims=True)
        if s_far is not None:
            far = slice(0, HALF) if t == 1 else slice(HALF, BLK)
            k_far, v_far = (ko, vo) if t == 1 else (kp, vp)
            p_far = jnp.exp(s_far - log_t)
            w_far = mm_nt(dt, v_far[far, :])
            inner += jnp.sum(p_far * w_far, axis=1, keepdims=True)
        g_mem = (p_mem * (w_mem - inner)).astype(BF)
        g_near32 = p_near * (w_near - inner)
        g_near = g_near32.astype(BF)
        dq = mm(g_mem, km[...])
        zero = jnp.zeros((), BF)
        if has_prev:
            g_own = jnp.where(lower, g_near32, 0.0).astype(BF)
            g_prev = jnp.where(lower, 0.0, g_near32).astype(BF)
            p_own = jnp.where(lower, p_near, 0.0).astype(BF)
            p_prev = jnp.where(lower, 0.0, p_near).astype(BF)
            g_edge = (p_edge * (w_edge - inner)).astype(BF).astype(F32)
            p_edge16 = p_edge.astype(BF).astype(F32)
            dq += mm(g_prev, kp[rows, :]) + g_edge * k_edge
            dkp[rows, :] += mm_tn(g_prev, qt) + g_edge * qt.astype(F32)
            dvp[rows, :] += mm_tn(p_prev, dt) + p_edge16 * dt.astype(F32)
        else:
            g_own = g_near
            p_own = p_near.astype(BF)
        dq += mm(g_own, ko[rows, :])
        dko[rows, :] += mm_tn(g_own, qt)
        dvo[rows, :] += mm_tn(p_own, dt)
        g_far32 = jnp.zeros((HALF, HALF), F32)
        if s_far is not None:
            g_far = (p_far * (w_far - inner)).astype(BF)
            g_far32 = g_far.astype(F32)
            dq += mm(g_far, k_far[far, :])
            dk_far, dv_far = (dko, dvo) if t == 1 else (dkp, dvp)
            dk_far[far, :] += mm_tn(g_far, qt)
            dv_far[far, :] += mm_tn(p_far.astype(BF), dt)
        d_tok[rows, head_cols(0, h)] = (dq * SCALE).astype(d_tok.dtype)
        g_round = g_near.astype(F32)
        wide = [g_round, g_far32] if t == 0 else [g_far32, g_round]
        wide = jnp.concatenate(wide, axis=1)
        for a in range(HALF // 8):
            shift = (BLK - 8 * a - t * HALF) % BLK
            part = wide[8 * a : 8 * a + 8, :]
            slab = slab + (pltpu.roll(part, shift, 1) if shift else part)
        if has_prev:
            at = lax.broadcasted_iota(jnp.int32, (8, BLK), 0) * BLK
            at = at + lax.broadcasted_iota(jnp.int32, (8, BLK), 1)
            edge_sum = jnp.sum(g_edge, axis=0, keepdims=True)
            slab = slab + jnp.where(at == 1, edge_sum, 0.0)
        add_k = mm_tn(g_mem, qt)
        add_v = mm_tn(p_mem.astype(BF), dt)
        if t == 0:
            dkm[...] = add_k
            dvm[...] = add_v
        else:
            dkm[...] += add_k
            dvm[...] += add_v
    rel[0] = slab
    k_tok = dko[...] * SCALE + ak[...]
    v_tok = dvo[...] + av[...]
    d_tok[:, head_cols(1, h)] = k_tok.astype(d_tok.dtype)
    d_tok[:, head_cols(2, h)] = v_tok.astype(d_tok.dtype)
    if has_prev:
        d_mem[:, head_cols(0, h)] = sq[...].astype(BF)
        d_mem[:, head_cols(1, h)] = (dkm[...] * SCALE + sk[...]).astype(BF)
        d_mem[:, head_cols(2, h)] = (dvm[...] + sv[...]).astype(BF)
        d_prev[:, head_cols(0, h)] = dkp[...] * SCALE
        d_prev[:, head_cols(1, h)] = dvp[...]
    else:
        d_mem[:, head_cols(0, h)] = dkm[...] * SCALE
        d_mem[:, head_cols(1, h)] = dvm[...]


def tok_backward(block, proj, mem_proj, bias, grad_mix, logs, add_tok, add_mem=None):
    has_prev = block > 0
    specs = [col(block, 0), col(0, 1), col(0, 2), col(block, 1), col(block, 2)]
    specs += [pl.BlockSpec((1, BLK, BLK), lambda h: (h, 0, 0)), col(block, 0), full((BLK, DH))]
    ops = [proj, mem_proj, mem_proj, proj, proj, bias, grad_mix, logs]
    scratch = 4
    if has_prev:
        specs += [col(block - 1, 1), col(block - 1, 2), col(0, 0), col(0, 1), col(0, 2)]
        ops += [proj, proj, add_mem, add_mem, add_mem]
        scratch = 6
    specs += [col(0, 0), col(0, 1)]
    ops += [add_tok, add_tok]
    kind = BF if has_prev else F32
    rel_spec = pl.BlockSpec((1, 8, BLK), lambda h: (h, 0, 0))
    rel_shape = jax.ShapeDtypeStruct((HL, 8, BLK), F32)
    wide = 3 * KEEP if has_prev else 2 * KEEP
    out_specs = [full((BLK, wide)), full((BLK, 3 * KEEP))]
    out_shape = [
        jax.ShapeDtypeStruct((BLK, wide), kind),
        jax.ShapeDtypeStruct((BLK, 3 * KEEP), kind),
    ]
    if has_prev:
        out_specs.append(full((BLK, 2 * KEEP)))
        out_shape.append(jax.ShapeDtypeStruct((BLK, 2 * KEEP), F32))
    return pl.pallas_call(
        functools.partial(tok_bwd_kernel, has_prev),
        grid=(HL,),
        in_specs=specs,
        out_specs=out_specs + [rel_spec],
        out_shape=out_shape + [rel_shape],
        scratch_shapes=[pltpu.VMEM((BLK, DH), F32)] * scratch,
        name="tok_bwd",
        **params(flops=10 * BLK * 1280 * KEEP, moved=12 * 2**20, trans=HL * BLK * 1024),
    )(*ops)


def normal_parts(u):
    bell = jnp.exp(-0.5 * (u * u))
    t = 1.0 / (1.0 + (0.3275911 * math.sqrt(0.5)) * jnp.abs(u))
    poly = 1.061405429 * t - 1.453152027
    poly = poly * t + 1.421413741
    poly = poly * t - 0.284496736
    poly = poly * t + 0.254829592
    tail = (0.5 * poly) * (t * bell)
    return jnp.where(u >= 0, 1.0 - tail, tail), bell * (1.0 / math.sqrt(2.0 * math.pi))


MAIN = 96
REST = DH - MAIN
TILE = 4 * DH


def mlp_kernel(h0, h1, d0, d1, u0, u1, w0, w1, *refs):
    a_keep, a_send, b_keep, b_send, c_keep, c_send, o0, o1, e0, e1 = refs[:10]
    accs = refs[10:]
    t = pl.program_id(0)
    in_x, in_y = t // 2, lax.rem(t, 2)

    @pl.when(t == 0)
    def _():
        for ref in accs:
            ref[...] = jnp.zeros_like(ref)

    wu = jnp.where(in_y == 0, u0[...], u1[...])
    wd = jnp.concatenate([w0[...], w1[...]], axis=0)
    kept = []
    for r in range(2):
        h = (h0, h1)[r]
        d = (d0, d1)[r]
        u = mm_nt(h[...], wu)
        dg = mm_nt(d[...], wd)
        phi, pdf = normal_parts(u)
        g = (u * phi).astype(BF)
        du = (dg * (phi + u * pdf)).astype(BF)
        accs[r][...] += mm(g, wd)
        accs[2 + r][...] += mm(du, wu)
        kept.append((g, du))
    gd = (mm_tn(kept[0][0], d0[...]) + mm_tn(kept[1][0], d1[...])).astype(BF)
    gu = (mm_tn(kept[0][1], h0[...]) + mm_tn(kept[1][1], h1[...])).astype(BF)
    gd, gu = gd.reshape(4, DH, D), gu.reshape(4, DH, D)
    for z1 in range(2):
        side = (c_keep, c_send)[z1]
        for z2 in range(2):
            side[0, 0, z2, 0:REST, :] = gu[2 * z1 + z2, MAIN:, :]
            side[0, 0, z2, REST:, :] = gd[2 * z1 + z2, MAIN:, :]
    for bit in range(2):

        @pl.when(in_x == bit)
        def _():
            for z in range(4):
                (a_keep, a_send)[bit][0, z // 2, z % 2] = gu[z, 0:MAIN, :]

        @pl.when(in_y == bit)
        def _():
            for z in range(4):
                (b_keep, b_send)[bit][z // 2, 0, z % 2] = gd[z, 0:MAIN, :]

    @pl.when(t == pl.num_programs(0) - 1)
    def _():
        o0[...] = accs[0][...]
        o1[...] = accs[1][...].astype(BF)
        e0[...] = accs[2][...]
        e1[...] = accs[3][...].astype(BF)


def mlp(h0, h1, d0, d1, u0, u1, w0, w1):
    act = full((BLK, D))
    up0 = pl.BlockSpec((TILE, D), lambda t: (t // 2, 0))
    up1 = pl.BlockSpec((TILE, D), lambda t: (t // 2, 0))
    down = pl.BlockSpec((TILE // 2, D), lambda t: ((t % 2) * 2 + t // 2, 0))
    tail = (MAIN, D)
    a_keep = pl.BlockSpec((1, 2, 2) + tail, lambda t: (jnp.minimum(t, 1), 0, 0, 0, 0))
    a_send = pl.BlockSpec((1, 2, 2) + tail, lambda t: (jnp.maximum(t - 2, 0), 0, 0, 0, 0))
    b_keep = pl.BlockSpec((2, 1, 2) + tail, lambda t: (0, t // 2, 0, 0, 0))
    b_send = pl.BlockSpec((2, 1, 2) + tail, lambda t: (0, t // 3, 0, 0, 0))
    c_spec = pl.BlockSpec((1, 1, 2, 2 * REST, D), lambda t: (t // 2, t % 2, 0, 0, 0))
    big_shape = jax.ShapeDtypeStruct((2, 2, 2, MAIN, D), BF)
    rest_shape = jax.ShapeDtypeStruct((2, 2, 2, 2 * REST, D), BF)
    return pl.pallas_call(
        mlp_kernel,
        grid=(4,),
        in_specs=[act] * 4 + [up0, up1, down, down],
        out_specs=[a_keep, a_send, b_keep, b_send, c_spec, c_spec] + [act] * 4,
        scratch_shapes=[pltpu.VMEM((BLK, D), F32)] * 4,
        out_shape=[big_shape] * 4
        + [rest_shape] * 2
        + [
            jax.ShapeDtypeStruct((BLK, D), F32),
            jax.ShapeDtypeStruct((BLK, D), BF),
            jax.ShapeDtypeStruct((BLK, D), F32),
            jax.ShapeDtypeStruct((BLK, D), BF),
        ],
        name="mlp",
        **params(flops=12 * D * D * 2 * D, moved=26 * 2**20, vmem=VMEM_MLP),
    )(h0, h1, d0, d1, u0, u1, w0, w1)


def halves_kernel(*refs):
    count = len(refs) // 4
    for keep, got, out_keep, out_send in zip(
        refs[:count], refs[count : 2 * count], refs[2 * count :: 2], refs[2 * count + 1 :: 2]
    ):
        out_keep[...] = (keep[0].astype(F32) + got[0].astype(F32)).astype(BF)
        out_send[...] = (keep[1].astype(F32) + got[1].astype(F32)).astype(BF)


def add_halves(keeps, gots):
    shapes = [k.shape for k in keeps]
    flat = [k.reshape(2, -1, k.shape[-1]) for k in keeps]
    flat_got = [g.reshape(2, -1, g.shape[-1]) for g in gots]
    steps = 4
    while any((k.shape[1] // steps) % 16 or k.shape[1] % steps for k in flat):
        steps //= 2
    ins, outs, out_shapes = [], [], []
    for k in flat:
        rows, width = k.shape[1] // steps, k.shape[2]
        ins.append(pl.BlockSpec((2, rows, width), lambda t: (0, t, 0)))
        outs += [pl.BlockSpec((rows, width), lambda t: (t, 0))] * 2
        out_shapes += [jax.ShapeDtypeStruct(k.shape[1:], BF)] * 2
    done = pl.pallas_call(
        halves_kernel,
        grid=(steps,),
        in_specs=ins * 2,
        out_specs=outs,
        out_shape=out_shapes,
        name="halves",
        **params(),
    )(*flat, *flat_got)
    done = [d.reshape(sh[1:]) for d, sh in zip(done, [s for s in shapes for _ in range(2)])]
    return done[0::2], done[1::2]


def eight_rows(values):
    return jnp.sum(values.reshape(-1, 8, values.shape[-1]), axis=0)


def mid_back_kernel(mid, gain, e_own, e_got, d_own, o_own, o_got, dmid, da, out, gsum):
    rows = mid[...]
    back, gain_rows = norm_back(rows, gain[...], e_own[...] + e_got[...].astype(F32))
    total = d_own[...].astype(F32) + back
    dmid[...] = total
    da[...] = total.astype(BF)
    out[...] = (rows + o_own[...] + o_got[...].astype(F32)).astype(BF)

    @pl.when(pl.program_id(0) == 0)
    def _():
        gsum[...] = jnp.zeros_like(gsum)

    gsum[...] += eight_rows(gain_rows)


def mid_back(mid, gain, e_own, e_got, d_own, o_own, o_got):
    row = pl.BlockSpec((DH, D), lambda t: (t, 0))
    return pl.pallas_call(
        mid_back_kernel,
        grid=(BLK // DH,),
        in_specs=[row, full((1, D))] + [row] * 5,
        out_specs=[row, row, row, full((8, D))],
        out_shape=[
            jax.ShapeDtypeStruct((BLK, D), F32),
            jax.ShapeDtypeStruct((BLK, D), BF),
            jax.ShapeDtypeStruct((BLK, D), BF),
            jax.ShapeDtypeStruct((8, D), F32),
        ],
        name="mid_back",
        **params(vmem=VMEM_GRADS),
    )(mid, gain, e_own, e_got, d_own, o_own, o_got)


def out_back_kernel(me, own, oth, wo, ot0, ot1, dot_all, grad):
    first = me[0] == 0
    da0 = jnp.where(first, own[...], oth[...])
    da1 = jnp.where(first, oth[...], own[...])
    dot_all[0:BLK, :] = mm_nt(da0, wo[...]).astype(BF)
    dot_all[BLK:, :] = mm_nt(da1, wo[...]).astype(BF)
    grad[...] = (mm_tn(ot0[...], da0) + mm_tn(ot1[...], da1)).astype(BF)


def out_back(me, own, oth, wo, ot0, ot1):
    return pl.pallas_call(
        out_back_kernel,
        grid_spec=pltpu.PrefetchScalarGridSpec(
            num_scalar_prefetch=1,
            grid=(1,),
            in_specs=[full((BLK, D))] * 2 + [full((KEEP, D))] + [full((BLK, KEEP))] * 2,
            out_specs=[full((2 * BLK, KEEP)), full((KEEP, D))],
        ),
        out_shape=[
            jax.ShapeDtypeStruct((2 * BLK, KEEP), BF),
            jax.ShapeDtypeStruct((KEEP, D), BF),
        ],
        name="out_back",
        **params(vmem=VMEM_GRADS),
    )(me, own, oth, wo, ot0, ot1)


def proj_back_kernel(me, a, b, w, own, oth):
    first = me[0] == 0
    own[...] = mm_nt(jnp.where(first, a[...], b[...]), w[...])
    oth[...] = mm_nt(jnp.where(first, b[...], a[...]), w[...]).astype(BF)


def proj_both_kernel(me, a, b, w, own, oth):
    term = mm_nt(a[...], w[...])
    own[...] = term
    oth[...] = term.astype(BF)


def proj_back(me, a, b, w):
    kernel = proj_both_kernel if b is None else proj_back_kernel
    rows = a.shape[0] // 2 if b is a else a.shape[0]
    side = 1 if b is a else 0
    return pl.pallas_call(
        kernel,
        grid_spec=pltpu.PrefetchScalarGridSpec(
            num_scalar_prefetch=1,
            grid=(4,),
            in_specs=[
                pl.BlockSpec((rows, 3 * KEEP), lambda t, me: (0, 0)),
                pl.BlockSpec((rows, 3 * KEEP), lambda t, me: (side, 0)),
                pl.BlockSpec((D // 4, 3 * KEEP), lambda t, me: (t, 0)),
            ],
            out_specs=[pl.BlockSpec((rows, D // 4), lambda t, me: (0, t))] * 2,
        ),
        out_shape=[
            jax.ShapeDtypeStruct((rows, D), F32),
            jax.ShapeDtypeStruct((rows, D), BF),
        ],
        name="proj_back",
        **params(),
    )(me, a, a if b is None else b, w)


def state_back_kernel(me, *refs):
    state1, gain, own, got, ds2, gate, wu, os0, os1, dz1, zz1, state0, zz0 = refs[:13]
    ds1, dos0, grad_wu, gate_sum, acc = refs[13:]
    t = pl.program_id(0)
    last = ds2[...]
    back = norm_back(state1[...], gain[...], own[...] + got[...].astype(F32))[0]
    total = gate[...] * last + back
    ds1[...] = total
    dz0 = ((1.0 - gate[...]) * total).astype(BF)
    dos0[...] = mm_nt(dz0, wu[...]).astype(BF)

    @pl.when(t == 0)
    def _():
        acc[...] = jnp.zeros_like(acc)
        gate_sum[...] = jnp.zeros_like(gate_sum)

    acc[...] += mm_tn(os0[...], dz0) + mm_tn(os1[...], dz1[...])

    @pl.when(t // 2 == me[0])
    def _():
        terms = last * (state1[...] - zz1[...]) + total * (state0[...] - zz0[...])
        gate_sum[...] += eight_rows(terms)

    @pl.when(t == 3)
    def _():
        grad_wu[...] = acc[...].astype(BF)


def state_back(me, state1, gain, own, got, ds2, gate, wu, os0, os1, dz1, zz1, state0, zz0):
    row = pl.BlockSpec((DH, D), lambda t, me: (t, 0))
    head = pl.BlockSpec((DH, KEEP), lambda t, me: (t, 0))
    half = pl.BlockSpec((DH, D), lambda t, me: (t % 2, 0))
    line = full((1, D))
    return pl.pallas_call(
        state_back_kernel,
        grid_spec=pltpu.PrefetchScalarGridSpec(
            num_scalar_prefetch=1,
            grid=(4,),
            in_specs=[row, line, row, row, row, line, full((KEEP, D)), head, head, row, half]
            + [row, row],
            out_specs=[row, head, full((KEEP, D)), full((8, D))],
            scratch_shapes=[pltpu.VMEM((KEEP, D), F32)],
        ),
        out_shape=[
            jax.ShapeDtypeStruct((BLK, D), F32),
            jax.ShapeDtypeStruct((BLK, KEEP), BF),
            jax.ShapeDtypeStruct((KEEP, D), BF),
            jax.ShapeDtypeStruct((8, D), F32),
        ],
        name="state_back",
        **params(vmem=VMEM_GRADS),
    )(me, state1, gain, own, got, ds2, gate, wu, os0, os1, dz1, zz1, state0, zz0)


def row_back_kernel(me, values, gain, own, got, scale, base, out):
    back = norm_back(values[...].astype(F32), gain[...], own[...] + got[...].astype(F32))[0]
    out[...] = (scale[...] * base[...] + back).astype(BF)


def row_back(me, values, gain, own, got, scale, base):
    count = own.shape[0] // DH
    skip = values.shape[0] // DH - count
    row = pl.BlockSpec((DH, D), lambda t, me: (t, 0))
    mine = pl.BlockSpec((DH, D), lambda t, me: (me[0] * skip + t, 0))
    return pl.pallas_call(
        row_back_kernel,
        grid_spec=pltpu.PrefetchScalarGridSpec(
            num_scalar_prefetch=1,
            grid=(count,),
            in_specs=[mine, full((1, D)), row, row, full((1, D)), mine],
            out_specs=row,
        ),
        out_shape=jax.ShapeDtypeStruct(own.shape, BF),
        name="row_back",
        **params(vmem=VMEM_GRADS),
    )(me, values, gain, own, got, scale, base)


def proj_grad_kernel(me, *refs):
    xa, xb, sa, sb, pa, pb, ra, rb, small = refs[:9]
    a_keep, a_send, b_keep, b_send, c_keep, c_send, tok, st = refs[9:]
    x0, y0 = me[1], me[3]
    in_z = lax.rem(pl.program_id(0), 2)
    tok[...] = mm_tn(xa[...], pa[...]) + mm_tn(xb[...], pb[...])
    st[...] = mm_tn(sa[...], ra[...]) + mm_tn(sb[...], rb[...])

    def write(ref, xr, yr, sub):
        rows = pl.ds(pl.multiple_of((x0 ^ xr) * DH, DH), DH)
        cols = pl.ds(pl.multiple_of((y0 ^ yr) * 768 + sub * 256, 256), 256)
        ref[0:DH, :] = tok[rows, cols].astype(BF)
        ref[DH : 2 * DH, :] = st[rows, cols].astype(BF)

    for xr in range(2):
        for yr in range(2):
            write((a_keep, a_send)[xr].at[yr, 0, 0], xr, yr, 0)
            (a_keep, a_send)[xr][yr, 0, 0, 2 * DH :, :] = small[x0 ^ xr, y0 ^ yr]
            write((b_keep, b_send)[yr].at[0, xr, 0], xr, yr, 1)
    for zb in range(2):

        @pl.when(in_z == zb)
        def _():
            for xr in range(2):
                for yr in range(2):
                    write((c_keep, c_send)[zb].at[xr, yr, 0], xr, yr, 2)


def proj_grads(me, xn, sn0, sn1, dp0, dp1, dr0, dr1, small):
    lhs = pl.BlockSpec((BLK, 2 * DH), lambda q, me: (0, q ^ me[2]))
    lhs1 = pl.BlockSpec((BLK, 2 * DH), lambda q, me: (1, q ^ me[2]))
    rhs = full((BLK, 3 * KEEP))
    shape = jax.ShapeDtypeStruct((2, 2, 2, 2 * DH, 2 * DH), BF)
    tall = jax.ShapeDtypeStruct((2, 2, 2, 2 * DH + 16, 2 * DH), BF)
    tail = (2 * DH, 2 * DH)
    a_tail = (2 * DH + 16, 2 * DH)
    a_spec = pl.BlockSpec((2, 1, 1) + a_tail, lambda q, me: (0, q % 2, q // 2, 0, 0))
    small_spec = pl.BlockSpec((2, 2, 16, 256), lambda q, me: (q ^ me[2], 0, 0, 0))
    b_spec = pl.BlockSpec((1, 2, 1) + tail, lambda q, me: (q % 2, 0, q // 2, 0, 0))
    c_spec = pl.BlockSpec((2, 2, 1) + tail, lambda q, me: (0, 0, q // 2, 0, 0))
    return pl.pallas_call(
        proj_grad_kernel,
        grid_spec=pltpu.PrefetchScalarGridSpec(
            num_scalar_prefetch=1,
            grid=(4,),
            in_specs=[lhs, lhs1, lhs, lhs, rhs, rhs, rhs, rhs, small_spec],
            out_specs=[a_spec, a_spec, b_spec, b_spec, c_spec, c_spec],
            scratch_shapes=[pltpu.VMEM((2 * DH, 3 * KEEP), F32)] * 2,
        ),
        out_shape=[tall] * 2 + [shape] * 4,
        name="proj_grad",
        **params(flops=4 * D * D * 3 * KEEP, moved=16 * 2**20, vmem=VMEM_GRADS),
    )(me, xn, xn, sn0, sn1, dp0, dp1, dr0, dr1, small)


def place_proj_kernel(me, p0, p1, w_tok, w_state, tok, st, gain_tok, gain_st, small):
    c0, y0 = me[0], me[3]
    starts = (0, 2 * DH + 16, 4 * DH + 16)
    for cr in range(2):
        for yr in range(2):
            src = (p0, p1)[cr].at[yr]
            for sub in range(3):
                for i in range(2):
                    j = 6 * (y0 ^ yr) + 2 * sub + i
                    at = (j // HL) * D + (2 * (j % HL) + (c0 ^ cr)) * DH
                    dst = pl.ds(pl.multiple_of(at, DH), DH)
                    cols = slice(i * DH, (i + 1) * DH)
                    row = starts[sub]
                    tok[:, dst] = src[row : row + DH, cols].astype(F32)
                    st[:, dst] = src[row + DH : row + 2 * DH, cols].astype(F32)
    for yr in range(2):
        first = p0[yr, 2 * DH : 2 * DH + 16, :].astype(F32)
        small[y0 ^ yr] = first + p1[yr, 2 * DH : 2 * DH + 16, :].astype(F32)
    ones = jnp.ones((8, 3 * D), F32)
    for out, grad, weight in ((gain_tok, tok, w_tok), (gain_st, st, w_state)):
        out[...] = lax.dot_general(
            ones,
            grad[...] * weight[...].astype(F32),
            (((1,), (1,)), ((), ())),
            precision=lax.Precision.HIGHEST,
            preferred_element_type=F32,
        )


def place_proj(me, p0, p1, w_tok, w_state):
    one = jax.ShapeDtypeStruct((DH, 3 * D), F32)
    line = jax.ShapeDtypeStruct((8, DH), F32)
    return pl.pallas_call(
        place_proj_kernel,
        grid_spec=pltpu.PrefetchScalarGridSpec(
            num_scalar_prefetch=1,
            grid=(1,),
            in_specs=[full(p0.shape)] * 2 + [full(w_tok.shape)] * 2,
            out_specs=[full((DH, 3 * D))] * 2 + [full((8, DH))] * 2 + [full((2, 16, 256))],
        ),
        out_shape=[one, one, line, line, jax.ShapeDtypeStruct((2, 16, 256), F32)],
        name="place_proj",
        **params(moved=5 * 2**20),
    )(me, p0, p1, w_tok, w_state)


def place_mlp_kernel(me, p0, p1, up, down):
    c0, y0 = me[0], me[3]
    for cr in range(2):
        for yr in range(2):
            src = (p0, p1)[cr].at[yr]
            row = ((c0 ^ cr) * 2 + (y0 ^ yr)) * DH
            big = pl.ds(pl.multiple_of(row, DH), MAIN)
            rest = pl.ds(pl.multiple_of(row + MAIN, REST), REST)
            up[big, :] = src[0:MAIN].astype(F32)
            down[big, :] = src[MAIN : 2 * MAIN].astype(F32)
            up[rest, :] = src[2 * MAIN : 2 * MAIN + REST].astype(F32)
            down[rest, :] = src[2 * MAIN + REST :].astype(F32)


def place_mlp(me, p0, p1):
    one = jax.ShapeDtypeStruct((2 * p0.shape[1], D), F32)
    return pl.pallas_call(
        place_mlp_kernel,
        grid_spec=pltpu.PrefetchScalarGridSpec(
            num_scalar_prefetch=1,
            grid=(1,),
            in_specs=[full(p0.shape)] * 2,
            out_specs=[full(one.shape)] * 2,
        ),
        out_shape=[one, one],
        name="place_mlp",
        **params(moved=6 * 2**20),
    )(me, p0, p1)


def body(
    tokens,
    state_in,
    gain_tok,
    gain_state,
    gain_mlp,
    w_tok,
    w_state,
    w_out,
    w_update,
    gate_bias,
    rel_bias,
    w_up,
    w_down,
    d_out,
    d_state_next,
):
    c = lax.axis_index("c")
    x = lax.axis_index("x")
    z = lax.axis_index("s")
    y = lax.axis_index("y")
    z1, z2 = z % 2, z // 2
    me = jnp.stack([c, x, z, y]).astype(jnp.int32)
    on_diag = c == x
    slots = state_in.shape[0]
    srows = state_in.shape[1]

    def pick(value, got):
        return jnp.where(on_diag, value, got)

    def by_block(own, other):
        return jnp.where(c == 0, jnp.concatenate([own, other]), jnp.concatenate([other, own]))

    def my_half(rows):
        return lax.dynamic_slice_in_dim(rows, c * HALF, HALF, 0)

    def other_half(rows):
        return lax.dynamic_slice_in_dim(rows, (1 - c) * HALF, HALF, 0)

    def to_slot(value, k):
        return lax.ppermute(value, "s", [(i, i ^ k) for i in range(slots)])

    def slot(value, k):
        return lax.dynamic_index_in_dim(value, z ^ k, 0, keepdims=False)

    def slot_order(parts):
        stacked = jnp.stack(parts).reshape(2, 2, srows, D)
        return untwist(stacked, (z2, z1)).reshape(slots, srows, D)

    def half_sum(part, got):
        return (part.astype(F32) + got.astype(F32)).astype(BF)

    def slot_spread(value):
        return [value[0]] + [to_slot(value[k], k) for k in range(1, slots)]

    subs = pick_columns(me, w_tok, w_state)
    small = jnp.stack([gain_tok, gain_state, gain_mlp, gate_bias])
    small = jnp.concatenate([small, jnp.pad(rel_bias, ((0, 0), (0, DH - NB)))])
    small = jnp.pad(small, ((0, 11), (0, DH)))
    ha, hb, hc = jnp.concatenate([subs[0], small]), subs[1], subs[2]
    got = [xch(hc, "z2"), xch(hb, "z2"), xch(ha, "z2"), diag_send(state_in), diag_send(tokens)]
    quarter = DH // 4
    at = (c * 2 + y) * quarter
    ho = jnp.concatenate(
        [
            lax.dynamic_slice_in_dim(w_out, at, quarter, 0),
            lax.dynamic_slice_in_dim(w_update, at, quarter, 0),
        ]
    )

    gc, gb, ga, g_states, g_tokens, ho = fence(got + [ho], got[:4])
    ha, hb, hc = jnp.stack([ha, ga]), jnp.stack([hb, gb]), jnp.stack([hc, gc])
    got = [xch(ha, "z1"), xch(hb, "x"), xch(hc, "y")]
    states = pick(state_in, g_states)
    half = [slot(states, 0), to_slot(slot(states, 2), 2)]
    g_piece = diag_send(ho)

    ga, gb, gc, half, g_piece, g_tokens = fence(
        got + [half, g_piece, g_tokens], got + [half, g_piece, g_tokens]
    )
    ha, hb, hc = jnp.stack([ha, ga]), jnp.stack([hb, gb]), jnp.stack([hc, gc])
    got = [xch(ha, "y"), xch(hb, "z1"), xch(hc, "x")]
    half = half + [to_slot(slot(states, 3), 3)]
    x_own = pick(tokens, g_tokens)
    x_oth = xch(x_own, "c")
    ho = pick(ho, g_piece)

    ga, gb, gc, half, ho, x_own, x_oth = fence(
        got + [half, ho, x_own, x_oth], got + [half, x_oth]
    )
    half = half[:1] + [to_slot(slot(states, 1), 1)] + half[1:]
    ha, hb, hc = jnp.stack([ha, ga]), jnp.stack([hb, gb]), jnp.stack([hc, gc])
    got = [xch(ha, "x"), xch(hb, "y"), xch(hc, "z1")]
    half = jnp.concatenate(half)
    state0 = by_block(half, xch(half, "c")).astype(F32)
    rows = by_block(x_own, x_oth).astype(F32)
    x_hat = norm_parts(rows)[0]
    s_hat = norm_parts(state0)[0]
    go = xch(ho, "z2")

    hid = w_up.shape[0] // 4
    hid_at = (c * 2 + y) * hid
    hu = lax.dynamic_slice_in_dim(w_up, hid_at, hid, 0)
    hd = lax.dynamic_slice_in_dim(w_down, hid_at, hid, 0)
    got, go, hu, hd, x_hat, s_hat, d_out, d_state_next = fence(
        (got, go, hu, hd, x_hat, s_hat, d_out, d_state_next), (got, x_hat, s_hat)
    )
    ho = jnp.stack([ho, go])
    go = xch(ho, "z1")
    gm = [xch(hu, "z2"), xch(hd, "z2")]
    g_states = diag_send(d_state_next)
    w_tok_l, w_state_l, small_all = lay_tables(me, (ha, got[0]), (hb, got[1]), (hc, got[2]))
    vectors = small_all[:, :4, :DH].transpose(1, 0, 2).reshape(4, D).astype(F32)
    g_tok, g_state, g_mlp = vectors[0], vectors[1], vectors[2]
    gate = jax.nn.sigmoid(vectors[3])
    xn = (x_hat * g_tok).astype(BF)
    proj = mm(xn, w_tok_l).astype(BF)

    go, gm, g_states, proj, small_all = fence(
        (go, gm, g_states, proj, small_all), (go, g_states, proj)
    )
    ho = jnp.stack([ho, go])
    go = xch(ho, "x")
    d_states = pick(d_state_next, g_states)
    sn0 = (s_hat * g_state).astype(BF)
    r0 = mm(sn0, w_state_l).astype(BF)
    rel_rows = small_all[:, 4, :NB].reshape(HL, 2, NB)
    rel_mine = lax.dynamic_index_in_dim(rel_rows, c, 1, keepdims=False)
    hot = jnp.asarray(slab_buckets())[None, :] == jnp.arange(NB, dtype=jnp.int32)[:, None]
    base = mm(rel_mine, hot.astype(BF)).reshape(HL, 8, BLK)
    bias = bias_tables(base)

    go, gm, r0, bias, d_states = fence((go, gm, r0, bias, d_states), (go, gm, r0, bias))
    ho = jnp.stack([ho, go])
    go = xch(ho, "y")
    hu, hd = jnp.stack([hu, gm[0]]), jnp.stack([hd, gm[1]])
    gm = [xch(hu, "z1"), xch(hd, "x")]
    os0, log_s0 = mem_forward(0, proj, r0)
    ot0, log_t0 = tok_forward(0, proj, r0, bias)

    go, gm, os0, ot0, d_states = fence((go, gm, os0, ot0, d_states), (go, gm, os0, ot0))
    wo, wu = lay_out_tables(me, ho, go)
    hu, hd = jnp.stack([hu, gm[0]]), jnp.stack([hd, gm[1]])
    gm = [xch(hu, "x"), xch(hd, "y")]
    d_half = [slot(d_states, 0)] + [to_slot(slot(d_states, k), k) for k in range(1, slots)]
    zp0 = mm(os0, wu)
    zz0 = zp0 + xch(zp0.astype(BF), "c").astype(F32)
    state1 = gate * state0 + (1.0 - gate) * zz0
    sn1 = (norm_parts(state1)[0] * g_state).astype(BF)
    r1 = mm(sn1, w_state_l).astype(BF)
    ot1, log_t1 = tok_forward(1, proj, r1, bias)

    gm, ot1, r1, d_out, d_half = fence((gm, ot1, r1, d_out, d_half), (gm, ot1, d_half))
    hu, hd = jnp.stack([hu, gm[0]]), jnp.stack([hd, gm[1]])
    gm = [xch(hu, "y"), xch(hd, "z1")]
    d_half = jnp.concatenate(d_half)
    ds2 = by_block(d_half, xch(d_half, "c")).astype(F32)
    d_own = pick(d_out, diag_send(d_out))
    d_oth = xch(d_own, "c")
    part0, part1 = mm(ot0, wo), mm(ot1, wo)
    part_own = jnp.where(c == 0, part0, part1)
    part_oth = jnp.where(c == 0, part1, part0).astype(BF)
    mid = x_own.astype(F32) + part_own + xch(part_oth, "c").astype(F32)
    h_own = (norm_parts(mid)[0] * g_mlp).astype(BF)
    h_oth = xch(h_own, "c")
    os1, log_s1 = mem_forward(1, proj, r1)
    zp1 = mm(os1, wu)
    zz1 = my_half(zp1) + xch(other_half(zp1).astype(BF), "c").astype(F32)
    state1_half = my_half(state1)
    state2_half = (gate * state1_half + (1.0 - gate) * zz1).astype(BF)
    dz1 = ((1.0 - gate) * ds2).astype(BF)
    dos1 = mm_nt(dz1, wu).astype(BF)
    dm1, dt1 = mem_backward(1, proj, r1, dos1, log_s1)

    gm, h_own, h_oth, d_own, d_oth, state2_half = fence(
        (gm, h_own, h_oth, d_own, d_oth, state2_half),
        (gm, h_own, h_oth, d_own, d_oth, state2_half, dm1),
    )
    out_rows = slot_spread(state2_half.reshape(slots, srows, D))
    ma, ma_out, mb, mb_out, mc, mc_out, o_own, o_oth, e_own, e_oth = mlp(
        h_own,
        h_oth,
        d_own,
        d_oth,
        hu.reshape(-1, D),
        gm[0].reshape(-1, D),
        hd.reshape(-1, D),
        gm[1].reshape(-1, D),
    )

    out_rows, ma_out, mb_out, mc_out, o_oth, e_oth = fence(
        (out_rows, ma_out, mb_out, mc_out, o_oth, e_oth), (out_rows, o_oth, e_oth)
    )
    got = [xch(ma_out, "x"), xch(mb_out, "y"), xch(mc_out, "z1")]
    state_next = slot_order(out_rows)
    e_got, o_got = xch(e_oth, "c"), xch(o_oth, "c")
    dmid, da_own, output, gain_rows = mid_back(
        mid, g_mlp[None], e_own, e_got, d_own, o_own, o_got
    )
    dot_all, grad_wo = out_back(me, da_own, xch(da_own, "c"), wo, ot0, ot1)
    dr1, dp1, dprev, rel1 = tok_backward(1, proj, r1, bias, dot_all, log_t1, dt1, dm1)

    got, dr1, dprev, output, state_next = fence(
        (got, dr1, dprev, output, state_next), (got, dr1, dprev, output)
    )
    (ma, mb, mc), sends = add_halves((ma, mb, mc), got)
    got = [xch(s, b) for s, b in zip(sends, ("y", "z1", "x"))]
    got += [diag_send(output), diag_send(state_next)]
    dsn1, dsn1_send = proj_back(me, dr1, None, w_state_l)
    dsn1_got = xch(dsn1_send, "c")
    dm0, dt0, rel0 = tok_backward(0, proj, r0, bias, dot_all, log_t0, dprev)

    got, dm0, dt0, dsn1, dsn1_got = fence((got, dm0, dt0, dsn1, dsn1_got), (got, dm0, dsn1_got))
    output = pick(output, got[3])
    state_next = pick(state_next, got[4]).astype(F32)
    (ma, mb, mc), sends = add_halves((ma, mb, mc), got[:3])
    got = [xch(s, b) for s, b in zip(sends, ("z1", "x", "y"))]
    ds1, dos0, grad_wu, gate_rows = state_back(
        me,
        state1,
        g_state[None],
        dsn1,
        dsn1_got,
        ds2,
        gate[None],
        wu,
        os0,
        os1,
        dz1,
        zz1,
        state0,
        zz0,
    )
    grad_gate = jnp.sum(gate_rows, axis=0) * gate * (1.0 - gate)
    grad_g_mlp = jnp.sum(gain_rows, axis=0)
    rel_sum = (rel0 + rel1).reshape(HL, 8 * BLK)
    grad_rel = lax.dot_general(
        rel_sum,
        hot.astype(F32),
        (((1,), (1,)), ((), ())),
        precision=lax.Precision.HIGHEST,
        preferred_element_type=F32,
    )
    both = jnp.stack([grad_rel, jnp.zeros_like(grad_rel)], axis=1)
    both = jnp.where(c == 0, both, jnp.flip(both, 1)).reshape(H, NB)
    first = jnp.concatenate([grad_g_mlp.reshape(H, DH), jnp.pad(both, ((0, 0), (0, DH - NB)))], 1)
    second = jnp.pad(grad_gate.reshape(H, DH), ((0, 0), (0, DH)))
    small_sums = jnp.stack([first, second], axis=1)[:, :, None, :].astype(BF)
    small_sums = jnp.pad(small_sums, ((0, 0), (0, 0), (0, 15), (0, 0)))
    outs = jnp.stack([grad_wo, grad_wu]).astype(BF).reshape(2, 2, 2, 2, 2, quarter, D)

    got, dos0, outs = fence((got, dos0, outs), (got, dos0, outs))
    (ma, mb, mc), sends = add_halves((ma, mb, mc), got)
    got_m = [xch(s, "z2") for s in sends]
    names = ["z2", "z1", "x", "y"]
    spots = {"z2": z2, "z1": z1, "x": x, "y": y}

    def split_outs(value, bit):
        axis = names.index(bit) + 1
        names.remove(bit)
        keep = lax.dynamic_index_in_dim(value, spots[bit], axis, keepdims=False)
        send = lax.dynamic_index_in_dim(value, 1 - spots[bit], axis, keepdims=False)
        return keep, send

    keep_o, send_o = split_outs(outs, "y")
    got_o = xch(send_o, "y")
    dr0, dp0 = mem_backward(0, proj, r0, dos0, log_s0, dm0, dt0)

    got_o, got_m, dr0, dp0, xn, sn0, sn1 = fence(
        (got_o, got_m, dr0, dp0, xn, sn0, sn1), (got_o, got_m, dr0, dp0)
    )
    mlp_part = [half_sum(h, g) for h, g in zip((ma, mb, mc), got_m)]
    mlp_part = over_groups(jnp.concatenate(mlp_part))
    got_m = xch(mlp_part, "y")
    keep_o, send_o = split_outs(half_sum(keep_o, got_o), "x")
    got_o = xch(send_o, "x")
    ha, ha_out, hb, hb_out, hc, hc_out = proj_grads(
        me, xn, sn0, sn1, dp0, dp1, dr0, dr1, small_sums
    )

    got_o, got_m, ha_out, hb_out, hc_out, dr0, dp0 = fence(
        (got_o, got_m, ha_out, hb_out, hc_out, dr0, dp0), (got_o, got_m, ha_out)
    )
    both_m = jnp.stack([mlp_part, got_m])
    got_c = xch(both_m, "c")
    got = [xch(ha_out, "x"), xch(hb_out, "y"), xch(hc_out, "z1")]
    dxn, dxn_send = proj_back(me, dp0, dp1, w_tok_l)
    dxn_got = xch(dxn_send, "c")
    dsn0, dsn0_send = proj_back(me, dr0, dr0, w_state_l)
    dsn0_got = xch(dsn0_send, "c")

    got, got_o, dxn_got, dsn0_got = fence(
        (got, got_o, dxn_got, dsn0_got), (got, got_o, dxn_got, dsn0_got)
    )
    (ha, hb, hc), sends = add_halves((ha, hb, hc), got)
    got = [xch(s, b) for s, b in zip(sends, ("y", "z1", "x"))]
    keep_o, send_o = split_outs(half_sum(keep_o, got_o), "z1")
    got_o = xch(send_o, "z1")
    one = jnp.ones((1, D), F32)
    grad_tokens = row_back(me, x_own, g_tok[None], dxn, dxn_got, one, dmid)

    got, got_o, grad_tokens, dsn0_got = fence(
        (got, got_o, grad_tokens, dsn0_got), (got, got_o, grad_tokens)
    )
    (ha, hb, hc), sends = add_halves((ha, hb, hc), got)
    got = [xch(s, b) for s, b in zip(sends, ("z1", "x", "y"))]
    keep_o, send_o = split_outs(half_sum(keep_o, got_o), "z2")
    got_o = xch(send_o, "z2")
    grad_state = row_back(me, state0, g_state[None], dsn0, dsn0_got, gate[None], ds1)
    grad_state = grad_state.reshape(slots, srows, D)

    got, got_o, grad_state, grad_tokens = fence(
        (got, got_o, grad_state, grad_tokens), (got, got_o, grad_state)
    )
    (ha, hb, hc), sends = add_halves((ha, hb, hc), got)
    got = [xch(s, "z2") for s in sends]
    got_t = diag_send(grad_tokens)
    outs = over_groups(half_sum(keep_o, got_o))
    outs = jnp.stack([outs, xch(outs, "y")])
    grad_up, grad_down = place_mlp(me, both_m, got_c)

    got, got_t, outs, grad_state, grad_up = fence(
        (got, got_t, outs, grad_state, grad_up), (got, got_t, outs, grad_up)
    )
    part = over_groups(jnp.concatenate([half_sum(h, g) for h, g in zip((ha, hb, hc), got)]))
    got_y = xch(part, "y")
    grad_rows = slot_spread(grad_state)
    outs = jnp.stack([outs, xch(outs, "x")])
    grad_tokens = pick(grad_tokens, got_t).astype(F32)

    got_y, grad_rows, outs = fence((got_y, grad_rows, outs), (got_y, grad_rows, outs))
    both_t = jnp.stack([part, got_y])
    got_p = xch(both_t, "c")
    grad_state = slot_order(grad_rows)
    grad_state = pick(grad_state, diag_send(grad_state)).astype(F32)
    outs = untwist(outs, (x, y)).transpose(2, 0, 1, 3, 4).reshape(2, DH, D)
    outs = pick(outs, xch(outs, "c")).astype(F32)
    grad_tok_w, grad_state_w, rows_tok, rows_st, small = place_proj(
        me, both_t, got_p, w_tok, w_state
    )
    grad_g_tok = rows_tok[0] / gain_tok.astype(F32)
    grad_g_state = rows_st[0] / gain_state.astype(F32)

    return (
        output,
        state_next,
        grad_tokens,
        grad_state,
        grad_g_tok,
        grad_g_state,
        small[0, 0, :DH],
        grad_tok_w,
        grad_state_w,
        outs[0],
        outs[1],
        small[1, 0, :DH],
        small[0, 0:1, DH : DH + NB],
        grad_up,
        grad_down,
    )


def solution(mesh):
    reps, shards = mesh.devices.shape
    grid = Mesh(mesh.devices.reshape(reps // 4, 2, 2, shards // 2, 2), ("h", "y", "c", "s", "x"))
    rep, shard = ("h", "y", "c"), ("s", "x")
    every = rep + shard
    by_token = P(every, None)
    by_state = P(rep, shard, None)
    line = P(shard)
    table = P(shard, None)
    params_spec = (line, line, line, table, table, table, table, line, table, table, table)
    return jax.shard_map(
        body,
        mesh=grid,
        in_specs=(by_token, by_state) + params_spec + (by_token, by_state),
        out_specs=(by_token, by_state, by_token, by_state) + params_spec,
        check_vma=False,
    )
```

```python
import functools
import math

import jax
import jax.numpy as jnp
import numpy as np
from jax import lax
from jax.experimental import pallas as pl
from jax.experimental.pallas import tpu as pltpu
from jax.sharding import Mesh
from jax.sharding import PartitionSpec as P


D = 1024
H = 8
HL = 4
DH = D // H
BLK = 512
M = 512
NB = 32
REACH = 128
HALF = 256
KEEP = HL * DH
NEG = -1e30
eps = 1e-06
SCALE = 1.0 / math.sqrt(DH)
BF = jnp.bfloat16
F32 = jnp.float32

AXIS_BITS = {"c": ("c", 1), "x": ("x", 1), "y": ("y", 1), "z1": ("s", 1), "z2": ("s", 2)}
VMEM_MLP = 44
VMEM_GRADS = 56
VMEM_MOST = 18
COST_CUT = 10


def xch(value, bit):
    axis, mask = AXIS_BITS[bit]
    count = lax.axis_size(axis)
    return lax.ppermute(value, axis, [(i, i ^ mask) for i in range(count)])


def diag_send(value):
    return lax.ppermute(value, ("c", "x"), [(1, 2), (2, 1)])


def over_groups(part):
    groups = lax.axis_size("h")
    step = 1
    while step < groups:
        got = lax.ppermute(part, "h", [(i, i ^ step) for i in range(groups)])
        part = (part.astype(F32) + got.astype(F32)).astype(part.dtype)
        step *= 2
    return part


def fence(values, done):
    leaves, tree = jax.tree.flatten(values)
    tied = lax.optimization_barrier(tuple(leaves) + tuple(jax.tree.leaves(done)))
    return jax.tree.unflatten(tree, tied[: len(leaves)])


def untwist(value, bits):
    for axis, bit in enumerate(bits):
        value = jnp.where(bit == 1, jnp.flip(value, axis), value)
    return value


def mm(a, b):
    return jnp.dot(a, b, preferred_element_type=F32)


def mm_nt(a, b):
    return lax.dot_general(a, b, (((1,), (1,)), ((), ())), preferred_element_type=F32)


def mm_tn(a, b):
    return lax.dot_general(a, b, (((0,), (0,)), ((), ())), preferred_element_type=F32)


def norm_parts(values):
    centered = values - jnp.mean(values, axis=-1, keepdims=True)
    variance = jnp.mean(centered * centered, axis=-1, keepdims=True)
    rstd = lax.rsqrt(variance + eps)
    return centered * rstd, rstd


def norm_back(values, gain, grad):
    hat, rstd = norm_parts(values)
    g = grad * gain
    inner = g - jnp.mean(g, axis=-1, keepdims=True)
    inner = inner - hat * jnp.mean(g * hat, axis=-1, keepdims=True)
    return inner * rstd, grad * hat


def bucket_table(block_len, bucket_count, reach_len):
    distance = np.arange(2 * block_len + 1)
    exact = bucket_count // 2
    ratio = np.log(np.maximum(distance, 1) / exact) / np.log(reach_len / exact)
    far = np.minimum(
        exact + np.floor(ratio * (bucket_count - exact)).astype(np.int64), bucket_count - 1
    )
    return np.where(distance < exact, distance, far).astype(np.int32)


def slab_buckets():
    s = np.arange(8)[:, None]
    col = np.arange(BLK)[None, :]
    return bucket_table(BLK, NB, REACH)[(s - col) % BLK].reshape(-1)


def params(flops=0, moved=0, trans=0, grid=1, vmem=VMEM_MOST):
    return dict(
        compiler_params=pltpu.CompilerParams(
            vmem_limit_bytes=vmem * 2**20, dimension_semantics=("arbitrary",) * grid
        ),
        cost_estimate=pl.CostEstimate(
            flops=flops // COST_CUT, bytes_accessed=moved // COST_CUT, transcendentals=0
        ),
    )


def full(shape, memory_space=None):
    return pl.BlockSpec(
        shape, lambda *_: (0,) * len(shape), pipeline_mode=pl.Buffered(buffer_count=1)
    )


def pick_kernel(me, tok, st, *outs):
    c, y = me[0], me[3]
    for sub in range(3):
        for i in range(2):
            j = 6 * y + 2 * sub + i
            col = (j // HL) * D + (2 * (j % HL) + c) * DH
            src = pl.ds(pl.multiple_of(col, DH), DH)
            dst = slice(i * DH, (i + 1) * DH)
            outs[sub][0:DH, dst] = tok[:, src]
            outs[sub][DH : 2 * DH, dst] = st[:, src]


def pick_columns(me, w_tok, w_state):
    one = jax.ShapeDtypeStruct((2 * DH, 2 * DH), BF)
    return pl.pallas_call(
        pick_kernel,
        grid_spec=pltpu.PrefetchScalarGridSpec(
            num_scalar_prefetch=1,
            grid=(1,),
            in_specs=[full(w_tok.shape), full(w_state.shape)],
            out_specs=[full((2 * DH, 2 * DH))] * 3,
        ),
        out_shape=[one] * 3,
        name="pick",
        **params(moved=3 * 2**20),
    )(me, w_tok, w_state)


def lay_kernel(me, a0, a1, b0, b1, c0, c1, tok, st, small):
    q = pl.program_id(0)
    x0, y0 = me[1], me[3]
    low = lax.rem(q, 2) == 0
    c_val = jnp.where(low, c0[...], c1[...])
    for xr in range(2):
        for yr in range(2):
            va = (a0, a1)[xr][yr, 0, 0]
            vb = (b0, b1)[yr][0, xr, 0]
            vc = c_val[xr, yr, 0]
            rows = pl.ds(pl.multiple_of((x0 ^ xr) * DH, DH), DH)
            for sub, v in enumerate((va, vb, vc)):
                cols = pl.ds(pl.multiple_of((y0 ^ yr) * 768 + sub * 256, 256), 256)
                tok[rows, cols] = v[0:DH]
                st[rows, cols] = v[DH : 2 * DH]
        small[x0 ^ xr] = (a0, a1)[xr][0, 0, 0, 2 * DH : 2 * DH + 16]


def lay_tables(me, a, b, c):
    ra = a[0].shape[-2]
    a_spec = pl.BlockSpec((2, 1, 1, ra, 256), lambda q, me: (0, q % 2, q // 2, 0, 0))
    b_spec = pl.BlockSpec((1, 2, 1, 256, 256), lambda q, me: (q % 2, 0, q // 2, 0, 0))
    c_spec = pl.BlockSpec((2, 2, 1, 256, 256), lambda q, me: (0, 0, q // 2, 0, 0))
    w_spec = pl.BlockSpec((2 * DH, 3 * KEEP), lambda q, me: (q ^ me[2], 0))
    return pl.pallas_call(
        lay_kernel,
        grid_spec=pltpu.PrefetchScalarGridSpec(
            num_scalar_prefetch=1,
            grid=(4,),
            in_specs=[a_spec, a_spec, b_spec, b_spec, c_spec, c_spec],
            out_specs=[
                w_spec,
                w_spec,
                pl.BlockSpec((2, 16, 256), lambda q, me: (q ^ me[2], 0, 0)),
            ],
        ),
        out_shape=[
            jax.ShapeDtypeStruct((D, 3 * KEEP), BF),
            jax.ShapeDtypeStruct((D, 3 * KEEP), BF),
            jax.ShapeDtypeStruct((8, 16, 256), BF),
        ],
        name="lay",
        **params(moved=14 * 2**20),
    )(me, *a, *b, *c)


def lay_out_kernel(last, me, low, high, out):
    x0, z0, y0 = me[1], me[2], me[3]
    q = low.shape[3]
    for yr in range(2):
        for xr in range(2):
            for zr in range(4):
                row = (z0 ^ zr) * DH + ((x0 ^ xr) * 2 + (y0 ^ yr)) * q
                if last == "y":
                    v = (low, high)[yr][zr % 2, xr, zr // 2]
                else:
                    v = (low, high)[zr % 2][yr, xr, zr // 2]
                out[pl.ds(pl.multiple_of(row, q), q), :] = v


def lay_out_table(last, me, low, high):
    return pl.pallas_call(
        functools.partial(lay_out_kernel, last),
        grid_spec=pltpu.PrefetchScalarGridSpec(
            num_scalar_prefetch=1,
            grid=(1,),
            in_specs=[full(low.shape), full(high.shape)],
            out_specs=full((KEEP, D)),
        ),
        out_shape=jax.ShapeDtypeStruct((KEEP, D), BF),
        name="lay_out",
        **params(moved=2 * 2**20),
    )(me, low, high)


def bias_kernel(base, out):
    slab = base[0]
    for a in range(0, 64, 2):
        two = jnp.concatenate(
            [pltpu.roll(slab, 8 * a, 1), pltpu.roll(slab, 8 * a + 8, 1)], axis=0
        )
        out[0, 8 * a : 8 * a + 16, :] = two.astype(BF)


def bias_tables(base):
    return pl.pallas_call(
        bias_kernel,
        grid=(HL,),
        in_specs=[pl.BlockSpec((1, 8, BLK), lambda h: (h, 0, 0))],
        out_specs=pl.BlockSpec((1, BLK, BLK), lambda h: (h, 0, 0)),
        out_shape=jax.ShapeDtypeStruct((HL, BLK, BLK), BF),
        name="bias",
        **params(moved=2 * 2**20),
    )(base)


def lower_mask():
    rows = lax.broadcasted_iota(jnp.int32, (HALF, HALF), 0)
    cols = lax.broadcasted_iota(jnp.int32, (HALF, HALF), 1)
    return rows >= cols


def head_lane(h):
    return lax.broadcasted_iota(jnp.int32, (HALF, DH), 1) == h


def window_scores(t, has_prev, qt, ko, kp, bias, rows, lower):
    near = bias[0, rows, rows].astype(F32)
    near_own = mm_nt(qt, ko[rows, :]) * SCALE
    if has_prev:
        near_prev = mm_nt(qt, kp[rows, :]) * SCALE
        s_near = jnp.where(lower, near_own, near_prev) + near
    else:
        s_near = jnp.where(lower, near_own + near, NEG)
    s_far = None
    if t == 1:
        s_far = mm_nt(qt, ko[0:HALF, :]) * SCALE + bias[0, rows, 0:HALF].astype(F32)
    elif has_prev:
        s_far = mm_nt(qt, kp[HALF:BLK, :]) * SCALE + bias[0, rows, HALF:BLK].astype(F32)
    s_edge = None
    if has_prev:
        pair = qt.astype(F32) * kp[rows, :].astype(F32)
        s_edge = jnp.sum(pair, axis=1, keepdims=True) * SCALE + bias[0, 0:1, 1:2].astype(F32)
    return s_near, s_far, s_edge


def tok_fwd_kernel(has_prev, *refs):
    if has_prev:
        q, km, vm, ko, vo, bias, kp, vp, out, logs = refs
    else:
        q, km, vm, ko, vo, bias, out, logs = refs
        kp = vp = None
    h = pl.program_id(0)
    lower = lower_mask()
    for t in range(2):
        rows = slice(t * HALF, (t + 1) * HALF)
        qt = q[rows, :]
        s_mem = mm_nt(qt, km[...]) * SCALE
        s_near, s_far, s_edge = window_scores(t, has_prev, qt, ko, kp, bias, rows, lower)
        top = jnp.maximum(
            jnp.max(s_mem, axis=1, keepdims=True), jnp.max(s_near, axis=1, keepdims=True)
        )
        if s_far is not None:
            top = jnp.maximum(top, jnp.max(s_far, axis=1, keepdims=True))
        if has_prev:
            top = jnp.maximum(top, s_edge)
        e_mem = jnp.exp(s_mem - top)
        e_near = jnp.exp(s_near - top)
        total = jnp.sum(e_mem, axis=1, keepdims=True) + jnp.sum(e_near, axis=1, keepdims=True)
        acc = mm(e_mem.astype(BF), vm[...])
        if has_prev:
            acc += mm(jnp.where(lower, e_near, 0.0).astype(BF), vo[rows, :])
            acc += mm(jnp.where(lower, 0.0, e_near).astype(BF), vp[rows, :])
            e_edge = jnp.exp(s_edge - top)
            total += e_edge
            acc += e_edge * vp[rows, :].astype(F32)
        else:
            acc += mm(e_near.astype(BF), vo[rows, :])
        if s_far is not None:
            e_far = jnp.exp(s_far - top)
            total += jnp.sum(e_far, axis=1, keepdims=True)
            v_far = vo[0:HALF, :] if t == 1 else vp[HALF:BLK, :]
            acc += mm(e_far.astype(BF), v_far)
        out[rows, :] = (acc / total).astype(BF)
        keep = jnp.where(h == 0, 0.0, logs[rows, :])
        logs[rows, :] = jnp.where(head_lane(h), top + jnp.log(total), keep)


def col(block, at):
    return pl.BlockSpec((BLK, DH), lambda h: (block, at * HL + h))


def tok_forward(block, proj, mem_proj, bias):
    has_prev = block > 0
    specs = [col(block, 0), col(0, 1), col(0, 2), col(block, 1), col(block, 2)]
    specs += [pl.BlockSpec((1, BLK, BLK), lambda h: (h, 0, 0))]
    ops = [proj, mem_proj, mem_proj, proj, proj, bias]
    if has_prev:
        specs += [col(block - 1, 1), col(block - 1, 2)]
        ops += [proj, proj]
    return pl.pallas_call(
        functools.partial(tok_fwd_kernel, has_prev),
        grid=(HL,),
        in_specs=specs,
        out_specs=[col(0, 0), full((BLK, DH))],
        out_shape=[
            jax.ShapeDtypeStruct((BLK, KEEP), BF),
            jax.ShapeDtypeStruct((BLK, DH), F32),
        ],
        name="tok_fwd",
        **params(flops=4 * BLK * 1280 * KEEP, moved=8 * 2**20, trans=HL * BLK * 1024),
    )(*ops)


def mem_fwd_kernel(q, ks, vs, ko, vo, out, logs):
    h = pl.program_id(0)
    for t in range(2):
        rows = slice(t * HALF, (t + 1) * HALF)
        qt = q[rows, :]
        s1 = mm_nt(qt, ks[...]) * SCALE
        s2 = mm_nt(qt, ko[...]) * SCALE
        top = jnp.maximum(jnp.max(s1, axis=1, keepdims=True), jnp.max(s2, axis=1, keepdims=True))
        e1 = jnp.exp(s1 - top)
        e2 = jnp.exp(s2 - top)
        total = jnp.sum(e1, axis=1, keepdims=True) + jnp.sum(e2, axis=1, keepdims=True)
        acc = mm(e1.astype(BF), vs[...]) + mm(e2.astype(BF), vo[...])
        out[rows, :] = (acc / total).astype(BF)
        keep = jnp.where(h == 0, 0.0, logs[rows, :])
        logs[rows, :] = jnp.where(head_lane(h), top + jnp.log(total), keep)


def mem_forward(block, proj, mem_proj):
    return pl.pallas_call(
        mem_fwd_kernel,
        grid=(HL,),
        in_specs=[col(0, 0), col(0, 1), col(0, 2), col(block, 1), col(block, 2)],
        out_specs=[col(0, 0), full((BLK, DH))],
        out_shape=[
            jax.ShapeDtypeStruct((BLK, KEEP), BF),
            jax.ShapeDtypeStruct((BLK, DH), F32),
        ],
        name="mem_fwd",
        **params(flops=4 * BLK * 1024 * KEEP, moved=4 * 2**20, trans=HL * BLK * 1024),
    )(mem_proj, mem_proj, mem_proj, proj, proj)


def head_cols(at, h):
    return pl.ds(pl.multiple_of((at * HL + h) * DH, DH), DH)


def mem_bwd_kernel(final, *refs):
    if final:
        q, ks, vs, ko, vo, do, logs, aks, avs, aq, ak, av, d_mem, d_tok, dks, dvs, dko, dvo = refs
    else:
        q, ks, vs, ko, vo, do, logs, d_mem, d_tok, dks, dvs, dko, dvo = refs
    h = pl.program_id(0)
    kind = BF if final else F32
    for t in range(2):
        rows = slice(t * HALF, (t + 1) * HALF)
        qt = q[rows, :]
        dt = do[rows, :]
        log_t = jnp.sum(jnp.where(head_lane(h), logs[rows, :], 0.0), axis=1, keepdims=True)
        p1 = jnp.exp(mm_nt(qt, ks[...]) * SCALE - log_t)
        p2 = jnp.exp(mm_nt(qt, ko[...]) * SCALE - log_t)
        w1 = mm_nt(dt, vs[...])
        w2 = mm_nt(dt, vo[...])
        inner = jnp.sum(p1 * w1, axis=1, keepdims=True) + jnp.sum(p2 * w2, axis=1, keepdims=True)
        g1 = (p1 * (w1 - inner)).astype(BF)
        g2 = (p2 * (w2 - inner)).astype(BF)
        dq = (mm(g1, ks[...]) + mm(g2, ko[...])) * SCALE
        d_mem[rows, head_cols(0, h)] = dq.astype(kind)
        terms = (
            (dks, mm_tn(g1, qt) * SCALE),
            (dko, mm_tn(g2, qt) * SCALE),
            (dvs, mm_tn(p1.astype(BF), dt)),
            (dvo, mm_tn(p2.astype(BF), dt)),
        )
        for ref, term in terms:
            if t == 0:
                ref[...] = term
            else:
                ref[...] += term
    if final:
        d_mem[:, head_cols(1, h)] = (dks[...] + aks[...]).astype(BF)
        d_mem[:, head_cols(2, h)] = (dvs[...] + avs[...]).astype(BF)
        d_tok[:, head_cols(0, h)] = aq[...].astype(BF)
        d_tok[:, head_cols(1, h)] = (dko[...] + ak[...]).astype(BF)
        d_tok[:, head_cols(2, h)] = (dvo[...] + av[...]).astype(BF)
    else:
        d_mem[:, head_cols(1, h)] = dks[...]
        d_mem[:, head_cols(2, h)] = dvs[...]
        d_tok[:, head_cols(0, h)] = dko[...]
        d_tok[:, head_cols(1, h)] = dvo[...]


def mem_backward(block, proj, mem_proj, grad_mix, logs, add_mem=None, add_tok=None):
    final = add_mem is not None
    specs = [col(0, 0), col(0, 1), col(0, 2), col(block, 1), col(block, 2), col(0, 0)]
    specs += [full((BLK, DH))]
    ops = [mem_proj, mem_proj, mem_proj, proj, proj, grad_mix, logs]
    if final:
        specs += [col(0, 0), col(0, 1), col(0, 0), col(0, 1), col(0, 2)]
        ops += [add_mem, add_mem, add_tok, add_tok, add_tok]
    kind = BF if final else F32
    wide = 3 * KEEP if final else 2 * KEEP
    return pl.pallas_call(
        functools.partial(mem_bwd_kernel, final),
        grid=(HL,),
        in_specs=specs,
        out_specs=[full((BLK, 3 * KEEP)), full((BLK, wide))],
        out_shape=[
            jax.ShapeDtypeStruct((BLK, 3 * KEEP), kind),
            jax.ShapeDtypeStruct((BLK, wide), kind),
        ],
        scratch_shapes=[pltpu.VMEM((BLK, DH), F32)] * 4,
        name="mem_bwd",
        **params(flops=10 * BLK * 1024 * KEEP, moved=9 * 2**20, trans=HL * BLK * 1024),
    )(*ops)


def tok_bwd_kernel(has_prev, *refs):
    if has_prev:
        q, km, vm, ko, vo, bias, do, logs, kp, vp, sq, sk, sv, ak, av = refs[:15]
        d_mem, d_tok, d_prev, rel, dkm, dvm, dko, dvo, dkp, dvp = refs[15:]
    else:
        q, km, vm, ko, vo, bias, do, logs, ak, av = refs[:10]
        d_mem, d_tok, rel, dkm, dvm, dko, dvo = refs[10:]
        kp = vp = None
    h = pl.program_id(0)
    lower = lower_mask()
    slab = jnp.zeros((8, BLK), F32)
    dko[...] = jnp.zeros_like(dko)
    dvo[...] = jnp.zeros_like(dvo)
    if has_prev:
        dkp[...] = jnp.zeros_like(dkp)
        dvp[...] = jnp.zeros_like(dvp)
    for t in range(2):
        rows = slice(t * HALF, (t + 1) * HALF)
        qt = q[rows, :]
        dt = do[rows, :]
        log_t = jnp.sum(jnp.where(head_lane(h), logs[rows, :], 0.0), axis=1, keepdims=True)
        p_mem = jnp.exp(mm_nt(qt, km[...]) * SCALE - log_t)
        s_near, s_far, s_edge = window_scores(t, has_prev, qt, ko, kp, bias, rows, lower)
        p_near = jnp.exp(s_near - log_t)
        w_mem = mm_nt(dt, vm[...])
        w_near = mm_nt(dt, vo[rows, :])
        inner = jnp.sum(p_mem * w_mem, axis=1, keepdims=True)
        if has_prev:
            w_near = jnp.where(lower, w_near, mm_nt(dt, vp[rows, :]))
            p_edge = jnp.exp(s_edge - log_t)
            v_edge = vp[rows, :].astype(F32)
            k_edge = kp[rows, :].astype(F32)
            w_edge = jnp.sum(dt.astype(F32) * v_edge, axis=1, keepdims=True)
            inner += p_edge * w_edge
        inner += jnp.sum(p_near * w_near, axis=1, keepdims=True)
        if s_far is not None:
            far = slice(0, HALF) if t == 1 else slice(HALF, BLK)
            k_far, v_far = (ko, vo) if t == 1 else (kp, vp)
            p_far = jnp.exp(s_far - log_t)
            w_far = mm_nt(dt, v_far[far, :])
            inner += jnp.sum(p_far * w_far, axis=1, keepdims=True)
        g_mem = (p_mem * (w_mem - inner)).astype(BF)
        g_near32 = p_near * (w_near - inner)
        g_near = g_near32.astype(BF)
        dq = mm(g_mem, km[...])
        zero = jnp.zeros((), BF)
        if has_prev:
            g_own = jnp.where(lower, g_near32, 0.0).astype(BF)
            g_prev = jnp.where(lower, 0.0, g_near32).astype(BF)
            p_own = jnp.where(lower, p_near, 0.0).astype(BF)
            p_prev = jnp.where(lower, 0.0, p_near).astype(BF)
            g_edge = (p_edge * (w_edge - inner)).astype(BF).astype(F32)
            p_edge16 = p_edge.astype(BF).astype(F32)
            dq += mm(g_prev, kp[rows, :]) + g_edge * k_edge
            dkp[rows, :] += mm_tn(g_prev, qt) + g_edge * qt.astype(F32)
            dvp[rows, :] += mm_tn(p_prev, dt) + p_edge16 * dt.astype(F32)
        else:
            g_own = g_near
            p_own = p_near.astype(BF)
        dq += mm(g_own, ko[rows, :])
        dko[rows, :] += mm_tn(g_own, qt)
        dvo[rows, :] += mm_tn(p_own, dt)
        g_far32 = jnp.zeros((HALF, HALF), F32)
        if s_far is not None:
            g_far = (p_far * (w_far - inner)).astype(BF)
            g_far32 = g_far.astype(F32)
            dq += mm(g_far, k_far[far, :])
            dk_far, dv_far = (dko, dvo) if t == 1 else (dkp, dvp)
            dk_far[far, :] += mm_tn(g_far, qt)
            dv_far[far, :] += mm_tn(p_far.astype(BF), dt)
        d_tok[rows, head_cols(0, h)] = (dq * SCALE).astype(d_tok.dtype)
        g_round = g_near.astype(F32)
        wide = [g_round, g_far32] if t == 0 else [g_far32, g_round]
        wide = jnp.concatenate(wide, axis=1)
        for a in range(HALF // 8):
            shift = (BLK - 8 * a - t * HALF) % BLK
            part = wide[8 * a : 8 * a + 8, :]
            slab = slab + (pltpu.roll(part, shift, 1) if shift else part)
        if has_prev:
            at = lax.broadcasted_iota(jnp.int32, (8, BLK), 0) * BLK
            at = at + lax.broadcasted_iota(jnp.int32, (8, BLK), 1)
            edge_sum = jnp.sum(g_edge, axis=0, keepdims=True)
            slab = slab + jnp.where(at == 1, edge_sum, 0.0)
        add_k = mm_tn(g_mem, qt)
        add_v = mm_tn(p_mem.astype(BF), dt)
        if t == 0:
            dkm[...] = add_k
            dvm[...] = add_v
        else:
            dkm[...] += add_k
            dvm[...] += add_v
    rel[0] = slab
    k_tok = dko[...] * SCALE + ak[...]
    v_tok = dvo[...] + av[...]
    d_tok[:, head_cols(1, h)] = k_tok.astype(d_tok.dtype)
    d_tok[:, head_cols(2, h)] = v_tok.astype(d_tok.dtype)
    if has_prev:
        d_mem[:, head_cols(0, h)] = sq[...].astype(BF)
        d_mem[:, head_cols(1, h)] = (dkm[...] * SCALE + sk[...]).astype(BF)
        d_mem[:, head_cols(2, h)] = (dvm[...] + sv[...]).astype(BF)
        d_prev[:, head_cols(0, h)] = dkp[...] * SCALE
        d_prev[:, head_cols(1, h)] = dvp[...]
    else:
        d_mem[:, head_cols(0, h)] = dkm[...] * SCALE
        d_mem[:, head_cols(1, h)] = dvm[...]


def tok_backward(block, proj, mem_proj, bias, grad_mix, logs, add_tok, add_mem=None):
    has_prev = block > 0
    specs = [col(block, 0), col(0, 1), col(0, 2), col(block, 1), col(block, 2)]
    specs += [pl.BlockSpec((1, BLK, BLK), lambda h: (h, 0, 0)), col(block, 0), full((BLK, DH))]
    ops = [proj, mem_proj, mem_proj, proj, proj, bias, grad_mix, logs]
    scratch = 4
    if has_prev:
        specs += [col(block - 1, 1), col(block - 1, 2), col(0, 0), col(0, 1), col(0, 2)]
        ops += [proj, proj, add_mem, add_mem, add_mem]
        scratch = 6
    specs += [col(0, 0), col(0, 1)]
    ops += [add_tok, add_tok]
    kind = BF if has_prev else F32
    rel_spec = pl.BlockSpec((1, 8, BLK), lambda h: (h, 0, 0))
    rel_shape = jax.ShapeDtypeStruct((HL, 8, BLK), F32)
    wide = 3 * KEEP if has_prev else 2 * KEEP
    out_specs = [full((BLK, wide)), full((BLK, 3 * KEEP))]
    out_shape = [
        jax.ShapeDtypeStruct((BLK, wide), kind),
        jax.ShapeDtypeStruct((BLK, 3 * KEEP), kind),
    ]
    if has_prev:
        out_specs.append(full((BLK, 2 * KEEP)))
        out_shape.append(jax.ShapeDtypeStruct((BLK, 2 * KEEP), F32))
    return pl.pallas_call(
        functools.partial(tok_bwd_kernel, has_prev),
        grid=(HL,),
        in_specs=specs,
        out_specs=out_specs + [rel_spec],
        out_shape=out_shape + [rel_shape],
        scratch_shapes=[pltpu.VMEM((BLK, DH), F32)] * scratch,
        name="tok_bwd",
        **params(flops=10 * BLK * 1280 * KEEP, moved=12 * 2**20, trans=HL * BLK * 1024),
    )(*ops)


def normal_parts(u):
    bell = jnp.exp(-0.5 * (u * u))
    t = 1.0 / (1.0 + (0.3275911 * math.sqrt(0.5)) * jnp.abs(u))
    poly = 1.061405429 * t - 1.453152027
    poly = poly * t + 1.421413741
    poly = poly * t - 0.284496736
    poly = poly * t + 0.254829592
    tail = (0.5 * poly) * (t * bell)
    return jnp.where(u >= 0, 1.0 - tail, tail), bell * (1.0 / math.sqrt(2.0 * math.pi))


MAIN = 96
REST = DH - MAIN
TILE = 4 * DH


def mlp_kernel(h0, h1, d0, d1, u0, u1, w0, w1, r0, r1, *refs):
    a_keep, a_send, b_keep, b_send, c_keep, c_send, o0, o1, e0, e1 = refs[:10]
    accs = refs[10:]
    t = pl.program_id(0)
    in_x, in_y = t // 2, lax.rem(t, 2)

    @pl.when(t == 0)
    def _():
        for ref in accs:
            ref[...] = jnp.zeros_like(ref)

    rest = jnp.where(in_x == 0, r0[...], r1[...]).reshape(4, 2 * REST, D)
    wu = jnp.where(in_y == 0, u0[...], u1[...]).reshape(4 * MAIN, D)
    wu = jnp.concatenate([wu, rest[:, 0:REST].reshape(4 * REST, D)], axis=0)
    wd = [w0[...].reshape(2 * MAIN, D), w1[...].reshape(2 * MAIN, D)]
    wd = jnp.concatenate(wd + [rest[:, REST:].reshape(4 * REST, D)], axis=0)
    kept = []
    for r in range(2):
        h = (h0, h1)[r]
        d = (d0, d1)[r]
        u = mm_nt(h[...], wu)
        dg = mm_nt(d[...], wd)
        phi, pdf = normal_parts(u)
        g = (u * phi).astype(BF)
        du = (dg * (phi + u * pdf)).astype(BF)
        accs[r][...] += mm(g, wd)
        accs[2 + r][...] += mm(du, wu)
        kept.append((g, du))
    gd = (mm_tn(kept[0][0], d0[...]) + mm_tn(kept[1][0], d1[...])).astype(BF)
    gu = (mm_tn(kept[0][1], h0[...]) + mm_tn(kept[1][1], h1[...])).astype(BF)
    gd_rest, gu_rest = (v[4 * MAIN :].reshape(4, REST, D) for v in (gd, gu))
    gd, gu = (v[0 : 4 * MAIN].reshape(4, MAIN, D) for v in (gd, gu))
    for z1 in range(2):
        side = (c_keep, c_send)[z1]
        for z2 in range(2):
            side[0, 0, z2, 0:REST, :] = gu_rest[2 * z1 + z2]
            side[0, 0, z2, REST:, :] = gd_rest[2 * z1 + z2]
    for bit in range(2):

        @pl.when(in_x == bit)
        def _():
            for z in range(4):
                (a_keep, a_send)[bit][0, z // 2, z % 2] = gu[z]

        @pl.when(in_y == bit)
        def _():
            for z in range(4):
                (b_keep, b_send)[bit][z // 2, 0, z % 2] = gd[z]

    @pl.when(t == pl.num_programs(0) - 1)
    def _():
        for ref, acc in zip((o0, o1, e0, e1), accs):
            ref[...] = acc[...].astype(BF)


def mlp(h0, h1, d0, d1, u0, u1, w0, w1, r0, r1):
    act = full((BLK, D))
    up = pl.BlockSpec((1, 2, 2, MAIN, D), lambda t: (t // 2, 0, 0, 0, 0))
    down = pl.BlockSpec((1, 1, 2, MAIN, D), lambda t: (t % 2, t // 2, 0, 0, 0))
    rest_block = (2, 1, 2, 2 * REST, D)
    rest0 = pl.BlockSpec(rest_block, lambda t: (0, jnp.minimum(t, 1), 0, 0, 0))
    rest1 = pl.BlockSpec(rest_block, lambda t: (0, jnp.maximum(t - 2, 0), 0, 0, 0))
    tail = (MAIN, D)
    a_keep = pl.BlockSpec((1, 2, 2) + tail, lambda t: (jnp.minimum(t, 1), 0, 0, 0, 0))
    a_send = pl.BlockSpec((1, 2, 2) + tail, lambda t: (jnp.maximum(t - 2, 0), 0, 0, 0, 0))
    b_keep = pl.BlockSpec((2, 1, 2) + tail, lambda t: (0, t // 2, 0, 0, 0))
    b_send = pl.BlockSpec((2, 1, 2) + tail, lambda t: (0, t // 3, 0, 0, 0))
    c_spec = pl.BlockSpec((1, 1, 2, 2 * REST, D), lambda t: (t // 2, t % 2, 0, 0, 0))
    big_shape = jax.ShapeDtypeStruct((2, 2, 2, MAIN, D), BF)
    rest_shape = jax.ShapeDtypeStruct((2, 2, 2, 2 * REST, D), BF)
    return pl.pallas_call(
        mlp_kernel,
        grid=(4,),
        in_specs=[act] * 4 + [up, up, down, down, rest0, rest1],
        out_specs=[a_keep, a_send, b_keep, b_send, c_spec, c_spec] + [act] * 4,
        scratch_shapes=[pltpu.VMEM((BLK, D), F32)] * 4,
        out_shape=[big_shape] * 4
        + [rest_shape] * 2
        + [jax.ShapeDtypeStruct((BLK, D), BF)] * 4,
        name="mlp",
        **params(flops=12 * D * D * 2 * D, moved=26 * 2**20, vmem=VMEM_MLP),
    )(h0, h1, d0, d1, u0, u1, w0, w1, r0, r1)


def halves_kernel(*refs):
    count = len(refs) // 4
    for keep, got, out_keep, out_send in zip(
        refs[:count], refs[count : 2 * count], refs[2 * count :: 2], refs[2 * count + 1 :: 2]
    ):
        out_keep[...] = (keep[0].astype(F32) + got[0].astype(F32)).astype(BF)
        out_send[...] = (keep[1].astype(F32) + got[1].astype(F32)).astype(BF)


def add_halves(keeps, gots):
    shapes = [k.shape for k in keeps]
    flat = [k.reshape(2, -1, k.shape[-1]) for k in keeps]
    flat_got = [g.reshape(2, -1, g.shape[-1]) for g in gots]
    steps = 4
    while any((k.shape[1] // steps) % 16 or k.shape[1] % steps for k in flat):
        steps //= 2
    ins, outs, out_shapes = [], [], []
    for k in flat:
        rows, width = k.shape[1] // steps, k.shape[2]
        ins.append(pl.BlockSpec((2, rows, width), lambda t: (0, t, 0)))
        outs += [pl.BlockSpec((rows, width), lambda t: (t, 0))] * 2
        out_shapes += [jax.ShapeDtypeStruct(k.shape[1:], BF)] * 2
    done = pl.pallas_call(
        halves_kernel,
        grid=(steps,),
        in_specs=ins * 2,
        out_specs=outs,
        out_shape=out_shapes,
        name="halves",
        **params(),
    )(*flat, *flat_got)
    done = [d.reshape(sh[1:]) for d, sh in zip(done, [s for s in shapes for _ in range(2)])]
    return done[0::2], done[1::2]


def eight_rows(values):
    return jnp.sum(values.reshape(-1, 8, values.shape[-1]), axis=0)


def mid_back_kernel(mid, gain, e_own, e_got, d_own, o_own, o_got, dmid, da, out, gsum):
    rows = mid[...]
    back, gain_rows = norm_back(
        rows, gain[...], e_own[...].astype(F32) + e_got[...].astype(F32)
    )
    total = d_own[...].astype(F32) + back
    dmid[...] = total
    da[...] = total.astype(BF)
    out[...] = (rows + o_own[...].astype(F32) + o_got[...].astype(F32)).astype(BF)

    @pl.when(pl.program_id(0) == 0)
    def _():
        gsum[...] = jnp.zeros_like(gsum)

    gsum[...] += eight_rows(gain_rows)


def mid_back(mid, gain, e_own, e_got, d_own, o_own, o_got):
    row = pl.BlockSpec((DH, D), lambda t: (t, 0))
    return pl.pallas_call(
        mid_back_kernel,
        grid=(BLK // DH,),
        in_specs=[row, full((1, D))] + [row] * 5,
        out_specs=[row, row, row, full((8, D))],
        out_shape=[
            jax.ShapeDtypeStruct((BLK, D), F32),
            jax.ShapeDtypeStruct((BLK, D), BF),
            jax.ShapeDtypeStruct((BLK, D), BF),
            jax.ShapeDtypeStruct((8, D), F32),
        ],
        name="mid_back",
        **params(vmem=VMEM_GRADS),
    )(mid, gain, e_own, e_got, d_own, o_own, o_got)


def out_back_kernel(me, own, oth, wo, ot0, ot1, dot_all, grad):
    first = me[0] == 0
    da0 = jnp.where(first, own[...], oth[...])
    da1 = jnp.where(first, oth[...], own[...])
    dot_all[0:BLK, :] = mm_nt(da0, wo[...]).astype(BF)
    dot_all[BLK:, :] = mm_nt(da1, wo[...]).astype(BF)
    grad[...] = (mm_tn(ot0[...], da0) + mm_tn(ot1[...], da1)).astype(BF)


def out_back(me, own, oth, wo, ot0, ot1):
    return pl.pallas_call(
        out_back_kernel,
        grid_spec=pltpu.PrefetchScalarGridSpec(
            num_scalar_prefetch=1,
            grid=(1,),
            in_specs=[full((BLK, D))] * 2 + [full((KEEP, D))] + [full((BLK, KEEP))] * 2,
            out_specs=[full((2 * BLK, KEEP)), full((KEEP, D))],
        ),
        out_shape=[
            jax.ShapeDtypeStruct((2 * BLK, KEEP), BF),
            jax.ShapeDtypeStruct((KEEP, D), BF),
        ],
        name="out_back",
        **params(vmem=VMEM_GRADS),
    )(me, own, oth, wo, ot0, ot1)


def proj_back_kernel(me, a, b, w, own, oth):
    first = me[0] == 0
    own[...] = mm_nt(jnp.where(first, a[...], b[...]), w[...]).astype(BF)
    oth[...] = mm_nt(jnp.where(first, b[...], a[...]), w[...]).astype(BF)


def proj_one_kernel(a, w, own):
    own[...] = mm_nt(a[...], w[...]).astype(BF)


def proj_one(a, w):
    rows = a.shape[0]
    return pl.pallas_call(
        proj_one_kernel,
        grid=(4,),
        in_specs=[full(a.shape), pl.BlockSpec((D // 4, 3 * KEEP), lambda t: (t, 0))],
        out_specs=pl.BlockSpec((rows, D // 4), lambda t: (0, t)),
        out_shape=jax.ShapeDtypeStruct((rows, D), BF),
        name="proj_one",
        **params(),
    )(a, w)


def proj_back(me, a, b, w):
    rows = a.shape[0] // 2 if b is a else a.shape[0]
    side = 1 if b is a else 0
    return pl.pallas_call(
        proj_back_kernel,
        grid_spec=pltpu.PrefetchScalarGridSpec(
            num_scalar_prefetch=1,
            grid=(4,),
            in_specs=[
                pl.BlockSpec((rows, 3 * KEEP), lambda t, me: (0, 0)),
                pl.BlockSpec((rows, 3 * KEEP), lambda t, me: (side, 0)),
                pl.BlockSpec((D // 4, 3 * KEEP), lambda t, me: (t, 0)),
            ],
            out_specs=[pl.BlockSpec((rows, D // 4), lambda t, me: (0, t))] * 2,
        ),
        out_shape=[jax.ShapeDtypeStruct((rows, D), BF)] * 2,
        name="proj_back",
        **params(),
    )(me, a, b, w)


def state_back_kernel(me, *refs):
    state1, gain, own, got, ds2, gate, wu, os0, os1, dz1, zz1, state0, zz0 = refs[:13]
    ds1, dos0, grad_wu, gate_sum, acc = refs[13:]
    t = pl.program_id(0)
    last = ds2[...].astype(F32)
    back = norm_back(
        state1[...], gain[...], own[...].astype(F32) + got[...].astype(F32)
    )[0]
    total = gate[...] * last + back
    ds1[...] = total
    dz0 = ((1.0 - gate[...]) * total).astype(BF)
    dos0[...] = mm_nt(dz0, wu[...]).astype(BF)

    @pl.when(t == 0)
    def _():
        acc[...] = jnp.zeros_like(acc)
        gate_sum[...] = jnp.zeros_like(gate_sum)

    acc[...] += mm_tn(os0[...], dz0) + mm_tn(os1[...], dz1[...])

    @pl.when(t // 2 == me[0])
    def _():
        step = state0[...].astype(F32) - zz0[...].astype(F32)
        terms = last * (state1[...] - zz1[...].astype(F32)) + total * step
        gate_sum[...] += eight_rows(terms)

    @pl.when(t == 3)
    def _():
        grad_wu[...] = acc[...].astype(BF)


def state_back(me, state1, gain, own, got, ds2, gate, wu, os0, os1, dz1, zz1, state0, zz0):
    row = pl.BlockSpec((DH, D), lambda t, me: (t, 0))
    head = pl.BlockSpec((DH, KEEP), lambda t, me: (t, 0))
    half = pl.BlockSpec((DH, D), lambda t, me: (t % 2, 0))
    line = full((1, D))
    return pl.pallas_call(
        state_back_kernel,
        grid_spec=pltpu.PrefetchScalarGridSpec(
            num_scalar_prefetch=1,
            grid=(4,),
            in_specs=[row, line, row, row, row, line, full((KEEP, D)), head, head, row, half]
            + [row, row],
            out_specs=[row, head, full((KEEP, D)), full((8, D))],
            scratch_shapes=[pltpu.VMEM((KEEP, D), F32)],
        ),
        out_shape=[
            jax.ShapeDtypeStruct((BLK, D), F32),
            jax.ShapeDtypeStruct((BLK, KEEP), BF),
            jax.ShapeDtypeStruct((KEEP, D), BF),
            jax.ShapeDtypeStruct((8, D), F32),
        ],
        name="state_back",
        **params(vmem=VMEM_GRADS),
    )(me, state1, gain, own, got, ds2, gate, wu, os0, os1, dz1, zz1, state0, zz0)


def row_back_kernel(me, values, gain, own, got, scale, base, out):
    back = norm_back(
        values[...].astype(F32), gain[...], own[...].astype(F32) + got[...].astype(F32)
    )[0]
    out[...] = (scale[...] * base[...] + back).astype(BF)


def row_back(me, values, gain, own, got, scale, base):
    count = own.shape[0] // DH
    skip = values.shape[0] // DH - count
    row = pl.BlockSpec((DH, D), lambda t, me: (t, 0))
    mine = pl.BlockSpec((DH, D), lambda t, me: (me[0] * skip + t, 0))
    return pl.pallas_call(
        row_back_kernel,
        grid_spec=pltpu.PrefetchScalarGridSpec(
            num_scalar_prefetch=1,
            grid=(count,),
            in_specs=[mine, full((1, D)), row, row, full((1, D)), mine],
            out_specs=row,
        ),
        out_shape=jax.ShapeDtypeStruct(own.shape, BF),
        name="row_back",
        **params(vmem=VMEM_GRADS),
    )(me, values, gain, own, got, scale, base)


def proj_grad_kernel(me, *refs):
    xa, xb, sa, sb, pa, pb, ra, rb, small = refs[:9]
    a_keep, a_send, b_keep, b_send, c_keep, c_send, tok, st = refs[9:]
    x0, y0 = me[1], me[3]
    in_z = lax.rem(pl.program_id(0), 2)
    tok[...] = mm_tn(xa[...], pa[...]) + mm_tn(xb[...], pb[...])
    st[...] = mm_tn(sa[...], ra[...]) + mm_tn(sb[...], rb[...])

    def write(ref, xr, yr, sub):
        rows = pl.ds(pl.multiple_of((x0 ^ xr) * DH, DH), DH)
        cols = pl.ds(pl.multiple_of((y0 ^ yr) * 768 + sub * 256, 256), 256)
        ref[0:DH, :] = tok[rows, cols].astype(BF)
        ref[DH : 2 * DH, :] = st[rows, cols].astype(BF)

    for xr in range(2):
        for yr in range(2):
            write((a_keep, a_send)[xr].at[yr, 0, 0], xr, yr, 0)
            (a_keep, a_send)[xr][yr, 0, 0, 2 * DH :, :] = small[x0 ^ xr, y0 ^ yr]
            write((b_keep, b_send)[yr].at[0, xr, 0], xr, yr, 1)
    for zb in range(2):

        @pl.when(in_z == zb)
        def _():
            for xr in range(2):
                for yr in range(2):
                    write((c_keep, c_send)[zb].at[xr, yr, 0], xr, yr, 2)


def proj_grads(me, xn, sn0, sn1, dp0, dp1, dr0, dr1, small):
    lhs = pl.BlockSpec((BLK, 2 * DH), lambda q, me: (0, q ^ me[2]))
    lhs1 = pl.BlockSpec((BLK, 2 * DH), lambda q, me: (1, q ^ me[2]))
    rhs = full((BLK, 3 * KEEP))
    shape = jax.ShapeDtypeStruct((2, 2, 2, 2 * DH, 2 * DH), BF)
    tall = jax.ShapeDtypeStruct((2, 2, 2, 2 * DH + 16, 2 * DH), BF)
    tail = (2 * DH, 2 * DH)
    a_tail = (2 * DH + 16, 2 * DH)
    a_spec = pl.BlockSpec((2, 1, 1) + a_tail, lambda q, me: (0, q % 2, q // 2, 0, 0))
    small_spec = pl.BlockSpec((2, 2, 16, 256), lambda q, me: (q ^ me[2], 0, 0, 0))
    b_spec = pl.BlockSpec((1, 2, 1) + tail, lambda q, me: (q % 2, 0, q // 2, 0, 0))
    c_spec = pl.BlockSpec((2, 2, 1) + tail, lambda q, me: (0, 0, q // 2, 0, 0))
    return pl.pallas_call(
        proj_grad_kernel,
        grid_spec=pltpu.PrefetchScalarGridSpec(
            num_scalar_prefetch=1,
            grid=(4,),
            in_specs=[lhs, lhs1, lhs, lhs, rhs, rhs, rhs, rhs, small_spec],
            out_specs=[a_spec, a_spec, b_spec, b_spec, c_spec, c_spec],
            scratch_shapes=[pltpu.VMEM((2 * DH, 3 * KEEP), F32)] * 2,
        ),
        out_shape=[tall] * 2 + [shape] * 4,
        name="proj_grad",
        **params(flops=4 * D * D * 3 * KEEP, moved=16 * 2**20, vmem=VMEM_GRADS),
    )(me, xn, xn, sn0, sn1, dp0, dp1, dr0, dr1, small)


def place_proj_kernel(me, p0, p1, w_tok, w_state, tok, st, gain_tok, gain_st, small):
    c0, y0 = me[0], me[3]
    starts = (0, 2 * DH + 16, 4 * DH + 16)
    for cr in range(2):
        for yr in range(2):
            src = (p0, p1)[cr].at[yr]
            for sub in range(3):
                for i in range(2):
                    j = 6 * (y0 ^ yr) + 2 * sub + i
                    at = (j // HL) * D + (2 * (j % HL) + (c0 ^ cr)) * DH
                    dst = pl.ds(pl.multiple_of(at, DH), DH)
                    cols = slice(i * DH, (i + 1) * DH)
                    row = starts[sub]
                    tok[:, dst] = src[row : row + DH, cols].astype(F32)
                    st[:, dst] = src[row + DH : row + 2 * DH, cols].astype(F32)
    for yr in range(2):
        first = p0[yr, 2 * DH : 2 * DH + 16, :].astype(F32)
        small[y0 ^ yr] = first + p1[yr, 2 * DH : 2 * DH + 16, :].astype(F32)
    ones = jnp.ones((8, 3 * D), F32)
    for out, grad, weight in ((gain_tok, tok, w_tok), (gain_st, st, w_state)):
        out[...] = lax.dot_general(
            ones,
            grad[...] * weight[...].astype(F32),
            (((1,), (1,)), ((), ())),
            precision=lax.Precision.HIGHEST,
            preferred_element_type=F32,
        )


def place_proj(me, p0, p1, w_tok, w_state):
    one = jax.ShapeDtypeStruct((DH, 3 * D), F32)
    line = jax.ShapeDtypeStruct((8, DH), F32)
    return pl.pallas_call(
        place_proj_kernel,
        grid_spec=pltpu.PrefetchScalarGridSpec(
            num_scalar_prefetch=1,
            grid=(1,),
            in_specs=[full(p0.shape)] * 2 + [full(w_tok.shape)] * 2,
            out_specs=[full((DH, 3 * D))] * 2 + [full((8, DH))] * 2 + [full((2, 16, 256))],
        ),
        out_shape=[one, one, line, line, jax.ShapeDtypeStruct((2, 16, 256), F32)],
        name="place_proj",
        **params(moved=5 * 2**20),
    )(me, p0, p1, w_tok, w_state)


def place_mlp_kernel(me, p0, p1, up, down):
    c0, y0 = me[0], me[3]
    for cr in range(2):
        for yr in range(2):
            src = (p0, p1)[cr].at[yr]
            row = ((c0 ^ cr) * 2 + (y0 ^ yr)) * DH
            big = pl.ds(pl.multiple_of(row, DH), MAIN)
            rest = pl.ds(pl.multiple_of(row + MAIN, REST), REST)
            up[big, :] = src[0:MAIN].astype(F32)
            down[big, :] = src[MAIN : 2 * MAIN].astype(F32)
            up[rest, :] = src[2 * MAIN : 2 * MAIN + REST].astype(F32)
            down[rest, :] = src[2 * MAIN + REST :].astype(F32)


def place_mlp(me, p0, p1):
    one = jax.ShapeDtypeStruct((2 * p0.shape[1], D), F32)
    return pl.pallas_call(
        place_mlp_kernel,
        grid_spec=pltpu.PrefetchScalarGridSpec(
            num_scalar_prefetch=1,
            grid=(1,),
            in_specs=[full(p0.shape)] * 2,
            out_specs=[full(one.shape)] * 2,
        ),
        out_shape=[one, one],
        name="place_mlp",
        **params(moved=6 * 2**20),
    )(me, p0, p1)


def body(
    tokens,
    state_in,
    gain_tok,
    gain_state,
    gain_mlp,
    w_tok,
    w_state,
    w_out,
    w_update,
    gate_bias,
    rel_bias,
    w_up,
    w_down,
    d_out,
    d_state_next,
):
    c = lax.axis_index("c")
    x = lax.axis_index("x")
    z = lax.axis_index("s")
    y = lax.axis_index("y")
    z1, z2 = z % 2, z // 2
    me = jnp.stack([c, x, z, y]).astype(jnp.int32)
    on_diag = c == x
    slots = state_in.shape[0]
    srows = state_in.shape[1]

    def pick(value, got):
        return jnp.where(on_diag, value, got)

    def by_block(own, other):
        return jnp.where(c == 0, jnp.concatenate([own, other]), jnp.concatenate([other, own]))

    def my_half(rows):
        return lax.dynamic_slice_in_dim(rows, c * HALF, HALF, 0)

    def other_half(rows):
        return lax.dynamic_slice_in_dim(rows, (1 - c) * HALF, HALF, 0)

    def to_slot(value, k):
        return lax.ppermute(value, "s", [(i, i ^ k) for i in range(slots)])

    def slot(value, k):
        return lax.dynamic_index_in_dim(value, z ^ k, 0, keepdims=False)

    def slot_order(parts):
        stacked = jnp.stack(parts).reshape(2, 2, srows, D)
        return untwist(stacked, (z2, z1)).reshape(slots, srows, D)

    def half_sum(part, got):
        return (part.astype(F32) + got.astype(F32)).astype(BF)

    def slot_spread(value):
        return [value[0]] + [to_slot(value[k], k) for k in range(1, slots)]

    subs = pick_columns(me, w_tok, w_state)
    small = jnp.stack([gain_tok, gain_state, gain_mlp, gate_bias])
    small = jnp.concatenate([small, jnp.pad(rel_bias, ((0, 0), (0, DH - NB)))])
    small = jnp.pad(small, ((0, 11), (0, DH)))
    ha, hb, hc = jnp.concatenate([subs[0], small]), subs[1], subs[2]
    got = [xch(hc, "z2"), xch(hb, "z2"), xch(ha, "z2"), diag_send(state_in), diag_send(tokens)]
    quarter = DH // 4
    at = (c * 2 + y) * quarter
    ho = jnp.concatenate(
        [
            lax.dynamic_slice_in_dim(w_out, at, quarter, 0),
            lax.dynamic_slice_in_dim(w_update, at, quarter, 0),
        ]
    )

    gc, gb, ga, g_states, g_tokens, ho = fence(got + [ho], got[:4])
    ha, hb, hc = jnp.stack([ha, ga]), jnp.stack([hb, gb]), jnp.stack([hc, gc])
    got = [xch(ha, "z1"), xch(hb, "x"), xch(hc, "y")]
    states = pick(state_in, g_states)
    half = [slot(states, 0), to_slot(slot(states, 2), 2)]
    g_piece = diag_send(ho)

    ga, gb, gc, half, g_piece, g_tokens = fence(
        got + [half, g_piece, g_tokens], got + [half, g_piece, g_tokens]
    )
    ha, hb, hc = jnp.stack([ha, ga]), jnp.stack([hb, gb]), jnp.stack([hc, gc])
    got = [xch(ha, "y"), xch(hb, "z1"), xch(hc, "x")]
    half = half + [to_slot(slot(states, 3), 3)]
    x_own = pick(tokens, g_tokens)
    x_oth = xch(x_own, "c")
    ho = pick(ho, g_piece)
    hid = w_up.shape[0] // 4
    hid_at = (c * 2 + y) * hid
    hu = lax.dynamic_slice_in_dim(w_up, hid_at, hid, 0)
    hd = lax.dynamic_slice_in_dim(w_down, hid_at, hid, 0)
    hm = jnp.concatenate([hu[:MAIN], hd[:MAIN], hu[MAIN:], hd[MAIN:]])

    def three(value):
        return value[:MAIN], value[MAIN : 2 * MAIN], value[2 * MAIN :]

    def stacks(held, got):
        return [jnp.stack([h, g]) for h, g in zip(held, got)]

    def sends(held, bits):
        return [xch(h, b) for h, b in zip(held, bits)]

    ga, gb, gc, half, ho, x_own, x_oth, hm = fence(
        got + [half, ho, x_own, x_oth, hm], got + [half, x_oth]
    )
    half = half[:1] + [to_slot(slot(states, 1), 1)] + half[1:]
    ha, hb, hc = jnp.stack([ha, ga]), jnp.stack([hb, gb]), jnp.stack([hc, gc])
    got = [xch(ha, "x"), xch(hb, "y"), xch(hc, "z1")]
    half = jnp.concatenate(half)
    state0 = by_block(half, xch(half, "c"))
    rows = by_block(x_own, x_oth).astype(F32)
    x_hat = norm_parts(rows)[0]
    s_hat = norm_parts(state0.astype(F32))[0]
    go = xch(ho, "z2")

    got, go, hm, x_hat, s_hat, d_out, d_state_next = fence(
        (got, go, hm, x_hat, s_hat, d_out, d_state_next), (got, x_hat, s_hat)
    )
    ho = jnp.stack([ho, go])
    gm = xch(hm, "z2")
    go = xch(ho, "x")
    g_states = diag_send(d_state_next)
    w_tok_l, w_state_l, small_all = lay_tables(me, (ha, got[0]), (hb, got[1]), (hc, got[2]))
    vectors = small_all[:, :4, :DH].transpose(1, 0, 2).reshape(4, D).astype(F32)
    g_tok, g_state, g_mlp = vectors[0], vectors[1], vectors[2]
    gate = jax.nn.sigmoid(vectors[3])
    xn = (x_hat * g_tok).astype(BF)
    proj = mm(xn, w_tok_l).astype(BF)

    go, g_states, proj, small_all = fence((go, g_states, proj, small_all), (go, proj))
    ho = jnp.stack([ho, go])
    tu, to = ho[:, :, quarter:], ho[:, :, :quarter]
    gt, go = xch(tu, "z1"), xch(to, "y")
    d_states = pick(d_state_next, g_states)
    d_rows = [slot(d_states, 0)] + [to_slot(slot(d_states, k), k) for k in (1, 2)]
    sn0 = (s_hat * g_state).astype(BF)
    r0 = mm(sn0, w_state_l).astype(BF)
    rel_rows = small_all[:, 4, :NB].reshape(HL, 2, NB)
    rel_mine = lax.dynamic_index_in_dim(rel_rows, c, 1, keepdims=False)
    hot = jnp.asarray(slab_buckets())[None, :] == jnp.arange(NB, dtype=jnp.int32)[:, None]
    base = mm(rel_mine, hot.astype(BF)).reshape(HL, 8, BLK)
    bias = bias_tables(base)
    os0, log_s0 = mem_forward(0, proj, r0)

    gt, go, gm, r0, os0, bias, d_states, d_rows = fence(
        (gt, go, gm, r0, os0, bias, d_states, d_rows), (gt, gm, os0, bias)
    )
    d_rows = d_rows + [to_slot(slot(d_states, 3), 3)]
    tu = jnp.stack([tu, gt])
    gt = xch(tu, "y")
    hm = stacks(three(hm), three(gm))
    gm = sends(hm, ("z1", "x", "y"))
    to = jnp.stack([to, go])
    ot0, log_t0 = tok_forward(0, proj, r0, bias)

    to, gt, gm, os0, ot0, d_half = fence((to, gt, gm, os0, ot0, d_rows), (gt, os0, ot0))
    wu = lay_out_table("y", me, tu, gt)
    hm = stacks(hm, gm)
    gm = sends(hm, ("x", "y", "z1"))
    go = xch(to, "z1")
    zp0 = mm(os0, wu)
    zz0 = zp0 + xch(zp0.astype(BF), "c").astype(F32)
    zz0_kept = zz0.astype(BF)
    state1 = gate * state0.astype(F32) + (1.0 - gate) * zz0
    sn1 = (norm_parts(state1)[0] * g_state).astype(BF)
    r1 = mm(sn1, w_state_l).astype(BF)
    ot1, log_t1 = tok_forward(1, proj, r1, bias)

    gm, go, ot1, r1, d_out, d_half = fence(
        (gm, go, ot1, r1, d_out, d_half), (gm, ot1, d_half)
    )
    wo = lay_out_table("z", me, to, go)
    hm = stacks(hm, gm)
    gm = sends(hm, ("y", "z1", "x"))
    d_half = jnp.concatenate(d_half)
    ds2 = by_block(d_half, xch(d_half, "c"))
    g_dout = diag_send(d_out)
    part0, part1 = mm(ot0, wo), mm(ot1, wo)
    part_own = jnp.where(c == 0, part0, part1)
    part_oth = jnp.where(c == 0, part1, part0).astype(BF)
    mid = x_own.astype(F32) + part_own + xch(part_oth, "c").astype(F32)
    h_own = (norm_parts(mid)[0] * g_mlp).astype(BF)
    h_oth = xch(h_own, "c")
    os1, log_s1 = mem_forward(1, proj, r1)
    zp1 = mm(os1, wu)
    zz1 = my_half(zp1) + xch(other_half(zp1).astype(BF), "c").astype(F32)
    state1_half = my_half(state1)
    state2_half = (gate * state1_half + (1.0 - gate) * zz1).astype(BF)
    dz1 = ((1.0 - gate) * ds2.astype(F32)).astype(BF)
    dos1 = mm_nt(dz1, wu).astype(BF)
    dm1, dt1 = mem_backward(1, proj, r1, dos1, log_s1)

    gm, h_own, h_oth, g_dout, state2_half = fence(
        (gm, h_own, h_oth, g_dout, state2_half), (gm, h_own, h_oth, g_dout, state2_half, dm1)
    )
    d_own = pick(d_out, g_dout)
    d_oth = xch(d_own, "c")
    out_rows = slot_spread(state2_half.reshape(slots, srows, D))
    ma, ma_out, mb, mb_out, mc, mc_out, o_own, o_oth, e_own, e_oth = mlp(
        h_own,
        h_oth,
        d_own,
        d_oth,
        hm[0],
        gm[0],
        hm[1],
        gm[1],
        hm[2],
        gm[2],
    )

    out_rows, ma_out, mb_out, mc_out, o_oth, e_oth = fence(
        (out_rows, ma_out, mb_out, mc_out, o_oth, e_oth), (out_rows, o_oth, e_oth)
    )
    got = [xch(ma_out, "x"), xch(mb_out, "y"), xch(mc_out, "z1")]
    state_next = slot_order(out_rows)
    e_got, o_got = xch(e_oth, "c"), xch(o_oth, "c")
    dmid, da_own, output, gain_rows = mid_back(
        mid, g_mlp[None], e_own, e_got, d_own, o_own, o_got
    )
    dot_all, grad_wo = out_back(me, da_own, xch(da_own, "c"), wo, ot0, ot1)
    dr1, dp1, dprev, rel1 = tok_backward(1, proj, r1, bias, dot_all, log_t1, dt1, dm1)

    got, dr1, dprev, output, state_next = fence(
        (got, dr1, dprev, output, state_next), (got, dr1, dprev, output)
    )
    (ma, mb, mc), sends = add_halves((ma, mb, mc), got)
    got = [xch(s, b) for s, b in zip(sends, ("y", "z1", "x"))]
    got += [diag_send(output), diag_send(state_next)]
    dsn1 = proj_one(dr1, w_state_l)
    dsn1_got = xch(dsn1, "c")
    dm0, dt0, rel0 = tok_backward(0, proj, r0, bias, dot_all, log_t0, dprev)

    got, dm0, dt0, dsn1, dsn1_got = fence((got, dm0, dt0, dsn1, dsn1_got), (got, dm0, dsn1_got))
    output = pick(output, got[3])
    state_next = pick(state_next, got[4]).astype(F32)
    (ma, mb, mc), sends = add_halves((ma, mb, mc), got[:3])
    got = [xch(s, b) for s, b in zip(sends, ("z1", "x", "y"))]
    ds1, dos0, grad_wu, gate_rows = state_back(
        me,
        state1,
        g_state[None],
        dsn1,
        dsn1_got,
        ds2,
        gate[None],
        wu,
        os0,
        os1,
        dz1,
        zz1.astype(BF),
        state0,
        zz0_kept,
    )
    grad_gate = jnp.sum(gate_rows, axis=0) * gate * (1.0 - gate)
    grad_g_mlp = jnp.sum(gain_rows, axis=0)
    rel_sum = (rel0 + rel1).reshape(HL, 8 * BLK)
    grad_rel = lax.dot_general(
        rel_sum,
        hot.astype(F32),
        (((1,), (1,)), ((), ())),
        precision=lax.Precision.HIGHEST,
        preferred_element_type=F32,
    )
    both = jnp.stack([grad_rel, jnp.zeros_like(grad_rel)], axis=1)
    both = jnp.where(c == 0, both, jnp.flip(both, 1)).reshape(H, NB)
    first = jnp.concatenate([grad_g_mlp.reshape(H, DH), jnp.pad(both, ((0, 0), (0, DH - NB)))], 1)
    second = jnp.pad(grad_gate.reshape(H, DH), ((0, 0), (0, DH)))
    small_sums = jnp.stack([first, second], axis=1)[:, :, None, :].astype(BF)
    small_sums = jnp.pad(small_sums, ((0, 0), (0, 0), (0, 15), (0, 0)))
    outs = jnp.stack([grad_wo, grad_wu]).astype(BF).reshape(2, 2, 2, 2, 2, quarter, D)

    got, dos0, outs = fence((got, dos0, outs), (got, dos0, outs))
    (ma, mb, mc), sends = add_halves((ma, mb, mc), got)
    got_m = [xch(s, "z2") for s in sends]
    names = ["z2", "z1", "x", "y"]
    spots = {"z2": z2, "z1": z1, "x": x, "y": y}

    def split_outs(value, bit):
        axis = names.index(bit) + 1
        names.remove(bit)
        keep = lax.dynamic_index_in_dim(value, spots[bit], axis, keepdims=False)
        send = lax.dynamic_index_in_dim(value, 1 - spots[bit], axis, keepdims=False)
        return keep, send

    keep_o, send_o = split_outs(outs, "y")
    got_o = xch(send_o, "y")
    dr0, dp0 = mem_backward(0, proj, r0, dos0, log_s0, dm0, dt0)

    got_o, got_m, dr0, dp0, xn, sn0, sn1 = fence(
        (got_o, got_m, dr0, dp0, xn, sn0, sn1), (got_o, got_m, dr0, dp0)
    )
    mlp_part = [half_sum(h, g) for h, g in zip((ma, mb, mc), got_m)]
    mlp_part = over_groups(jnp.concatenate(mlp_part))
    got_m = xch(mlp_part, "y")
    keep_o, send_o = split_outs(half_sum(keep_o, got_o), "x")
    got_o = xch(send_o, "x")
    ha, ha_out, hb, hb_out, hc, hc_out = proj_grads(
        me, xn, sn0, sn1, dp0, dp1, dr0, dr1, small_sums
    )

    got_o, got_m, ha_out, hb_out, hc_out, dr0, dp0 = fence(
        (got_o, got_m, ha_out, hb_out, hc_out, dr0, dp0), (got_o, got_m, ha_out)
    )
    both_m = jnp.stack([mlp_part, got_m])
    got_c = xch(both_m, "c")
    got = [xch(ha_out, "x"), xch(hb_out, "y"), xch(hc_out, "z1")]
    dxn, dxn_send = proj_back(me, dp0, dp1, w_tok_l)
    dxn_got = xch(dxn_send, "c")
    dsn0, dsn0_send = proj_back(me, dr0, dr0, w_state_l)
    dsn0_got = xch(dsn0_send, "c")

    got, got_o, dxn_got, dsn0_got = fence(
        (got, got_o, dxn_got, dsn0_got), (got, got_o, dxn_got, dsn0_got)
    )
    (ha, hb, hc), sends = add_halves((ha, hb, hc), got)
    got = [xch(s, b) for s, b in zip(sends, ("y", "z1", "x"))]
    keep_o, send_o = split_outs(half_sum(keep_o, got_o), "z1")
    got_o = xch(send_o, "z1")
    one = jnp.ones((1, D), F32)
    grad_tokens = row_back(me, x_own, g_tok[None], dxn, dxn_got, one, dmid)

    got, got_o, grad_tokens, dsn0_got = fence(
        (got, got_o, grad_tokens, dsn0_got), (got, got_o, grad_tokens)
    )
    (ha, hb, hc), sends = add_halves((ha, hb, hc), got)
    got = [xch(s, b) for s, b in zip(sends, ("z1", "x", "y"))]
    keep_o, send_o = split_outs(half_sum(keep_o, got_o), "z2")
    got_o = xch(send_o, "z2")
    grad_state = row_back(me, state0, g_state[None], dsn0, dsn0_got, gate[None], ds1)
    grad_state = grad_state.reshape(slots, srows, D)

    got, got_o, grad_state, grad_tokens = fence(
        (got, got_o, grad_state, grad_tokens), (got, got_o, grad_state)
    )
    (ha, hb, hc), sends = add_halves((ha, hb, hc), got)
    got = [xch(s, "z2") for s in sends]
    got_t = diag_send(grad_tokens)
    outs = over_groups(half_sum(keep_o, got_o))
    outs = jnp.stack([outs, xch(outs, "y")])
    grad_up, grad_down = place_mlp(me, both_m, got_c)

    got, got_t, outs, grad_state, grad_up = fence(
        (got, got_t, outs, grad_state, grad_up), (got, got_t, outs, grad_up)
    )
    part = over_groups(jnp.concatenate([half_sum(h, g) for h, g in zip((ha, hb, hc), got)]))
    got_y = xch(part, "y")
    grad_rows = slot_spread(grad_state)
    outs = jnp.stack([outs, xch(outs, "x")])
    grad_tokens = pick(grad_tokens, got_t).astype(F32)

    got_y, grad_rows, outs = fence((got_y, grad_rows, outs), (got_y,))
    both_t = jnp.stack([part, got_y])
    got_p = xch(both_t, "c")
    grad_state = slot_order(grad_rows)
    grad_state = pick(grad_state, diag_send(grad_state)).astype(F32)
    outs = untwist(outs, (x, y)).transpose(2, 0, 1, 3, 4).reshape(2, DH, D)
    outs = pick(outs, xch(outs, "c")).astype(F32)
    grad_tok_w, grad_state_w, rows_tok, rows_st, small = place_proj(
        me, both_t, got_p, w_tok, w_state
    )
    grad_g_tok = rows_tok[0] / gain_tok.astype(F32)
    grad_g_state = rows_st[0] / gain_state.astype(F32)

    return (
        output,
        state_next,
        grad_tokens,
        grad_state,
        grad_g_tok,
        grad_g_state,
        small[0, 0, :DH],
        grad_tok_w,
        grad_state_w,
        outs[0],
        outs[1],
        small[1, 0, :DH],
        small[0, 0:1, DH : DH + NB],
        grad_up,
        grad_down,
    )


def solution(mesh):
    reps, shards = mesh.devices.shape
    grid = Mesh(mesh.devices.reshape(reps // 4, 2, 2, shards // 2, 2), ("h", "y", "c", "s", "x"))
    rep, shard = ("h", "y", "c"), ("s", "x")
    every = rep + shard
    by_token = P(every, None)
    by_state = P(rep, shard, None)
    line = P(shard)
    table = P(shard, None)
    params_spec = (line, line, line, table, table, table, table, line, table, table, table)
    return jax.shard_map(
        body,
        mesh=grid,
        in_specs=(by_token, by_state) + params_spec + (by_token, by_state),
        out_specs=(by_token, by_state, by_token, by_state) + params_spec,
        check_vma=False,
    )
```

```python
import functools
import math

import jax
import jax.numpy as jnp
import numpy as np
from jax import lax
from jax.experimental import pallas as pl
from jax.experimental.pallas import tpu as pltpu
from jax.sharding import Mesh
from jax.sharding import PartitionSpec as P


D = 1024
H = 8
HL = 4
DH = D // H
BLK = 512
M = 512
NB = 32
REACH = 128
HALF = 256
KEEP = HL * DH
NEG = -1e30
eps = 1e-06
SCALE = 1.0 / math.sqrt(DH)
BF = jnp.bfloat16
F32 = jnp.float32

AXIS_BITS = {"c": ("c", 1), "x": ("x", 1), "y": ("y", 1), "z1": ("s", 1), "z2": ("s", 2)}
VMEM_MLP = 44
VMEM_GRADS = 56
VMEM_MOST = 18
COST_CUT = 10


def xch(value, bit):
    axis, mask = AXIS_BITS[bit]
    count = lax.axis_size(axis)
    return lax.ppermute(value, axis, [(i, i ^ mask) for i in range(count)])


def diag_send(value):
    return lax.ppermute(value, ("c", "x"), [(1, 2), (2, 1)])


def over_groups(part):
    groups = lax.axis_size("h")
    step = 1
    while step < groups:
        got = lax.ppermute(part, "h", [(i, i ^ step) for i in range(groups)])
        part = (part.astype(F32) + got.astype(F32)).astype(part.dtype)
        step *= 2
    return part


def fence(values, done):
    leaves, tree = jax.tree.flatten(values)
    tied = lax.optimization_barrier(tuple(leaves) + tuple(jax.tree.leaves(done)))
    return jax.tree.unflatten(tree, tied[: len(leaves)])


def untwist(value, bits):
    for axis, bit in enumerate(bits):
        value = jnp.where(bit == 1, jnp.flip(value, axis), value)
    return value


def mm(a, b):
    return jnp.dot(a, b, preferred_element_type=F32)


def mm_nt(a, b):
    return lax.dot_general(a, b, (((1,), (1,)), ((), ())), preferred_element_type=F32)


def mm_tn(a, b):
    return lax.dot_general(a, b, (((0,), (0,)), ((), ())), preferred_element_type=F32)


def norm_parts(values):
    centered = values - jnp.mean(values, axis=-1, keepdims=True)
    variance = jnp.mean(centered * centered, axis=-1, keepdims=True)
    rstd = lax.rsqrt(variance + eps)
    return centered * rstd, rstd


def norm_back(values, gain, grad):
    hat, rstd = norm_parts(values)
    g = grad * gain
    inner = g - jnp.mean(g, axis=-1, keepdims=True)
    inner = inner - hat * jnp.mean(g * hat, axis=-1, keepdims=True)
    return inner * rstd, grad * hat


def bucket_table(block_len, bucket_count, reach_len):
    distance = np.arange(2 * block_len + 1)
    exact = bucket_count // 2
    ratio = np.log(np.maximum(distance, 1) / exact) / np.log(reach_len / exact)
    far = np.minimum(
        exact + np.floor(ratio * (bucket_count - exact)).astype(np.int64), bucket_count - 1
    )
    return np.where(distance < exact, distance, far).astype(np.int32)


def slab_buckets():
    s = np.arange(8)[:, None]
    col = np.arange(BLK)[None, :]
    return bucket_table(BLK, NB, REACH)[(s - col) % BLK].reshape(-1)


def params(flops=0, moved=0, trans=0, grid=1, vmem=VMEM_MOST):
    return dict(
        compiler_params=pltpu.CompilerParams(
            vmem_limit_bytes=vmem * 2**20, dimension_semantics=("arbitrary",) * grid
        ),
        cost_estimate=pl.CostEstimate(
            flops=flops // COST_CUT, bytes_accessed=moved // COST_CUT, transcendentals=0
        ),
    )


def full(shape, memory_space=None):
    return pl.BlockSpec(
        shape, lambda *_: (0,) * len(shape), pipeline_mode=pl.Buffered(buffer_count=1)
    )


def pick_kernel(me, tok, st, *outs):
    c, y = me[0], me[3]
    for sub in range(3):
        for i in range(2):
            j = 6 * y + 2 * sub + i
            col = (j // HL) * D + (2 * (j % HL) + c) * DH
            src = pl.ds(pl.multiple_of(col, DH), DH)
            dst = slice(i * DH, (i + 1) * DH)
            outs[sub][0:DH, dst] = tok[:, src]
            outs[sub][DH : 2 * DH, dst] = st[:, src]


def pick_columns(me, w_tok, w_state):
    one = jax.ShapeDtypeStruct((2 * DH, 2 * DH), BF)
    return pl.pallas_call(
        pick_kernel,
        grid_spec=pltpu.PrefetchScalarGridSpec(
            num_scalar_prefetch=1,
            grid=(1,),
            in_specs=[full(w_tok.shape), full(w_state.shape)],
            out_specs=[full((2 * DH, 2 * DH))] * 3,
        ),
        out_shape=[one] * 3,
        name="pick",
        **params(moved=3 * 2**20),
    )(me, w_tok, w_state)


def lay_kernel(me, a0, a1, b0, b1, c0, c1, tok, st, small):
    q = pl.program_id(0)
    x0, y0 = me[1], me[3]
    low = lax.rem(q, 2) == 0
    c_val = jnp.where(low, c0[...], c1[...])
    for xr in range(2):
        for yr in range(2):
            va = (a0, a1)[xr][yr, 0, 0]
            vb = (b0, b1)[yr][0, xr, 0]
            vc = c_val[xr, yr, 0]
            rows = pl.ds(pl.multiple_of((x0 ^ xr) * DH, DH), DH)
            for sub, v in enumerate((va, vb, vc)):
                cols = pl.ds(pl.multiple_of((y0 ^ yr) * 768 + sub * 256, 256), 256)
                tok[rows, cols] = v[0:DH]
                st[rows, cols] = v[DH : 2 * DH]
        small[x0 ^ xr] = (a0, a1)[xr][0, 0, 0, 2 * DH : 2 * DH + 16]


def lay_tables(me, a, b, c):
    ra = a[0].shape[-2]
    a_spec = pl.BlockSpec((2, 1, 1, ra, 256), lambda q, me: (0, q % 2, q // 2, 0, 0))
    b_spec = pl.BlockSpec((1, 2, 1, 256, 256), lambda q, me: (q % 2, 0, q // 2, 0, 0))
    c_spec = pl.BlockSpec((2, 2, 1, 256, 256), lambda q, me: (0, 0, q // 2, 0, 0))
    w_spec = pl.BlockSpec((2 * DH, 3 * KEEP), lambda q, me: (q ^ me[2], 0))
    return pl.pallas_call(
        lay_kernel,
        grid_spec=pltpu.PrefetchScalarGridSpec(
            num_scalar_prefetch=1,
            grid=(4,),
            in_specs=[a_spec, a_spec, b_spec, b_spec, c_spec, c_spec],
            out_specs=[
                w_spec,
                w_spec,
                pl.BlockSpec((2, 16, 256), lambda q, me: (q ^ me[2], 0, 0)),
            ],
        ),
        out_shape=[
            jax.ShapeDtypeStruct((D, 3 * KEEP), BF),
            jax.ShapeDtypeStruct((D, 3 * KEEP), BF),
            jax.ShapeDtypeStruct((8, 16, 256), BF),
        ],
        name="lay",
        **params(moved=14 * 2**20),
    )(me, *a, *b, *c)


def lay_out_kernel(last, me, low, high, out):
    x0, z0, y0 = me[1], me[2], me[3]
    q = low.shape[3]
    for yr in range(2):
        for xr in range(2):
            for zr in range(4):
                row = (z0 ^ zr) * DH + ((x0 ^ xr) * 2 + (y0 ^ yr)) * q
                if last == "y":
                    v = (low, high)[yr][zr % 2, xr, zr // 2]
                else:
                    v = (low, high)[zr % 2][yr, xr, zr // 2]
                out[pl.ds(pl.multiple_of(row, q), q), :] = v


def lay_out_table(last, me, low, high):
    return pl.pallas_call(
        functools.partial(lay_out_kernel, last),
        grid_spec=pltpu.PrefetchScalarGridSpec(
            num_scalar_prefetch=1,
            grid=(1,),
            in_specs=[full(low.shape), full(high.shape)],
            out_specs=full((KEEP, D)),
        ),
        out_shape=jax.ShapeDtypeStruct((KEEP, D), BF),
        name="lay_out",
        **params(moved=2 * 2**20),
    )(me, low, high)


def bias_kernel(base, out):
    slab = base[0]
    for a in range(0, 64, 2):
        two = jnp.concatenate(
            [pltpu.roll(slab, 8 * a, 1), pltpu.roll(slab, 8 * a + 8, 1)], axis=0
        )
        out[0, 8 * a : 8 * a + 16, :] = two.astype(BF)


def bias_tables(base):
    return pl.pallas_call(
        bias_kernel,
        grid=(HL,),
        in_specs=[pl.BlockSpec((1, 8, BLK), lambda h: (h, 0, 0))],
        out_specs=pl.BlockSpec((1, BLK, BLK), lambda h: (h, 0, 0)),
        out_shape=jax.ShapeDtypeStruct((HL, BLK, BLK), BF),
        name="bias",
        **params(moved=2 * 2**20),
    )(base)


def lower_mask():
    rows = lax.broadcasted_iota(jnp.int32, (HALF, HALF), 0)
    cols = lax.broadcasted_iota(jnp.int32, (HALF, HALF), 1)
    return rows >= cols


def head_lane(h):
    return lax.broadcasted_iota(jnp.int32, (HALF, DH), 1) == h


def window_scores(t, has_prev, qt, ko, kp, bias, rows, lower):
    near = bias[0, rows, rows].astype(F32)
    near_own = mm_nt(qt, ko[rows, :]) * SCALE
    if has_prev:
        near_prev = mm_nt(qt, kp[rows, :]) * SCALE
        s_near = jnp.where(lower, near_own, near_prev) + near
    else:
        s_near = jnp.where(lower, near_own + near, NEG)
    s_far = None
    if t == 1:
        s_far = mm_nt(qt, ko[0:HALF, :]) * SCALE + bias[0, rows, 0:HALF].astype(F32)
    elif has_prev:
        s_far = mm_nt(qt, kp[HALF:BLK, :]) * SCALE + bias[0, rows, HALF:BLK].astype(F32)
    s_edge = None
    if has_prev:
        pair = qt.astype(F32) * kp[rows, :].astype(F32)
        s_edge = jnp.sum(pair, axis=1, keepdims=True) * SCALE + bias[0, 0:1, 1:2].astype(F32)
    return s_near, s_far, s_edge


def tok_fwd_kernel(has_prev, *refs):
    if has_prev:
        q, km, vm, ko, vo, bias, kp, vp, out, logs = refs
    else:
        q, km, vm, ko, vo, bias, out, logs = refs
        kp = vp = None
    h = pl.program_id(0)
    lower = lower_mask()
    for t in range(2):
        rows = slice(t * HALF, (t + 1) * HALF)
        qt = q[rows, :]
        s_mem = mm_nt(qt, km[...]) * SCALE
        s_near, s_far, s_edge = window_scores(t, has_prev, qt, ko, kp, bias, rows, lower)
        top = jnp.maximum(
            jnp.max(s_mem, axis=1, keepdims=True), jnp.max(s_near, axis=1, keepdims=True)
        )
        if s_far is not None:
            top = jnp.maximum(top, jnp.max(s_far, axis=1, keepdims=True))
        if has_prev:
            top = jnp.maximum(top, s_edge)
        e_mem = jnp.exp(s_mem - top)
        e_near = jnp.exp(s_near - top)
        total = jnp.sum(e_mem, axis=1, keepdims=True) + jnp.sum(e_near, axis=1, keepdims=True)
        acc = mm(e_mem.astype(BF), vm[...])
        if has_prev:
            acc += mm(jnp.where(lower, e_near, 0.0).astype(BF), vo[rows, :])
            acc += mm(jnp.where(lower, 0.0, e_near).astype(BF), vp[rows, :])
            e_edge = jnp.exp(s_edge - top)
            total += e_edge
            acc += e_edge * vp[rows, :].astype(F32)
        else:
            acc += mm(e_near.astype(BF), vo[rows, :])
        if s_far is not None:
            e_far = jnp.exp(s_far - top)
            total += jnp.sum(e_far, axis=1, keepdims=True)
            v_far = vo[0:HALF, :] if t == 1 else vp[HALF:BLK, :]
            acc += mm(e_far.astype(BF), v_far)
        out[rows, :] = (acc / total).astype(BF)
        keep = jnp.where(h == 0, 0.0, logs[rows, :])
        logs[rows, :] = jnp.where(head_lane(h), top + jnp.log(total), keep)


def col(block, at):
    return pl.BlockSpec((BLK, DH), lambda h: (block, at * HL + h))


def tok_forward(block, proj, mem_proj, bias):
    has_prev = block > 0
    specs = [col(block, 0), col(0, 1), col(0, 2), col(block, 1), col(block, 2)]
    specs += [pl.BlockSpec((1, BLK, BLK), lambda h: (h, 0, 0))]
    ops = [proj, mem_proj, mem_proj, proj, proj, bias]
    if has_prev:
        specs += [col(block - 1, 1), col(block - 1, 2)]
        ops += [proj, proj]
    return pl.pallas_call(
        functools.partial(tok_fwd_kernel, has_prev),
        grid=(HL,),
        in_specs=specs,
        out_specs=[col(0, 0), full((BLK, DH))],
        out_shape=[
            jax.ShapeDtypeStruct((BLK, KEEP), BF),
            jax.ShapeDtypeStruct((BLK, DH), F32),
        ],
        name="tok_fwd",
        **params(flops=4 * BLK * 1280 * KEEP, moved=8 * 2**20, trans=HL * BLK * 1024),
    )(*ops)


def mem_fwd_kernel(q, ks, vs, ko, vo, out, logs):
    h = pl.program_id(0)
    for t in range(2):
        rows = slice(t * HALF, (t + 1) * HALF)
        qt = q[rows, :]
        s1 = mm_nt(qt, ks[...]) * SCALE
        s2 = mm_nt(qt, ko[...]) * SCALE
        top = jnp.maximum(jnp.max(s1, axis=1, keepdims=True), jnp.max(s2, axis=1, keepdims=True))
        e1 = jnp.exp(s1 - top)
        e2 = jnp.exp(s2 - top)
        total = jnp.sum(e1, axis=1, keepdims=True) + jnp.sum(e2, axis=1, keepdims=True)
        acc = mm(e1.astype(BF), vs[...]) + mm(e2.astype(BF), vo[...])
        out[rows, :] = (acc / total).astype(BF)
        keep = jnp.where(h == 0, 0.0, logs[rows, :])
        logs[rows, :] = jnp.where(head_lane(h), top + jnp.log(total), keep)


def mem_forward(block, proj, mem_proj):
    return pl.pallas_call(
        mem_fwd_kernel,
        grid=(HL,),
        in_specs=[col(0, 0), col(0, 1), col(0, 2), col(block, 1), col(block, 2)],
        out_specs=[col(0, 0), full((BLK, DH))],
        out_shape=[
            jax.ShapeDtypeStruct((BLK, KEEP), BF),
            jax.ShapeDtypeStruct((BLK, DH), F32),
        ],
        name="mem_fwd",
        **params(flops=4 * BLK * 1024 * KEEP, moved=4 * 2**20, trans=HL * BLK * 1024),
    )(mem_proj, mem_proj, mem_proj, proj, proj)


def head_cols(at, h):
    return pl.ds(pl.multiple_of((at * HL + h) * DH, DH), DH)


def mem_bwd_kernel(final, *refs):
    if final:
        q, ks, vs, ko, vo, do, logs, aks, avs, aq, ak, av, d_mem, d_tok, dks, dvs, dko, dvo = refs
    else:
        q, ks, vs, ko, vo, do, logs, d_mem, d_tok, dks, dvs, dko, dvo = refs
    h = pl.program_id(0)
    kind = BF if final else F32
    for t in range(2):
        rows = slice(t * HALF, (t + 1) * HALF)
        qt = q[rows, :]
        dt = do[rows, :]
        log_t = jnp.sum(jnp.where(head_lane(h), logs[rows, :], 0.0), axis=1, keepdims=True)
        p1 = jnp.exp(mm_nt(qt, ks[...]) * SCALE - log_t)
        p2 = jnp.exp(mm_nt(qt, ko[...]) * SCALE - log_t)
        w1 = mm_nt(dt, vs[...])
        w2 = mm_nt(dt, vo[...])
        inner = jnp.sum(p1 * w1, axis=1, keepdims=True) + jnp.sum(p2 * w2, axis=1, keepdims=True)
        g1 = (p1 * (w1 - inner)).astype(BF)
        g2 = (p2 * (w2 - inner)).astype(BF)
        dq = (mm(g1, ks[...]) + mm(g2, ko[...])) * SCALE
        d_mem[rows, head_cols(0, h)] = dq.astype(kind)
        terms = (
            (dks, mm_tn(g1, qt) * SCALE),
            (dko, mm_tn(g2, qt) * SCALE),
            (dvs, mm_tn(p1.astype(BF), dt)),
            (dvo, mm_tn(p2.astype(BF), dt)),
        )
        for ref, term in terms:
            if t == 0:
                ref[...] = term
            else:
                ref[...] += term
    if final:
        d_mem[:, head_cols(1, h)] = (dks[...] + aks[...]).astype(BF)
        d_mem[:, head_cols(2, h)] = (dvs[...] + avs[...]).astype(BF)
        d_tok[:, head_cols(0, h)] = aq[...].astype(BF)
        d_tok[:, head_cols(1, h)] = (dko[...] + ak[...]).astype(BF)
        d_tok[:, head_cols(2, h)] = (dvo[...] + av[...]).astype(BF)
    else:
        d_mem[:, head_cols(1, h)] = dks[...]
        d_mem[:, head_cols(2, h)] = dvs[...]
        d_tok[:, head_cols(0, h)] = dko[...]
        d_tok[:, head_cols(1, h)] = dvo[...]


def mem_backward(block, proj, mem_proj, grad_mix, logs, add_mem=None, add_tok=None):
    final = add_mem is not None
    specs = [col(0, 0), col(0, 1), col(0, 2), col(block, 1), col(block, 2), col(0, 0)]
    specs += [full((BLK, DH))]
    ops = [mem_proj, mem_proj, mem_proj, proj, proj, grad_mix, logs]
    if final:
        specs += [col(0, 0), col(0, 1), col(0, 0), col(0, 1), col(0, 2)]
        ops += [add_mem, add_mem, add_tok, add_tok, add_tok]
    kind = BF if final else F32
    wide = 3 * KEEP if final else 2 * KEEP
    return pl.pallas_call(
        functools.partial(mem_bwd_kernel, final),
        grid=(HL,),
        in_specs=specs,
        out_specs=[full((BLK, 3 * KEEP)), full((BLK, wide))],
        out_shape=[
            jax.ShapeDtypeStruct((BLK, 3 * KEEP), kind),
            jax.ShapeDtypeStruct((BLK, wide), kind),
        ],
        scratch_shapes=[pltpu.VMEM((BLK, DH), F32)] * 4,
        name="mem_bwd",
        **params(
            flops=10 * BLK * 1024 * KEEP,
            moved=9 * 2**20,
            vmem=VMEM_GRADS if final else VMEM_MOST,
        ),
    )(*ops)


def tok_bwd_kernel(has_prev, *refs):
    if has_prev:
        q, km, vm, ko, vo, bias, do, logs, kp, vp, sq, sk, sv, ak, av = refs[:15]
        d_mem, d_tok, d_prev, rel, dkm, dvm, dko, dvo, dkp, dvp = refs[15:]
    else:
        q, km, vm, ko, vo, bias, do, logs, ak, av = refs[:10]
        d_mem, d_tok, rel, dkm, dvm, dko, dvo = refs[10:]
        kp = vp = None
    h = pl.program_id(0)
    lower = lower_mask()
    slab = jnp.zeros((8, BLK), F32)
    dko[...] = jnp.zeros_like(dko)
    dvo[...] = jnp.zeros_like(dvo)
    if has_prev:
        dkp[...] = jnp.zeros_like(dkp)
        dvp[...] = jnp.zeros_like(dvp)
    for t in range(2):
        rows = slice(t * HALF, (t + 1) * HALF)
        qt = q[rows, :]
        dt = do[rows, :]
        log_t = jnp.sum(jnp.where(head_lane(h), logs[rows, :], 0.0), axis=1, keepdims=True)
        p_mem = jnp.exp(mm_nt(qt, km[...]) * SCALE - log_t)
        s_near, s_far, s_edge = window_scores(t, has_prev, qt, ko, kp, bias, rows, lower)
        p_near = jnp.exp(s_near - log_t)
        w_mem = mm_nt(dt, vm[...])
        w_near = mm_nt(dt, vo[rows, :])
        inner = jnp.sum(p_mem * w_mem, axis=1, keepdims=True)
        if has_prev:
            w_near = jnp.where(lower, w_near, mm_nt(dt, vp[rows, :]))
            p_edge = jnp.exp(s_edge - log_t)
            v_edge = vp[rows, :].astype(F32)
            k_edge = kp[rows, :].astype(F32)
            w_edge = jnp.sum(dt.astype(F32) * v_edge, axis=1, keepdims=True)
            inner += p_edge * w_edge
        inner += jnp.sum(p_near * w_near, axis=1, keepdims=True)
        if s_far is not None:
            far = slice(0, HALF) if t == 1 else slice(HALF, BLK)
            k_far, v_far = (ko, vo) if t == 1 else (kp, vp)
            p_far = jnp.exp(s_far - log_t)
            w_far = mm_nt(dt, v_far[far, :])
            inner += jnp.sum(p_far * w_far, axis=1, keepdims=True)
        g_mem = (p_mem * (w_mem - inner)).astype(BF)
        g_near32 = p_near * (w_near - inner)
        g_near = g_near32.astype(BF)
        dq = mm(g_mem, km[...])
        zero = jnp.zeros((), BF)
        if has_prev:
            g_own = jnp.where(lower, g_near32, 0.0).astype(BF)
            g_prev = jnp.where(lower, 0.0, g_near32).astype(BF)
            p_own = jnp.where(lower, p_near, 0.0).astype(BF)
            p_prev = jnp.where(lower, 0.0, p_near).astype(BF)
            g_edge = (p_edge * (w_edge - inner)).astype(BF).astype(F32)
            p_edge16 = p_edge.astype(BF).astype(F32)
            dq += mm(g_prev, kp[rows, :]) + g_edge * k_edge
            dkp[rows, :] += mm_tn(g_prev, qt) + g_edge * qt.astype(F32)
            dvp[rows, :] += mm_tn(p_prev, dt) + p_edge16 * dt.astype(F32)
        else:
            g_own = g_near
            p_own = p_near.astype(BF)
        dq += mm(g_own, ko[rows, :])
        dko[rows, :] += mm_tn(g_own, qt)
        dvo[rows, :] += mm_tn(p_own, dt)
        g_far32 = jnp.zeros((HALF, HALF), F32)
        if s_far is not None:
            g_far = (p_far * (w_far - inner)).astype(BF)
            g_far32 = g_far.astype(F32)
            dq += mm(g_far, k_far[far, :])
            dk_far, dv_far = (dko, dvo) if t == 1 else (dkp, dvp)
            dk_far[far, :] += mm_tn(g_far, qt)
            dv_far[far, :] += mm_tn(p_far.astype(BF), dt)
        d_tok[rows, head_cols(0, h)] = (dq * SCALE).astype(d_tok.dtype)
        g_round = g_near.astype(F32)
        wide = [g_round, g_far32] if t == 0 else [g_far32, g_round]
        wide = jnp.concatenate(wide, axis=1)
        for a in range(HALF // 8):
            shift = (BLK - 8 * a - t * HALF) % BLK
            part = wide[8 * a : 8 * a + 8, :]
            slab = slab + (pltpu.roll(part, shift, 1) if shift else part)
        if has_prev:
            at = lax.broadcasted_iota(jnp.int32, (8, BLK), 0) * BLK
            at = at + lax.broadcasted_iota(jnp.int32, (8, BLK), 1)
            edge_sum = jnp.sum(g_edge, axis=0, keepdims=True)
            slab = slab + jnp.where(at == 1, edge_sum, 0.0)
        add_k = mm_tn(g_mem, qt)
        add_v = mm_tn(p_mem.astype(BF), dt)
        if t == 0:
            dkm[...] = add_k
            dvm[...] = add_v
        else:
            dkm[...] += add_k
            dvm[...] += add_v
    rel[0] = slab
    k_tok = dko[...] * SCALE + ak[...]
    v_tok = dvo[...] + av[...]
    d_tok[:, head_cols(1, h)] = k_tok.astype(d_tok.dtype)
    d_tok[:, head_cols(2, h)] = v_tok.astype(d_tok.dtype)
    if has_prev:
        d_mem[:, head_cols(0, h)] = sq[...].astype(BF)
        d_mem[:, head_cols(1, h)] = (dkm[...] * SCALE + sk[...]).astype(BF)
        d_mem[:, head_cols(2, h)] = (dvm[...] + sv[...]).astype(BF)
        d_prev[:, head_cols(0, h)] = dkp[...] * SCALE
        d_prev[:, head_cols(1, h)] = dvp[...]
    else:
        d_mem[:, head_cols(0, h)] = dkm[...] * SCALE
        d_mem[:, head_cols(1, h)] = dvm[...]


def tok_backward(block, proj, mem_proj, bias, grad_mix, logs, add_tok, add_mem=None):
    has_prev = block > 0
    specs = [col(block, 0), col(0, 1), col(0, 2), col(block, 1), col(block, 2)]
    specs += [pl.BlockSpec((1, BLK, BLK), lambda h: (h, 0, 0)), col(block, 0), full((BLK, DH))]
    ops = [proj, mem_proj, mem_proj, proj, proj, bias, grad_mix, logs]
    scratch = 4
    if has_prev:
        specs += [col(block - 1, 1), col(block - 1, 2), col(0, 0), col(0, 1), col(0, 2)]
        ops += [proj, proj, add_mem, add_mem, add_mem]
        scratch = 6
    specs += [col(0, 0), col(0, 1)]
    ops += [add_tok, add_tok]
    kind = BF if has_prev else F32
    rel_spec = pl.BlockSpec((1, 8, BLK), lambda h: (h, 0, 0))
    rel_shape = jax.ShapeDtypeStruct((HL, 8, BLK), F32)
    wide = 3 * KEEP if has_prev else 2 * KEEP
    out_specs = [full((BLK, wide)), full((BLK, 3 * KEEP))]
    out_shape = [
        jax.ShapeDtypeStruct((BLK, wide), kind),
        jax.ShapeDtypeStruct((BLK, 3 * KEEP), kind),
    ]
    if has_prev:
        out_specs.append(full((BLK, 2 * KEEP)))
        out_shape.append(jax.ShapeDtypeStruct((BLK, 2 * KEEP), F32))
    return pl.pallas_call(
        functools.partial(tok_bwd_kernel, has_prev),
        grid=(HL,),
        in_specs=specs,
        out_specs=out_specs + [rel_spec],
        out_shape=out_shape + [rel_shape],
        scratch_shapes=[pltpu.VMEM((BLK, DH), F32)] * scratch,
        name="tok_bwd",
        **params(
            flops=10 * BLK * 1280 * KEEP,
            moved=12 * 2**20,
            vmem=VMEM_GRADS if has_prev else VMEM_MOST,
        ),
    )(*ops)


def normal_parts(u):
    bell = jnp.exp(-0.5 * (u * u))
    t = 1.0 / (1.0 + (0.3275911 * math.sqrt(0.5)) * jnp.abs(u))
    poly = 1.061405429 * t - 1.453152027
    poly = poly * t + 1.421413741
    poly = poly * t - 0.284496736
    poly = poly * t + 0.254829592
    tail = (0.5 * poly) * (t * bell)
    return jnp.where(u >= 0, 1.0 - tail, tail), bell * (1.0 / math.sqrt(2.0 * math.pi))


MAIN = 96
REST = DH - MAIN
TILE = 4 * DH


def mlp_kernel(h0, h1, d0, d1, u0, u1, w0, w1, r0, r1, *refs):
    a_keep, a_send, b_keep, b_send, c_keep, c_send, o0, o1, e0, e1 = refs[:10]
    accs = refs[10:]
    t = pl.program_id(0)
    in_x, in_y = t // 2, lax.rem(t, 2)

    @pl.when(t == 0)
    def _():
        for ref in accs:
            ref[...] = jnp.zeros_like(ref)

    rest = jnp.where(in_x == 0, r0[...], r1[...]).reshape(4, 2 * REST, D)
    wu = jnp.where(in_y == 0, u0[...], u1[...]).reshape(4 * MAIN, D)
    wu = jnp.concatenate([wu, rest[:, 0:REST].reshape(4 * REST, D)], axis=0)
    wd = [w0[...].reshape(2 * MAIN, D), w1[...].reshape(2 * MAIN, D)]
    wd = jnp.concatenate(wd + [rest[:, REST:].reshape(4 * REST, D)], axis=0)
    kept = []
    for r in range(2):
        h = (h0, h1)[r]
        d = (d0, d1)[r]
        u = mm_nt(h[...], wu)
        dg = mm_nt(d[...], wd)
        phi, pdf = normal_parts(u)
        g = (u * phi).astype(BF)
        du = (dg * (phi + u * pdf)).astype(BF)
        accs[r][...] += mm(g, wd)
        accs[2 + r][...] += mm(du, wu)
        kept.append((g, du))
    gd = (mm_tn(kept[0][0], d0[...]) + mm_tn(kept[1][0], d1[...])).astype(BF)
    gu = (mm_tn(kept[0][1], h0[...]) + mm_tn(kept[1][1], h1[...])).astype(BF)
    gd_rest, gu_rest = (v[4 * MAIN :].reshape(4, REST, D) for v in (gd, gu))
    gd, gu = (v[0 : 4 * MAIN].reshape(4, MAIN, D) for v in (gd, gu))
    for z1 in range(2):
        side = (c_keep, c_send)[z1]
        for z2 in range(2):
            side[0, 0, z2, 0:REST, :] = gu_rest[2 * z1 + z2]
            side[0, 0, z2, REST:, :] = gd_rest[2 * z1 + z2]
    for bit in range(2):

        @pl.when(in_x == bit)
        def _():
            for z in range(4):
                (a_keep, a_send)[bit][0, z // 2, z % 2] = gu[z]

        @pl.when(in_y == bit)
        def _():
            for z in range(4):
                (b_keep, b_send)[bit][z // 2, 0, z % 2] = gd[z]

    @pl.when(t == pl.num_programs(0) - 1)
    def _():
        for ref, acc in zip((o0, o1, e0, e1), accs):
            ref[...] = acc[...].astype(BF)


def mlp(h0, h1, d0, d1, u0, u1, w0, w1, r0, r1):
    act = full((BLK, D))
    up = pl.BlockSpec((1, 2, 2, MAIN, D), lambda t: (t // 2, 0, 0, 0, 0))
    down = pl.BlockSpec((1, 1, 2, MAIN, D), lambda t: (t % 2, t // 2, 0, 0, 0))
    rest_block = (2, 1, 2, 2 * REST, D)
    rest0 = pl.BlockSpec(rest_block, lambda t: (0, jnp.minimum(t, 1), 0, 0, 0))
    rest1 = pl.BlockSpec(rest_block, lambda t: (0, jnp.maximum(t - 2, 0), 0, 0, 0))
    tail = (MAIN, D)
    a_keep = pl.BlockSpec((1, 2, 2) + tail, lambda t: (jnp.minimum(t, 1), 0, 0, 0, 0))
    a_send = pl.BlockSpec((1, 2, 2) + tail, lambda t: (jnp.maximum(t - 2, 0), 0, 0, 0, 0))
    b_keep = pl.BlockSpec((2, 1, 2) + tail, lambda t: (0, t // 2, 0, 0, 0))
    b_send = pl.BlockSpec((2, 1, 2) + tail, lambda t: (0, t // 3, 0, 0, 0))
    c_spec = pl.BlockSpec((1, 1, 2, 2 * REST, D), lambda t: (t // 2, t % 2, 0, 0, 0))
    big_shape = jax.ShapeDtypeStruct((2, 2, 2, MAIN, D), BF)
    rest_shape = jax.ShapeDtypeStruct((2, 2, 2, 2 * REST, D), BF)
    return pl.pallas_call(
        mlp_kernel,
        grid=(4,),
        in_specs=[act] * 4 + [up, up, down, down, rest0, rest1],
        out_specs=[a_keep, a_send, b_keep, b_send, c_spec, c_spec] + [act] * 4,
        scratch_shapes=[pltpu.VMEM((BLK, D), F32)] * 4,
        out_shape=[big_shape] * 4
        + [rest_shape] * 2
        + [jax.ShapeDtypeStruct((BLK, D), BF)] * 4,
        name="mlp",
        **params(flops=12 * D * D * 2 * D, moved=26 * 2**20, vmem=VMEM_MLP),
    )(h0, h1, d0, d1, u0, u1, w0, w1, r0, r1)


def halves_kernel(*refs):
    count = len(refs) // 4
    for keep, got, out_keep, out_send in zip(
        refs[:count], refs[count : 2 * count], refs[2 * count :: 2], refs[2 * count + 1 :: 2]
    ):
        out_keep[...] = (keep[0].astype(F32) + got[0].astype(F32)).astype(BF)
        out_send[...] = (keep[1].astype(F32) + got[1].astype(F32)).astype(BF)


def add_halves(keeps, gots):
    shapes = [k.shape for k in keeps]
    flat = [k.reshape(2, -1, k.shape[-1]) for k in keeps]
    flat_got = [g.reshape(2, -1, g.shape[-1]) for g in gots]
    steps = 4
    while any((k.shape[1] // steps) % 16 or k.shape[1] % steps for k in flat):
        steps //= 2
    ins, outs, out_shapes = [], [], []
    for k in flat:
        rows, width = k.shape[1] // steps, k.shape[2]
        ins.append(pl.BlockSpec((2, rows, width), lambda t: (0, t, 0)))
        outs += [pl.BlockSpec((rows, width), lambda t: (t, 0))] * 2
        out_shapes += [jax.ShapeDtypeStruct(k.shape[1:], BF)] * 2
    done = pl.pallas_call(
        halves_kernel,
        grid=(steps,),
        in_specs=ins * 2,
        out_specs=outs,
        out_shape=out_shapes,
        name="halves",
        **params(),
    )(*flat, *flat_got)
    done = [d.reshape(sh[1:]) for d, sh in zip(done, [s for s in shapes for _ in range(2)])]
    return done[0::2], done[1::2]


def eight_rows(values):
    return jnp.sum(values.reshape(-1, 8, values.shape[-1]), axis=0)


def mid_back_kernel(mid, gain, e_own, e_got, d_own, o_own, o_got, dmid, da, out, gsum):
    rows = mid[...]
    back, gain_rows = norm_back(
        rows, gain[...], e_own[...].astype(F32) + e_got[...].astype(F32)
    )
    total = d_own[...].astype(F32) + back
    dmid[...] = total
    da[...] = total.astype(BF)
    out[...] = (rows + o_own[...].astype(F32) + o_got[...].astype(F32)).astype(BF)

    @pl.when(pl.program_id(0) == 0)
    def _():
        gsum[...] = jnp.zeros_like(gsum)

    gsum[...] += eight_rows(gain_rows)


def mid_back(mid, gain, e_own, e_got, d_own, o_own, o_got):
    row = pl.BlockSpec((DH, D), lambda t: (t, 0))
    return pl.pallas_call(
        mid_back_kernel,
        grid=(BLK // DH,),
        in_specs=[row, full((1, D))] + [row] * 5,
        out_specs=[row, row, row, full((8, D))],
        out_shape=[
            jax.ShapeDtypeStruct((BLK, D), F32),
            jax.ShapeDtypeStruct((BLK, D), BF),
            jax.ShapeDtypeStruct((BLK, D), BF),
            jax.ShapeDtypeStruct((8, D), F32),
        ],
        name="mid_back",
        **params(vmem=VMEM_GRADS),
    )(mid, gain, e_own, e_got, d_own, o_own, o_got)


def out_back_kernel(me, own, oth, wo, ot0, ot1, dot_all, grad):
    first = me[0] == 0
    da0 = jnp.where(first, own[...], oth[...])
    da1 = jnp.where(first, oth[...], own[...])
    dot_all[0:BLK, :] = mm_nt(da0, wo[...]).astype(BF)
    dot_all[BLK:, :] = mm_nt(da1, wo[...]).astype(BF)
    grad[...] = (mm_tn(ot0[...], da0) + mm_tn(ot1[...], da1)).astype(BF)


def out_back(me, own, oth, wo, ot0, ot1):
    return pl.pallas_call(
        out_back_kernel,
        grid_spec=pltpu.PrefetchScalarGridSpec(
            num_scalar_prefetch=1,
            grid=(1,),
            in_specs=[full((BLK, D))] * 2 + [full((KEEP, D))] + [full((BLK, KEEP))] * 2,
            out_specs=[full((2 * BLK, KEEP)), full((KEEP, D))],
        ),
        out_shape=[
            jax.ShapeDtypeStruct((2 * BLK, KEEP), BF),
            jax.ShapeDtypeStruct((KEEP, D), BF),
        ],
        name="out_back",
        **params(vmem=VMEM_GRADS),
    )(me, own, oth, wo, ot0, ot1)


def proj_back_kernel(me, a, b, w, own, oth):
    first = me[0] == 0
    own[...] = mm_nt(jnp.where(first, a[...], b[...]), w[...]).astype(BF)
    oth[...] = mm_nt(jnp.where(first, b[...], a[...]), w[...]).astype(BF)


def proj_one_kernel(a, w, own):
    own[...] = mm_nt(a[...], w[...]).astype(BF)


def proj_one(a, w):
    rows = a.shape[0]
    return pl.pallas_call(
        proj_one_kernel,
        grid=(4,),
        in_specs=[full(a.shape), pl.BlockSpec((D // 4, 3 * KEEP), lambda t: (t, 0))],
        out_specs=pl.BlockSpec((rows, D // 4), lambda t: (0, t)),
        out_shape=jax.ShapeDtypeStruct((rows, D), BF),
        name="proj_one",
        **params(),
    )(a, w)


def proj_back(me, a, b, w):
    rows = a.shape[0] // 2 if b is a else a.shape[0]
    side = 1 if b is a else 0
    return pl.pallas_call(
        proj_back_kernel,
        grid_spec=pltpu.PrefetchScalarGridSpec(
            num_scalar_prefetch=1,
            grid=(4,),
            in_specs=[
                pl.BlockSpec((rows, 3 * KEEP), lambda t, me: (0, 0)),
                pl.BlockSpec((rows, 3 * KEEP), lambda t, me: (side, 0)),
                pl.BlockSpec((D // 4, 3 * KEEP), lambda t, me: (t, 0)),
            ],
            out_specs=[pl.BlockSpec((rows, D // 4), lambda t, me: (0, t))] * 2,
        ),
        out_shape=[jax.ShapeDtypeStruct((rows, D), BF)] * 2,
        name="proj_back",
        **params(),
    )(me, a, b, w)


def state_back_kernel(me, *refs):
    state1, gain, own, got, ds2, gate, wu, os0, os1, dz1, zz1, state0, zz0 = refs[:13]
    ds1, dos0, grad_wu, gate_sum, acc = refs[13:]
    t = pl.program_id(0)
    last = ds2[...].astype(F32)
    back = norm_back(
        state1[...], gain[...], own[...].astype(F32) + got[...].astype(F32)
    )[0]
    total = gate[...] * last + back
    ds1[...] = total
    dz0 = ((1.0 - gate[...]) * total).astype(BF)
    dos0[...] = mm_nt(dz0, wu[...]).astype(BF)

    @pl.when(t == 0)
    def _():
        acc[...] = jnp.zeros_like(acc)
        gate_sum[...] = jnp.zeros_like(gate_sum)

    acc[...] += mm_tn(os0[...], dz0) + mm_tn(os1[...], dz1[...])

    @pl.when(t // 2 == me[0])
    def _():
        step = state0[...].astype(F32) - zz0[...].astype(F32)
        terms = last * (state1[...] - zz1[...].astype(F32)) + total * step
        gate_sum[...] += eight_rows(terms)

    @pl.when(t == 3)
    def _():
        grad_wu[...] = acc[...].astype(BF)


def state_back(me, state1, gain, own, got, ds2, gate, wu, os0, os1, dz1, zz1, state0, zz0):
    row = pl.BlockSpec((DH, D), lambda t, me: (t, 0))
    head = pl.BlockSpec((DH, KEEP), lambda t, me: (t, 0))
    half = pl.BlockSpec((DH, D), lambda t, me: (t % 2, 0))
    line = full((1, D))
    return pl.pallas_call(
        state_back_kernel,
        grid_spec=pltpu.PrefetchScalarGridSpec(
            num_scalar_prefetch=1,
            grid=(4,),
            in_specs=[row, line, row, row, row, line, full((KEEP, D)), head, head, row, half]
            + [row, row],
            out_specs=[row, head, full((KEEP, D)), full((8, D))],
            scratch_shapes=[pltpu.VMEM((KEEP, D), F32)],
        ),
        out_shape=[
            jax.ShapeDtypeStruct((BLK, D), F32),
            jax.ShapeDtypeStruct((BLK, KEEP), BF),
            jax.ShapeDtypeStruct((KEEP, D), BF),
            jax.ShapeDtypeStruct((8, D), F32),
        ],
        name="state_back",
        **params(vmem=VMEM_GRADS),
    )(me, state1, gain, own, got, ds2, gate, wu, os0, os1, dz1, zz1, state0, zz0)


def row_back_kernel(me, values, gain, own, got, scale, base, out):
    back = norm_back(
        values[...].astype(F32), gain[...], own[...].astype(F32) + got[...].astype(F32)
    )[0]
    out[...] = (scale[...] * base[...] + back).astype(BF)


def row_back(me, values, gain, own, got, scale, base):
    count = own.shape[0] // DH
    skip = values.shape[0] // DH - count
    row = pl.BlockSpec((DH, D), lambda t, me: (t, 0))
    mine = pl.BlockSpec((DH, D), lambda t, me: (me[0] * skip + t, 0))
    return pl.pallas_call(
        row_back_kernel,
        grid_spec=pltpu.PrefetchScalarGridSpec(
            num_scalar_prefetch=1,
            grid=(count,),
            in_specs=[mine, full((1, D)), row, row, full((1, D)), mine],
            out_specs=row,
        ),
        out_shape=jax.ShapeDtypeStruct(own.shape, BF),
        name="row_back",
        **params(vmem=VMEM_GRADS),
    )(me, values, gain, own, got, scale, base)


def proj_grad_kernel(me, *refs):
    xa, xb, sa, sb, pa, pb, ra, rb, small = refs[:9]
    a_keep, a_send, b_keep, b_send, c_keep, c_send, tok, st = refs[9:]
    x0, y0 = me[1], me[3]
    in_z = lax.rem(pl.program_id(0), 2)
    tok[...] = mm_tn(xa[...], pa[...]) + mm_tn(xb[...], pb[...])
    st[...] = mm_tn(sa[...], ra[...]) + mm_tn(sb[...], rb[...])

    def write(ref, xr, yr, sub):
        rows = pl.ds(pl.multiple_of((x0 ^ xr) * DH, DH), DH)
        cols = pl.ds(pl.multiple_of((y0 ^ yr) * 768 + sub * 256, 256), 256)
        ref[0:DH, :] = tok[rows, cols].astype(BF)
        ref[DH : 2 * DH, :] = st[rows, cols].astype(BF)

    for xr in range(2):
        for yr in range(2):
            write((a_keep, a_send)[xr].at[yr, 0, 0], xr, yr, 0)
            (a_keep, a_send)[xr][yr, 0, 0, 2 * DH :, :] = small[x0 ^ xr, y0 ^ yr]
            write((b_keep, b_send)[yr].at[0, xr, 0], xr, yr, 1)
    for zb in range(2):

        @pl.when(in_z == zb)
        def _():
            for xr in range(2):
                for yr in range(2):
                    write((c_keep, c_send)[zb].at[xr, yr, 0], xr, yr, 2)


def proj_grads(me, xn, sn0, sn1, dp0, dp1, dr0, dr1, small):
    lhs = pl.BlockSpec((BLK, 2 * DH), lambda q, me: (0, q ^ me[2]))
    lhs1 = pl.BlockSpec((BLK, 2 * DH), lambda q, me: (1, q ^ me[2]))
    rhs = full((BLK, 3 * KEEP))
    shape = jax.ShapeDtypeStruct((2, 2, 2, 2 * DH, 2 * DH), BF)
    tall = jax.ShapeDtypeStruct((2, 2, 2, 2 * DH + 16, 2 * DH), BF)
    tail = (2 * DH, 2 * DH)
    a_tail = (2 * DH + 16, 2 * DH)
    a_spec = pl.BlockSpec((2, 1, 1) + a_tail, lambda q, me: (0, q % 2, q // 2, 0, 0))
    small_spec = pl.BlockSpec((2, 2, 16, 256), lambda q, me: (q ^ me[2], 0, 0, 0))
    b_spec = pl.BlockSpec((1, 2, 1) + tail, lambda q, me: (q % 2, 0, q // 2, 0, 0))
    c_spec = pl.BlockSpec((2, 2, 1) + tail, lambda q, me: (0, 0, q // 2, 0, 0))
    return pl.pallas_call(
        proj_grad_kernel,
        grid_spec=pltpu.PrefetchScalarGridSpec(
            num_scalar_prefetch=1,
            grid=(4,),
            in_specs=[lhs, lhs1, lhs, lhs, rhs, rhs, rhs, rhs, small_spec],
            out_specs=[a_spec, a_spec, b_spec, b_spec, c_spec, c_spec],
            scratch_shapes=[pltpu.VMEM((2 * DH, 3 * KEEP), F32)] * 2,
        ),
        out_shape=[tall] * 2 + [shape] * 4,
        name="proj_grad",
        **params(flops=4 * D * D * 3 * KEEP, moved=16 * 2**20, vmem=VMEM_GRADS),
    )(me, xn, xn, sn0, sn1, dp0, dp1, dr0, dr1, small)


def place_proj_kernel(me, p0, p1, w_tok, w_state, tok, st, gain_tok, gain_st, small):
    c0, y0 = me[0], me[3]
    starts = (0, 2 * DH + 16, 4 * DH + 16)
    for cr in range(2):
        for yr in range(2):
            src = (p0, p1)[cr].at[yr]
            for sub in range(3):
                for i in range(2):
                    j = 6 * (y0 ^ yr) + 2 * sub + i
                    at = (j // HL) * D + (2 * (j % HL) + (c0 ^ cr)) * DH
                    dst = pl.ds(pl.multiple_of(at, DH), DH)
                    cols = slice(i * DH, (i + 1) * DH)
                    row = starts[sub]
                    tok[:, dst] = src[row : row + DH, cols].astype(F32)
                    st[:, dst] = src[row + DH : row + 2 * DH, cols].astype(F32)
    for yr in range(2):
        first = p0[yr, 2 * DH : 2 * DH + 16, :].astype(F32)
        small[y0 ^ yr] = first + p1[yr, 2 * DH : 2 * DH + 16, :].astype(F32)
    ones = jnp.ones((8, 3 * D), F32)
    for out, grad, weight in ((gain_tok, tok, w_tok), (gain_st, st, w_state)):
        out[...] = lax.dot_general(
            ones,
            grad[...] * weight[...].astype(F32),
            (((1,), (1,)), ((), ())),
            precision=lax.Precision.HIGHEST,
            preferred_element_type=F32,
        )


def place_proj(me, p0, p1, w_tok, w_state):
    one = jax.ShapeDtypeStruct((DH, 3 * D), F32)
    line = jax.ShapeDtypeStruct((8, DH), F32)
    return pl.pallas_call(
        place_proj_kernel,
        grid_spec=pltpu.PrefetchScalarGridSpec(
            num_scalar_prefetch=1,
            grid=(1,),
            in_specs=[full(p0.shape)] * 2 + [full(w_tok.shape)] * 2,
            out_specs=[full((DH, 3 * D))] * 2 + [full((8, DH))] * 2 + [full((2, 16, 256))],
        ),
        out_shape=[one, one, line, line, jax.ShapeDtypeStruct((2, 16, 256), F32)],
        name="place_proj",
        **params(moved=5 * 2**20),
    )(me, p0, p1, w_tok, w_state)


def place_mlp_kernel(me, p0, p1, up, down):
    c0, y0 = me[0], me[3]
    for cr in range(2):
        for yr in range(2):
            src = (p0, p1)[cr].at[yr]
            row = ((c0 ^ cr) * 2 + (y0 ^ yr)) * DH
            big = pl.ds(pl.multiple_of(row, DH), MAIN)
            rest = pl.ds(pl.multiple_of(row + MAIN, REST), REST)
            up[big, :] = src[0:MAIN].astype(F32)
            down[big, :] = src[MAIN : 2 * MAIN].astype(F32)
            up[rest, :] = src[2 * MAIN : 2 * MAIN + REST].astype(F32)
            down[rest, :] = src[2 * MAIN + REST :].astype(F32)


def place_mlp(me, p0, p1):
    one = jax.ShapeDtypeStruct((2 * p0.shape[1], D), F32)
    return pl.pallas_call(
        place_mlp_kernel,
        grid_spec=pltpu.PrefetchScalarGridSpec(
            num_scalar_prefetch=1,
            grid=(1,),
            in_specs=[full(p0.shape)] * 2,
            out_specs=[full(one.shape)] * 2,
        ),
        out_shape=[one, one],
        name="place_mlp",
        **params(moved=6 * 2**20),
    )(me, p0, p1)


def body(
    tokens,
    state_in,
    gain_tok,
    gain_state,
    gain_mlp,
    w_tok,
    w_state,
    w_out,
    w_update,
    gate_bias,
    rel_bias,
    w_up,
    w_down,
    d_out,
    d_state_next,
):
    c = lax.axis_index("c")
    x = lax.axis_index("x")
    z = lax.axis_index("s")
    y = lax.axis_index("y")
    z1, z2 = z % 2, z // 2
    me = jnp.stack([c, x, z, y]).astype(jnp.int32)
    on_diag = c == x
    slots = state_in.shape[0]
    srows = state_in.shape[1]

    def pick(value, got):
        return jnp.where(on_diag, value, got)

    def by_block(own, other):
        return jnp.where(c == 0, jnp.concatenate([own, other]), jnp.concatenate([other, own]))

    def my_half(rows):
        return lax.dynamic_slice_in_dim(rows, c * HALF, HALF, 0)

    def other_half(rows):
        return lax.dynamic_slice_in_dim(rows, (1 - c) * HALF, HALF, 0)

    def to_slot(value, k):
        return lax.ppermute(value, "s", [(i, i ^ k) for i in range(slots)])

    def slot(value, k):
        return lax.dynamic_index_in_dim(value, z ^ k, 0, keepdims=False)

    def slot_order(parts):
        stacked = jnp.stack(parts).reshape(2, 2, srows, D)
        return untwist(stacked, (z2, z1)).reshape(slots, srows, D)

    def half_sum(part, got):
        return (part.astype(F32) + got.astype(F32)).astype(BF)

    def slot_spread(value):
        return [value[0]] + [to_slot(value[k], k) for k in range(1, slots)]

    subs = pick_columns(me, w_tok, w_state)
    small = jnp.stack([gain_tok, gain_state, gain_mlp, gate_bias])
    small = jnp.concatenate([small, jnp.pad(rel_bias, ((0, 0), (0, DH - NB)))])
    small = jnp.pad(small, ((0, 11), (0, DH)))
    ha, hb, hc = jnp.concatenate([subs[0], small]), subs[1], subs[2]
    got = [xch(hc, "z2"), xch(hb, "z2"), xch(ha, "z2"), diag_send(state_in), diag_send(tokens)]
    quarter = DH // 4
    at = (c * 2 + y) * quarter
    ho = jnp.concatenate(
        [
            lax.dynamic_slice_in_dim(w_out, at, quarter, 0),
            lax.dynamic_slice_in_dim(w_update, at, quarter, 0),
        ]
    )

    gc, gb, ga, g_states, g_tokens, ho = fence(got + [ho], got[:4])
    ha, hb, hc = jnp.stack([ha, ga]), jnp.stack([hb, gb]), jnp.stack([hc, gc])
    got = [xch(ha, "z1"), xch(hb, "x"), xch(hc, "y")]
    states = pick(state_in, g_states)
    half = [slot(states, 0), to_slot(slot(states, 2), 2)]
    g_piece = diag_send(ho)

    ga, gb, gc, half, g_piece, g_tokens = fence(
        got + [half, g_piece, g_tokens], got + [half, g_piece, g_tokens]
    )
    ha, hb, hc = jnp.stack([ha, ga]), jnp.stack([hb, gb]), jnp.stack([hc, gc])
    got = [xch(ha, "y"), xch(hb, "z1"), xch(hc, "x")]
    half = half + [to_slot(slot(states, 3), 3)]
    x_own = pick(tokens, g_tokens)
    x_oth = xch(x_own, "c")
    ho = pick(ho, g_piece)
    hid = w_up.shape[0] // 4
    hid_at = (c * 2 + y) * hid
    hu = lax.dynamic_slice_in_dim(w_up, hid_at, hid, 0)
    hd = lax.dynamic_slice_in_dim(w_down, hid_at, hid, 0)
    hm = jnp.concatenate([hu[:MAIN], hd[:MAIN], hu[MAIN:], hd[MAIN:]])

    def three(value):
        return value[:MAIN], value[MAIN : 2 * MAIN], value[2 * MAIN :]

    def stacks(held, got):
        return [jnp.stack([h, g]) for h, g in zip(held, got)]

    def sends(held, bits):
        return [xch(h, b) for h, b in zip(held, bits)]

    ga, gb, gc, half, ho, x_own, x_oth, hm = fence(
        got + [half, ho, x_own, x_oth, hm], got + [half, x_oth]
    )
    half = half[:1] + [to_slot(slot(states, 1), 1)] + half[1:]
    ha, hb, hc = jnp.stack([ha, ga]), jnp.stack([hb, gb]), jnp.stack([hc, gc])
    got = [xch(ha, "x"), xch(hb, "y"), xch(hc, "z1")]
    half = jnp.concatenate(half)
    state0 = by_block(half, xch(half, "c"))
    rows = by_block(x_own, x_oth).astype(F32)
    x_hat = norm_parts(rows)[0]
    s_hat = norm_parts(state0.astype(F32))[0]
    go = xch(ho, "z2")

    got, go, hm, x_hat, s_hat, d_out, d_state_next = fence(
        (got, go, hm, x_hat, s_hat, d_out, d_state_next), (got, x_hat, s_hat)
    )
    ho = jnp.stack([ho, go])
    gm = xch(hm, "z2")
    go = xch(ho, "x")
    g_states = diag_send(d_state_next)
    w_tok_l, w_state_l, small_all = lay_tables(me, (ha, got[0]), (hb, got[1]), (hc, got[2]))
    vectors = small_all[:, :4, :DH].transpose(1, 0, 2).reshape(4, D).astype(F32)
    g_tok, g_state, g_mlp = vectors[0], vectors[1], vectors[2]
    gate = jax.nn.sigmoid(vectors[3])
    xn = (x_hat * g_tok).astype(BF)
    proj = mm(xn, w_tok_l).astype(BF)

    go, g_states, proj, small_all = fence((go, g_states, proj, small_all), (go, proj))
    ho = jnp.stack([ho, go])
    tu, to = ho[:, :, quarter:], ho[:, :, :quarter]
    gt, go = xch(tu, "z1"), xch(to, "y")
    d_states = pick(d_state_next, g_states)
    d_rows = [slot(d_states, 0)] + [to_slot(slot(d_states, k), k) for k in (1, 2)]
    sn0 = (s_hat * g_state).astype(BF)
    r0 = mm(sn0, w_state_l).astype(BF)
    rel_rows = small_all[:, 4, :NB].reshape(HL, 2, NB)
    rel_mine = lax.dynamic_index_in_dim(rel_rows, c, 1, keepdims=False)
    hot = jnp.asarray(slab_buckets())[None, :] == jnp.arange(NB, dtype=jnp.int32)[:, None]
    base = mm(rel_mine, hot.astype(BF)).reshape(HL, 8, BLK)
    bias = bias_tables(base)
    os0, log_s0 = mem_forward(0, proj, r0)

    gt, go, gm, r0, os0, bias, d_states, d_rows = fence(
        (gt, go, gm, r0, os0, bias, d_states, d_rows), (gt, gm, os0, bias)
    )
    d_rows = d_rows + [to_slot(slot(d_states, 3), 3)]
    tu = jnp.stack([tu, gt])
    gt = xch(tu, "y")
    hm = stacks(three(hm), three(gm))
    gm = sends(hm, ("z1", "x", "y"))
    to = jnp.stack([to, go])
    ot0, log_t0 = tok_forward(0, proj, r0, bias)

    to, gt, gm, os0, ot0, d_half = fence((to, gt, gm, os0, ot0, d_rows), (gt, os0, ot0))
    wu = lay_out_table("y", me, tu, gt)
    hm = stacks(hm, gm)
    gm = sends(hm, ("x", "y", "z1"))
    go = xch(to, "z1")
    zp0 = mm(os0, wu)
    zz0 = zp0 + xch(zp0.astype(BF), "c").astype(F32)
    zz0_kept = zz0.astype(BF)
    state1 = gate * state0.astype(F32) + (1.0 - gate) * zz0
    sn1 = (norm_parts(state1)[0] * g_state).astype(BF)
    r1 = mm(sn1, w_state_l).astype(BF)
    ot1, log_t1 = tok_forward(1, proj, r1, bias)

    gm, go, ot1, r1, d_out, d_half = fence(
        (gm, go, ot1, r1, d_out, d_half), (gm, ot1, d_half)
    )
    wo = lay_out_table("z", me, to, go)
    hm = stacks(hm, gm)
    gm = sends(hm, ("y", "z1", "x"))
    d_half = jnp.concatenate(d_half)
    ds2 = by_block(d_half, xch(d_half, "c"))
    g_dout = diag_send(d_out)
    part0, part1 = mm(ot0, wo), mm(ot1, wo)
    part_own = jnp.where(c == 0, part0, part1)
    part_oth = jnp.where(c == 0, part1, part0).astype(BF)
    mid = x_own.astype(F32) + part_own + xch(part_oth, "c").astype(F32)
    h_own = (norm_parts(mid)[0] * g_mlp).astype(BF)
    h_oth = xch(h_own, "c")
    os1, log_s1 = mem_forward(1, proj, r1)
    zp1 = mm(os1, wu)
    zz1 = my_half(zp1) + xch(other_half(zp1).astype(BF), "c").astype(F32)
    state1_half = my_half(state1)
    state2_half = (gate * state1_half + (1.0 - gate) * zz1).astype(BF)
    dz1 = ((1.0 - gate) * ds2.astype(F32)).astype(BF)
    dos1 = mm_nt(dz1, wu).astype(BF)
    dm1, dt1 = mem_backward(1, proj, r1, dos1, log_s1)

    gm, h_own, h_oth, g_dout, state2_half = fence(
        (gm, h_own, h_oth, g_dout, state2_half), (gm, h_own, h_oth, g_dout, state2_half, dm1)
    )
    d_own = pick(d_out, g_dout)
    d_oth = xch(d_own, "c")
    out_rows = slot_spread(state2_half.reshape(slots, srows, D))
    ma, ma_out, mb, mb_out, mc, mc_out, o_own, o_oth, e_own, e_oth = mlp(
        h_own,
        h_oth,
        d_own,
        d_oth,
        hm[0],
        gm[0],
        hm[1],
        gm[1],
        hm[2],
        gm[2],
    )

    out_rows, ma_out, mb_out, mc_out, o_oth, e_oth = fence(
        (out_rows, ma_out, mb_out, mc_out, o_oth, e_oth), (out_rows, o_oth, e_oth)
    )
    got = [xch(ma_out, "x"), xch(mb_out, "y"), xch(mc_out, "z1")]
    state_next = slot_order(out_rows)
    e_got, o_got = xch(e_oth, "c"), xch(o_oth, "c")
    dmid, da_own, output, gain_rows = mid_back(
        mid, g_mlp[None], e_own, e_got, d_own, o_own, o_got
    )
    dot_all, grad_wo = out_back(me, da_own, xch(da_own, "c"), wo, ot0, ot1)
    dr1, dp1, dprev, rel1 = tok_backward(1, proj, r1, bias, dot_all, log_t1, dt1, dm1)

    got, dr1, dprev, output, state_next = fence(
        (got, dr1, dprev, output, state_next), (got, dr1, dprev, output)
    )
    (ma, mb, mc), sends = add_halves((ma, mb, mc), got)
    got = [xch(s, b) for s, b in zip(sends, ("y", "z1", "x"))]
    got += [diag_send(output), diag_send(state_next)]
    dsn1 = proj_one(dr1, w_state_l)
    dsn1_got = xch(dsn1, "c")
    dm0, dt0, rel0 = tok_backward(0, proj, r0, bias, dot_all, log_t0, dprev)

    got, dm0, dt0, dsn1, dsn1_got = fence((got, dm0, dt0, dsn1, dsn1_got), (got, dm0, dsn1_got))
    output = pick(output, got[3])
    state_next = pick(state_next, got[4]).astype(F32)
    (ma, mb, mc), sends = add_halves((ma, mb, mc), got[:3])
    got = [xch(s, b) for s, b in zip(sends, ("z1", "x", "y"))]
    ds1, dos0, grad_wu, gate_rows = state_back(
        me,
        state1,
        g_state[None],
        dsn1,
        dsn1_got,
        ds2,
        gate[None],
        wu,
        os0,
        os1,
        dz1,
        zz1.astype(BF),
        state0,
        zz0_kept,
    )
    grad_gate = jnp.sum(gate_rows, axis=0) * gate * (1.0 - gate)
    grad_g_mlp = jnp.sum(gain_rows, axis=0)
    rel_sum = (rel0 + rel1).reshape(HL, 8 * BLK)
    grad_rel = lax.dot_general(
        rel_sum,
        hot.astype(F32),
        (((1,), (1,)), ((), ())),
        precision=lax.Precision.HIGHEST,
        preferred_element_type=F32,
    )
    both = jnp.stack([grad_rel, jnp.zeros_like(grad_rel)], axis=1)
    both = jnp.where(c == 0, both, jnp.flip(both, 1)).reshape(H, NB)
    first = jnp.concatenate([grad_g_mlp.reshape(H, DH), jnp.pad(both, ((0, 0), (0, DH - NB)))], 1)
    second = jnp.pad(grad_gate.reshape(H, DH), ((0, 0), (0, DH)))
    small_sums = jnp.stack([first, second], axis=1)[:, :, None, :].astype(BF)
    small_sums = jnp.pad(small_sums, ((0, 0), (0, 0), (0, 15), (0, 0)))
    outs = jnp.stack([grad_wo, grad_wu]).astype(BF).reshape(2, 2, 2, 2, 2, quarter, D)

    got, dos0, outs = fence((got, dos0, outs), (got, dos0, outs))
    (ma, mb, mc), sends = add_halves((ma, mb, mc), got)
    got_m = [xch(s, "z2") for s in sends]
    names = ["z2", "z1", "x", "y"]
    spots = {"z2": z2, "z1": z1, "x": x, "y": y}

    def split_outs(value, bit):
        axis = names.index(bit) + 1
        names.remove(bit)
        keep = lax.dynamic_index_in_dim(value, spots[bit], axis, keepdims=False)
        send = lax.dynamic_index_in_dim(value, 1 - spots[bit], axis, keepdims=False)
        return keep, send

    keep_o, send_o = split_outs(outs, "y")
    got_o = xch(send_o, "y")
    dr0, dp0 = mem_backward(0, proj, r0, dos0, log_s0, dm0, dt0)

    got_o, got_m, dr0, dp0, xn, sn0, sn1 = fence(
        (got_o, got_m, dr0, dp0, xn, sn0, sn1), (got_o, got_m, dr0, dp0)
    )
    mlp_part = [half_sum(h, g) for h, g in zip((ma, mb, mc), got_m)]
    mlp_part = over_groups(jnp.concatenate(mlp_part))
    got_m = xch(mlp_part, "y")
    keep_o, send_o = split_outs(half_sum(keep_o, got_o), "x")
    got_o = xch(send_o, "x")
    ha, ha_out, hb, hb_out, hc, hc_out = proj_grads(
        me, xn, sn0, sn1, dp0, dp1, dr0, dr1, small_sums
    )

    got_o, got_m, ha_out, hb_out, hc_out, dr0, dp0 = fence(
        (got_o, got_m, ha_out, hb_out, hc_out, dr0, dp0), (got_o, got_m, ha_out)
    )
    both_m = jnp.stack([mlp_part, got_m])
    got_c = xch(both_m, "c")
    got = [xch(ha_out, "x"), xch(hb_out, "y"), xch(hc_out, "z1")]
    dxn, dxn_send = proj_back(me, dp0, dp1, w_tok_l)
    dxn_got = xch(dxn_send, "c")
    dsn0, dsn0_send = proj_back(me, dr0, dr0, w_state_l)
    dsn0_got = xch(dsn0_send, "c")

    got, got_o, dxn_got, dsn0_got = fence(
        (got, got_o, dxn_got, dsn0_got), (got, got_o, dxn_got, dsn0_got)
    )
    (ha, hb, hc), sends = add_halves((ha, hb, hc), got)
    got = [xch(s, b) for s, b in zip(sends, ("y", "z1", "x"))]
    keep_o, send_o = split_outs(half_sum(keep_o, got_o), "z1")
    got_o = xch(send_o, "z1")
    one = jnp.ones((1, D), F32)
    grad_tokens = row_back(me, x_own, g_tok[None], dxn, dxn_got, one, dmid)

    got, got_o, grad_tokens, dsn0_got = fence(
        (got, got_o, grad_tokens, dsn0_got), (got, got_o, grad_tokens)
    )
    (ha, hb, hc), sends = add_halves((ha, hb, hc), got)
    got = [xch(s, b) for s, b in zip(sends, ("z1", "x", "y"))]
    keep_o, send_o = split_outs(half_sum(keep_o, got_o), "z2")
    got_o = xch(send_o, "z2")
    grad_state = row_back(me, state0, g_state[None], dsn0, dsn0_got, gate[None], ds1)
    grad_state = grad_state.reshape(slots, srows, D)

    got, got_o, grad_state, grad_tokens = fence(
        (got, got_o, grad_state, grad_tokens), (got, got_o, grad_state)
    )
    (ha, hb, hc), sends = add_halves((ha, hb, hc), got)
    got = [xch(s, "z2") for s in sends]
    got_t = diag_send(grad_tokens)
    outs = over_groups(half_sum(keep_o, got_o))
    outs = jnp.stack([outs, xch(outs, "y")])
    grad_up, grad_down = place_mlp(me, both_m, got_c)

    got, got_t, outs, grad_state, grad_up = fence(
        (got, got_t, outs, grad_state, grad_up), (got, got_t, outs, grad_up)
    )
    part = over_groups(jnp.concatenate([half_sum(h, g) for h, g in zip((ha, hb, hc), got)]))
    got_y = xch(part, "y")
    grad_rows = slot_spread(grad_state)
    outs = jnp.stack([outs, xch(outs, "x")])
    grad_tokens = pick(grad_tokens, got_t).astype(F32)

    got_y, grad_rows, outs = fence((got_y, grad_rows, outs), (got_y,))
    both_t = jnp.stack([part, got_y])
    got_p = xch(both_t, "c")
    grad_state = slot_order(grad_rows)
    grad_state = pick(grad_state, diag_send(grad_state)).astype(F32)
    outs = untwist(outs, (x, y)).transpose(2, 0, 1, 3, 4).reshape(2, DH, D)
    outs = pick(outs, xch(outs, "c")).astype(F32)
    grad_tok_w, grad_state_w, rows_tok, rows_st, small = place_proj(
        me, both_t, got_p, w_tok, w_state
    )
    grad_g_tok = rows_tok[0] / gain_tok.astype(F32)
    grad_g_state = rows_st[0] / gain_state.astype(F32)

    return (
        output,
        state_next,
        grad_tokens,
        grad_state,
        grad_g_tok,
        grad_g_state,
        small[0, 0, :DH],
        grad_tok_w,
        grad_state_w,
        outs[0],
        outs[1],
        small[1, 0, :DH],
        small[0, 0:1, DH : DH + NB],
        grad_up,
        grad_down,
    )


def solution(mesh):
    reps, shards = mesh.devices.shape
    grid = Mesh(mesh.devices.reshape(reps // 4, 2, 2, shards // 2, 2), ("h", "y", "c", "s", "x"))
    rep, shard = ("h", "y", "c"), ("s", "x")
    every = rep + shard
    by_token = P(every, None)
    by_state = P(rep, shard, None)
    line = P(shard)
    table = P(shard, None)
    params_spec = (line, line, line, table, table, table, table, line, table, table, table)
    return jax.shard_map(
        body,
        mesh=grid,
        in_specs=(by_token, by_state) + params_spec + (by_token, by_state),
        out_specs=(by_token, by_state, by_token, by_state) + params_spec,
        check_vma=False,
    )
```
